128 devices in a mesh: section: 2 (over y_lo), ctx: 8 (over y_hi, z), fsdp: 8 (over x, core).
Axes of the slice: x: 4, y: 4 (y_hi: 2, y_lo: 2; y = y_hi * 2 + y_lo), z: 4, core: 2. Of those that a mesh axis runs over, the one named last changes fastest.
Arguments:
- inputs: bfloat16 [2, 8, 1024, 1024], P(None, 'fsdp', 'ctx'), may hold values from -6 to 6
- cotangent: bfloat16 [2, 8, 1024, 1024], P(None, 'fsdp', 'ctx'), may hold values from -6 to 6
- block_order: int32 [16], replicated, may hold values from 0 to 15, each once
- ln1_gain: bfloat16 [2, 1024], P('section', ('ctx', 'fsdp')), may hold values from 0.25 to 1.75
- ln1_bias: bfloat16 [2, 1024], P('section', ('ctx', 'fsdp')), may hold values from -2.5 to 2.5
- qkv_weight: bfloat16 [2, 1024, 3072], P('section', ('ctx', 'fsdp')), may hold values from -0.25 to 0.25
- qv_bias: bfloat16 [2, 2048], P('section', ('ctx', 'fsdp')), may hold values from -2.5 to 2.5
- out_weight: bfloat16 [2, 1024, 1024], P('section', ('ctx', 'fsdp')), may hold values from -1 to 1
- out_bias: bfloat16 [2, 1024], P('section', ('ctx', 'fsdp')), may hold values from -2.5 to 2.5
- ln2_gain: bfloat16 [2, 1024], P('section', ('ctx', 'fsdp')), may hold values from 0.25 to 1.75
- ln2_bias: bfloat16 [2, 1024], P('section', ('ctx', 'fsdp')), may hold values from -2.5 to 2.5
- fc_weight: bfloat16 [2, 1024, 4096], P('section', ('ctx', 'fsdp')), may hold values from -0.1875 to 0.1875
- fc_bias: bfloat16 [2, 4096], P('section', ('ctx', 'fsdp')), may hold values from -2.5 to 2.5
- proj_weight: bfloat16 [2, 4096, 1024], P('section', ('ctx', 'fsdp')), may hold values from -0.125 to 0.125
- proj_bias: bfloat16 [2, 1024], P('section', ('ctx', 'fsdp')), may hold values from -2.5 to 2.5
Outputs:
- acts: bfloat16 [2, 2, 8, 1024, 1024], P('section', None, 'fsdp', 'ctx')
- in_grads: float32 [2, 2, 8, 1024, 1024], P('section', None, 'fsdp', 'ctx')
- grad_ln1_gain: float32 [2, 1024], P('section', ('ctx', 'fsdp'))
- grad_ln1_bias: float32 [2, 1024], P('section', ('ctx', 'fsdp'))
- grad_qkv_weight: float32 [2, 1024, 3072], P('section', ('ctx', 'fsdp'))
- grad_qv_bias: float32 [2, 2048], P('section', ('ctx', 'fsdp'))
- grad_out_weight: float32 [2, 1024, 1024], P('section', ('ctx', 'fsdp'))
- grad_out_bias: float32 [2, 1024], P('section', ('ctx', 'fsdp'))
- grad_ln2_gain: float32 [2, 1024], P('section', ('ctx', 'fsdp'))
- grad_ln2_bias: float32 [2, 1024], P('section', ('ctx', 'fsdp'))
- grad_fc_weight: float32 [2, 1024, 4096], P('section', ('ctx', 'fsdp'))
- grad_fc_bias: float32 [2, 4096], P('section', ('ctx', 'fsdp'))
- grad_proj_weight: float32 [2, 4096, 1024], P('section', ('ctx', 'fsdp'))
- grad_proj_bias: float32 [2, 1024], P('section', ('ctx', 'fsdp'))
The draws below stay inside these ranges and needn't reach their ends.
Inputs may be any that keep to these rules, and one draw needn't show every extreme that they name: `block_order`: a permutation: each of 0 to 15 once.
All inputs are finite; a program needn't handle non-finite values.
Results may differ from the reference program's by a relative error of at most 0.025.
Values may be sent and summed in bfloat16 or wider, within the bound.
No kernel may reach another device: no remote copies, remote signals or barrier semaphores. Data moves between devices by JAX's collectives and lax.ppermute only.
A program may use at most 256 MiB of HBM per device.

```python
import jax
import jax.numpy as jnp
from jax import lax

D = 1024
HEADS = 16
HEAD_DIM = 64
FF = 4096
LENGTH = 1024
MICRO = 2
SEQS = 8
BLOCKS = 16
N_CTX = 8
N_FSDP = 8


def steps_of(own_key, extent, cuts, least, largest):
    def one(axis_at, shards_of):
        heights = jax.random.uniform(jax.random.fold_in(jax.random.fold_in(own_key, 6), axis_at), (shards_of,), jnp.float32, least / len(cuts), largest / len(cuts))
        return jnp.repeat(jnp.exp(heights), extent[axis_at] // shards_of).reshape((-1,) + (1,) * (len(extent) - axis_at - 1))

    gain = one(*cuts[0])
    for cut in cuts[1:]:
        gain = gain * one(*cut)
    return gain


def noise(rng, dims, deviation, reach, shards=(), kind=jnp.bfloat16):
    drawn = jax.random.normal(rng, dims, jnp.float32) * deviation
    if len(shards) > 0:
        drawn = steps_of(rng, dims, shards, -0.22, 0.18) * drawn
    return jnp.clip(drawn, min=-reach, max=reach).astype(kind)


def setup_inputs(seed: int = 0) -> dict:
    key_of = jax.random.split(jax.random.key(seed), 16)
    inputs = noise(key_of[0], (MICRO, SEQS, LENGTH, D), 1.0, 6.0, ((1, 8), (2, 8)))
    cotangent = noise(key_of[1], (MICRO, SEQS, LENGTH, D), 1.0, 6.0, ((1, 8), (2, 8)))
    block_order = jax.random.permutation(key_of[2], BLOCKS).astype(jnp.int32)
    ln1_gain = jnp.clip(1.0 + 0.15 * jax.random.normal(key_of[3], (2, D), jnp.float32), 0.25, 1.75).astype(jnp.bfloat16)
    ln1_bias = noise(key_of[4], (2, D), 0.3, 2.5, ((0, 2), (1, 64)))
    qkv_weight = noise(key_of[5], (2, D, 3 * D), (D // 2) ** -0.5, 0.25, ((0, 2), (1, 64)))
    qv_bias = noise(key_of[6], (2, 2 * D), 0.3, 2.5, ((0, 2), (1, 64)))
    out_weight = noise(key_of[7], (2, D, D), (D // 32) ** -0.5, 1.0, ((0, 2), (1, 64)))
    out_bias = noise(key_of[8], (2, D), 0.3, 2.5, ((0, 2), (1, 64)))
    ln2_gain = jnp.clip(1.0 + 0.15 * jax.random.normal(key_of[9], (2, D), jnp.float32), 0.25, 1.75).astype(jnp.bfloat16)
    ln2_bias = noise(key_of[10], (2, D), 0.3, 2.5, ((0, 2), (1, 64)))
    fc_weight = noise(key_of[11], (2, D, FF), D ** -0.5, 0.1875, ((0, 2), (1, 64)))
    fc_bias = noise(key_of[12], (2, FF), 0.3, 2.5, ((0, 2), (1, 64)))
    proj_weight = noise(key_of[13], (2, FF, D), (FF // 2) ** -0.5, 0.125, ((0, 2), (1, 64)))
    proj_bias = noise(key_of[14], (2, D), 0.3, 2.5, ((0, 2), (1, 64)))
    return dict(inputs=inputs, cotangent=cotangent, block_order=block_order, ln1_gain=ln1_gain, ln1_bias=ln1_bias, qkv_weight=qkv_weight, qv_bias=qv_bias, out_weight=out_weight, out_bias=out_bias, ln2_gain=ln2_gain, ln2_bias=ln2_bias, fc_weight=fc_weight, fc_bias=fc_bias, proj_weight=proj_weight, proj_bias=proj_bias)


@jax.custom_vjp
def low(v):
    return lax.optimization_barrier(v.astype(jnp.bfloat16)).astype(jnp.float32)

@jax.custom_vjp
def low_back(v):
    return v

def low_keep(v):
    return (low(v), None)

def low_pass(kept, grad):
    return (grad,)

def back_keep(v):
    return (v, None)

def back_low(kept, grad):
    return (low(grad),)
low.defvjp(low_keep, low_pass)
low_back.defvjp(back_keep, back_low)
EPSILON = 1e-05
MASKED = -1e+30

def product(left, right):
    return jnp.dot(left, right, precision=lax.Precision.HIGHEST)

def layer_norm(values, gain_vec, bias_vec):
    average = lax.optimization_barrier(jnp.mean(values, axis=-1, keepdims=True))
    centred = values - average
    spread = lax.optimization_barrier(jnp.mean(centred * centred, axis=-1, keepdims=True))
    return centred * lax.rsqrt(spread + EPSILON) * gain_vec + bias_vec

def layer(hidden, params, positions):
    ln1_gain, ln1_bias, qkv_weight, qv_bias, out_weight, out_bias, ln2_gain, ln2_bias, fc_weight, fc_bias, proj_weight, proj_bias = params
    length = hidden.shape[0]
    normed = low(layer_norm(hidden, ln1_gain, ln1_bias))
    key_zeros = jnp.zeros((D,), hidden.dtype)
    qkv_bias = jnp.concatenate([qv_bias[:D], key_zeros, qv_bias[D:]])
    projected = low(low_back(product(normed, qkv_weight) + qkv_bias))
    queries = projected[:, :D].reshape(length, HEADS, HEAD_DIM)
    keys_all = projected[:, D:2 * D].reshape(length, HEADS, HEAD_DIM)
    values_all = projected[:, 2 * D:].reshape(length, HEADS, HEAD_DIM)
    raw_scores = jnp.einsum('qhd,khd->hqk', queries, keys_all, precision=lax.Precision.HIGHEST)
    scores = low_back(raw_scores * HEAD_DIM ** (-0.5))
    allowed = positions[:, None] >= positions[None, :]
    scores = jnp.where(allowed[None], scores, MASKED)
    highest = lax.optimization_barrier(jnp.max(scores, axis=-1, keepdims=True))
    log_total = highest + jnp.log(lax.optimization_barrier(jnp.sum(jnp.exp(scores - highest), axis=-1, keepdims=True)))
    probs = low(jnp.exp(scores - log_total))
    attended = jnp.einsum('hqk,khd->qhd', probs, values_all, precision=lax.Precision.HIGHEST).reshape(length, D)
    attended = low(low_back(attended))
    middle = hidden + low_back(product(attended, out_weight) + out_bias)
    normed2 = low(layer_norm(middle, ln2_gain, ln2_bias))
    before = low_back(product(normed2, fc_weight) + fc_bias)
    activated = low(jax.nn.gelu(before, approximate=True))
    return middle + low_back(product(activated, proj_weight) + proj_bias)

def reference(inputs, cotangent, block_order, ln1_gain, ln1_bias, qkv_weight, qv_bias, out_weight, out_bias, ln2_gain, ln2_bias, fc_weight, fc_bias, proj_weight, proj_bias):
    stacked = (ln1_gain, ln1_bias, qkv_weight, qv_bias, out_weight, out_bias, ln2_gain, ln2_bias, fc_weight, fc_bias, proj_weight, proj_bias)
    first_layer = tuple((entry[0].astype(jnp.float32) for entry in stacked))
    second_layer = tuple((entry[1].astype(jnp.float32) for entry in stacked))
    block_rows = LENGTH // (2 * N_CTX)
    offsets = jnp.arange(block_rows, dtype=jnp.int32)
    positions = (block_order.astype(jnp.int32)[:, None] * block_rows + offsets[None, :]).reshape(LENGTH)

    def forward(start, params_first, params_second, extra):
        hidden = layer(start, params_first, positions)
        middle = low_back(low(hidden) + extra)
        return (layer(middle, params_second, positions), hidden)

    def one_sequence(totals, item):
        seq_in, seq_cot = item
        extra = jnp.zeros((LENGTH, D), jnp.float32)
        result, pullback, hidden = jax.vjp(forward, seq_in.astype(jnp.float32), first_layer, second_layer, extra, has_aux=True)
        grad_in, grad_first, grad_second, grad_mid = pullback(seq_cot.astype(jnp.float32))
        totals = jax.tree.map(lambda running, first_grad, second_grad: running + jnp.stack([first_grad, second_grad]), totals, grad_first, grad_second)
        return (totals, (hidden.astype(jnp.bfloat16), result.astype(jnp.bfloat16), grad_in, grad_mid))
    initial = tuple((jnp.zeros(entry.shape, jnp.float32) for entry in stacked))
    flat_in = inputs.reshape(MICRO * N_FSDP, LENGTH, D)
    flat_cot = cotangent.reshape(MICRO * N_FSDP, LENGTH, D)
    totals, outputs = lax.scan(one_sequence, initial, (flat_in, flat_cot))
    hidden_all, result_all, grad_in_all, grad_mid_all = outputs
    acts = jnp.stack([hidden_all, result_all]).reshape(2, MICRO, N_FSDP, LENGTH, D)
    in_grads = jnp.stack([grad_in_all, grad_mid_all]).reshape(2, MICRO, N_FSDP, LENGTH, D)
    return (acts, in_grads, totals[0], totals[1], totals[2], totals[3], totals[4], totals[5], totals[6], totals[7], totals[8], totals[9], totals[10], totals[11])
```

```python
import jax
import jax.numpy as jnp
from jax import lax
from jax.experimental import pallas as pl
from jax.experimental.pallas import tpu as pltpu
from jax.sharding import Mesh
from jax.sharding import PartitionSpec as P

D = 1024
HEADS = 16
HEAD_DIM = 64
FF = 4096
PAIRS = 8
PAIR = 128
TILE = 256
BLOCK = 64
CTX = ("ctx_0", "ctx_1")
FSDP = ("fsdp_0", "fsdp_1")
CTX_FSDP = CTX + FSDP
CHIPS = CTX + ("fsdp_0",)
CORE = "fsdp_1"
EPSILON = 1e-05
MASKED = -1e30
SCALE = HEAD_DIM**-0.5
BF16 = jnp.bfloat16
F32 = jnp.float32


def dot(left, right):
    return jnp.dot(left, right, preferred_element_type=F32)


def dot_rows(left, right):
    return lax.dot_general(left, right, (((0,), (0,)), ((), ())), preferred_element_type=F32)


def dot_back(left, right):
    return lax.dot_general(left, right, (((1,), (1,)), ((), ())), preferred_element_type=F32)


def swap_cores(value):
    return lax.ppermute(value, CORE, [(0, 1), (1, 0)])


def half(value, which, dim):
    size = value.shape[dim] // 2
    return lax.dynamic_slice_in_dim(value, which * size, size, dim)


def both_halves(mine, other, core, dim):
    size = mine.shape[dim]
    shape = list(mine.shape)
    shape[dim] = 2 * size
    whole = jnp.zeros(shape, mine.dtype)
    whole = lax.dynamic_update_slice_in_dim(whole, mine, core * size, dim)
    return lax.dynamic_update_slice_in_dim(whole, other, (1 - core) * size, dim)


def gather_weight(shard, core):
    mine, other = half(shard, core, 1), half(shard, 1 - core, 1)
    rows = both_halves(mine, swap_cores(other), core, 0)
    columns = lax.all_gather(rows, CHIPS, axis=0, tiled=True)
    return both_halves(columns, swap_cores(columns), core, 1)


def sum_weight(grad, core):
    rows, columns = grad.shape
    each = rows // 32
    parts = grad.reshape(2, 4, 4, each, columns).transpose(2, 1, 0, 3, 4)
    for axis in ("fsdp_0", "ctx_1", "ctx_0"):
        parts = lax.psum_scatter(parts, axis, scatter_dimension=0, tiled=False)
    mine, other = half(parts, core, 0), half(parts, 1 - core, 0)
    return both_halves(mine, swap_cores(other), core, 1).astype(F32)


def layer_norm(values, gain, bias):
    average = jnp.mean(values, axis=-1, keepdims=True)
    centred = values - average
    spread = jnp.mean(centred * centred, axis=-1, keepdims=True)
    inverse = lax.rsqrt(spread + EPSILON)
    normal = centred * inverse
    return normal * gain + bias, normal, inverse


def norm_back(upstream, normal, inverse, gain):
    scaled = upstream * gain
    first = jnp.mean(scaled, axis=-1, keepdims=True)
    second = jnp.mean(scaled * normal, axis=-1, keepdims=True)
    return (
        inverse * (scaled - first - normal * second),
        jnp.sum(upstream * normal, axis=0),
        jnp.sum(upstream, axis=0),
    )


def head_lanes(shape, head, dim):
    return lax.broadcasted_iota(jnp.int32, shape, dim) // HEAD_DIM == head


def causal(keys):
    rows = lax.broadcasted_iota(jnp.int32, (keys, TILE), 0)
    columns = lax.broadcasted_iota(jnp.int32, (keys, TILE), 1)
    return rows <= columns + (keys - TILE)


def stored_blocks(order_ref):
    for s in range(16):
        at = pl.multiple_of(order_ref[s] * BLOCK, BLOCK)
        yield s // 2, slice((s % 2) * BLOCK, (s % 2 + 1) * BLOCK), pl.ds(at, BLOCK)


def attention_kernel(order_ref, qkv_ref, out_ref, lse_ref, q, k, v, out):
    for device, rows, sorted_rows in stored_blocks(order_ref):
        q[sorted_rows, :] = qkv_ref[device, rows, 0:PAIR]
        k[sorted_rows, :] = qkv_ref[device, rows, PAIR : 2 * PAIR] * SCALE
        v[sorted_rows, :] = qkv_ref[device, rows, 2 * PAIR :]
    length = q.shape[0]
    lse_ref[...] = jnp.zeros_like(lse_ref)
    for tile in range(length // TILE):
        keys = (tile + 1) * TILE
        here = pl.ds(tile * TILE, TILE)
        outs = []
        for head in range(2):
            queries = q[here, :]
            queries = jnp.where(head_lanes(queries.shape, head, 1), queries, jnp.zeros_like(queries))
            scores = dot_back(k[0:keys, :], queries)
            scores = jnp.where(causal(keys), scores, MASKED)
            highest = jnp.max(scores, axis=0, keepdims=True)
            probs = jnp.exp(scores - highest)
            total = jnp.sum(probs, axis=0, keepdims=True)
            lse_ref[0, head : head + 1, here] = highest + jnp.log(total)
            attended = dot_rows(v[0:keys, :], probs.astype(BF16)) / total
            outs.append(attended[head * HEAD_DIM : (head + 1) * HEAD_DIM, :])
        out[here, :] = jnp.concatenate(outs, axis=0).T.astype(BF16)
    for device, rows, sorted_rows in stored_blocks(order_ref):
        out_ref[device, rows, :] = out[sorted_rows, :]


def attention_back_kernel(order_ref, qkv_ref, grad_ref, lse_ref, out_ref, q, k, v, g, dq, dk, dv):
    for device, rows, sorted_rows in stored_blocks(order_ref):
        q[sorted_rows, :] = qkv_ref[device, rows, 0:PAIR]
        k[sorted_rows, :] = qkv_ref[device, rows, PAIR : 2 * PAIR] * SCALE
        v[sorted_rows, :] = qkv_ref[device, rows, 2 * PAIR :]
        g[sorted_rows, :] = grad_ref[device, rows, :]
    length = q.shape[0]
    dk[...] = jnp.zeros_like(dk)
    dv[...] = jnp.zeros_like(dv)
    for tile in range(length // TILE):
        keys = (tile + 1) * TILE
        here = pl.ds(tile * TILE, TILE)
        outs = []
        for head in range(2):
            lanes = head_lanes((TILE, PAIR), head, 1)
            queries = q[here, :]
            queries = jnp.where(lanes, queries, jnp.zeros_like(queries))
            grads = g[here, :]
            grads = jnp.where(lanes, grads, jnp.zeros_like(grads))
            scores = dot_back(k[0:keys, :], queries)
            probs = jnp.exp(scores - lse_ref[0, head : head + 1, here])
            probs = jnp.where(causal(keys), probs, 0.0)
            grad_probs = dot_back(v[0:keys, :], grads)
            term = jnp.sum(probs * grad_probs, axis=0, keepdims=True)
            grad_scores = (probs * (grad_probs - term)).astype(BF16)
            dv[0:keys, :] += dot(probs.astype(BF16), grads)
            dk[0:keys, :] += dot(grad_scores, queries)
            grad_q = dot_rows(k[0:keys, :], grad_scores)
            outs.append(grad_q[head * HEAD_DIM : (head + 1) * HEAD_DIM, :])
        dq[here, :] = jnp.concatenate(outs, axis=0).T
    for device, rows, sorted_rows in stored_blocks(order_ref):
        out_ref[device, rows, 0:PAIR] = dq[sorted_rows, :].astype(BF16)
        out_ref[device, rows, PAIR : 2 * PAIR] = (dk[sorted_rows, :] * SCALE).astype(BF16)
        out_ref[device, rows, 2 * PAIR :] = dv[sorted_rows, :].astype(BF16)


def attention(qkv, order):
    devices, tokens, _ = qkv.shape
    rows = tokens // 2
    length = devices * rows
    block = lambda width: pl.BlockSpec((devices, rows, width), lambda m, order: (0, m, 0))
    return pl.pallas_call(
        attention_kernel,
        grid_spec=pltpu.PrefetchScalarGridSpec(
            num_scalar_prefetch=1,
            grid=(2,),
            in_specs=[block(3 * PAIR)],
            out_specs=[block(PAIR), pl.BlockSpec((1, 8, length), lambda m, order: (m, 0, 0))],
            scratch_shapes=[pltpu.VMEM((length, PAIR), BF16)] * 4,
        ),
        out_shape=[
            jax.ShapeDtypeStruct((devices, tokens, PAIR), BF16),
            jax.ShapeDtypeStruct((2, 8, length), F32),
        ],
        compiler_params=pltpu.CompilerParams(vmem_limit_bytes=48 * 2**20),
    )(order, qkv)


def attention_back(qkv, grad, lse, order):
    devices, tokens, _ = qkv.shape
    rows = tokens // 2
    length = devices * rows
    block = lambda width: pl.BlockSpec((devices, rows, width), lambda m, order: (0, m, 0))
    return pl.pallas_call(
        attention_back_kernel,
        grid_spec=pltpu.PrefetchScalarGridSpec(
            num_scalar_prefetch=1,
            grid=(2,),
            in_specs=[
                block(3 * PAIR),
                block(PAIR),
                pl.BlockSpec((1, 8, length), lambda m, order: (m, 0, 0)),
            ],
            out_specs=block(3 * PAIR),
            scratch_shapes=[pltpu.VMEM((length, PAIR), BF16)] * 4
            + [pltpu.VMEM((length, PAIR), F32)] * 3,
        ),
        out_shape=jax.ShapeDtypeStruct((devices, tokens, 3 * PAIR), BF16),
        compiler_params=pltpu.CompilerParams(vmem_limit_bytes=48 * 2**20),
    )(order, qkv, grad, lse)


def to_heads(values):
    tokens, columns = values.shape
    cut = values.reshape(tokens, PAIRS, columns // PAIRS).swapaxes(0, 1)
    return lax.all_to_all(cut, CTX, 0, 0, tiled=True)


def to_rows(values):
    _, tokens, width = values.shape
    back = lax.all_to_all(values, CTX, 0, 0, tiled=True)
    return back.swapaxes(0, 1).reshape(tokens, PAIRS * width)


def layer_forward(hidden, w, order):
    normed, normal1, inverse1 = layer_norm(hidden, w["ln1_gain"], w["ln1_bias"])
    normed = normed.astype(BF16)
    projected = (dot(normed, w["qkv"]) + w["qkv_bias"]).astype(BF16)
    qkv = to_heads(projected)
    heads, lse = attention(qkv, order)
    attended = to_rows(heads)
    middle = hidden + (dot(attended, w["out"]) + w["out_bias"])
    normed2, normal2, inverse2 = layer_norm(middle, w["ln2_gain"], w["ln2_bias"])
    normed2 = normed2.astype(BF16)
    before = dot(normed2, w["fc"]) + w["fc_bias"]
    activated = jax.nn.gelu(before, approximate=True).astype(BF16)
    result = middle + (dot(activated, w["proj"]) + w["proj_bias"])
    saved = dict(
        normed=normed,
        normal1=normal1,
        inverse1=inverse1,
        qkv=qkv,
        lse=lse,
        attended=attended,
        normal2=normal2,
        inverse2=inverse2,
        normed2=normed2,
        before=before,
        activated=activated,
    )
    return result, saved


def layer_backward(upstream, s, w, order):
    dy2 = upstream.astype(BF16)
    grad_act = dot_back(dy2, w["proj"])
    d_pre = jax.vjp(lambda u: jax.nn.gelu(u, approximate=True), s["before"])[1](grad_act)[0]
    d_pre = d_pre.astype(BF16)
    d_normed2 = dot_back(d_pre, w["fc"])
    through, ln2_gain, ln2_bias = norm_back(d_normed2, s["normal2"], s["inverse2"], w["ln2_gain"])
    d_mid = upstream + through
    dy1 = d_mid.astype(BF16)
    d_att = dot_back(dy1, w["out"]).astype(BF16)
    d_heads = to_heads(d_att)
    d_qkv = to_rows(attention_back(s["qkv"], d_heads, s["lse"], order))
    d_normed = dot_back(d_qkv, w["qkv"])
    through, ln1_gain, ln1_bias = norm_back(d_normed, s["normal1"], s["inverse1"], w["ln1_gain"])
    d_hidden = d_mid + through
    return d_hidden, dict(
        dy2=dy2,
        d_pre=d_pre,
        dy1=dy1,
        d_qkv=d_qkv,
        ln1_gain=ln1_gain,
        ln1_bias=ln1_bias,
        ln2_gain=ln2_gain,
        ln2_bias=ln2_bias,
    )


def weight_grad(left, right, core):
    mine, other = half(right, core, 1), half(right, 1 - core, 1)
    grad = dot_rows(left, mine) + dot_rows(swap_cores(left), swap_cores(other))
    return sum_weight(grad.astype(BF16), core)


def by_pair(values):
    lead = values.shape[:-1]
    return values.reshape(*lead, 3, PAIRS, PAIR).swapaxes(-2, -3).reshape(*lead, 3 * D)


def by_part(values):
    lead = values.shape[:-1]
    return values.reshape(*lead, PAIRS, 3, PAIR).swapaxes(-2, -3).reshape(*lead, 3 * D)


def on_device(
    inputs,
    cotangent,
    block_order,
    ln1_gain,
    ln1_bias,
    qkv_weight,
    qv_bias,
    out_weight,
    out_bias,
    ln2_gain,
    ln2_bias,
    fc_weight,
    fc_bias,
    proj_weight,
    proj_bias,
):
    section = lax.axis_index("section")
    core = lax.axis_index(CORE)
    first = section == 0
    micro, _, rows, _ = inputs.shape
    tokens = micro * rows
    own_inputs = inputs.reshape(tokens, D)
    own_cot = cotangent.reshape(tokens, D)

    vectors = (ln1_gain, ln1_bias, qv_bias, out_bias, ln2_gain, ln2_bias, fc_bias, proj_bias)
    widths = [v.shape[-1] for v in vectors]
    starts = [sum(widths[:i]) for i in range(len(widths))]
    packed = lax.all_gather(
        jnp.concatenate([v.reshape(1, -1) for v in vectors], axis=1), CTX_FSDP, axis=0, tiled=True
    )
    names = ("ln1_gain", "ln1_bias", "qv", "out_bias", "ln2_gain", "ln2_bias", "fc_bias", "proj_bias")
    w = {
        name: packed[:, start : start + width].reshape(-1).astype(F32)
        for name, start, width in zip(names, starts, widths)
    }
    qv = w.pop("qv")
    w["qkv_bias"] = by_pair(jnp.concatenate([qv[:D], jnp.zeros((D,), F32), qv[D:]]))
    w["qkv"] = gather_weight(by_pair(qkv_weight[0]), core)
    w["out"] = gather_weight(out_weight[0], core)
    w["fc"] = gather_weight(fc_weight[0], core)
    w["proj"] = gather_weight(proj_weight[0], core)

    result, _ = layer_forward(own_inputs.astype(F32), w, block_order)
    arriving = lax.ppermute(result.astype(BF16), "section", [(0, 1)])
    entry = jnp.where(first, own_inputs, arriving)
    result, saved = layer_forward(entry.astype(F32), w, block_order)
    acts = result.astype(BF16)

    d_hidden, _ = layer_backward(own_cot.astype(F32), saved, w, block_order)
    arriving = lax.ppermute(d_hidden.astype(BF16), "section", [(1, 0)])
    upstream = jnp.where(first, arriving, own_cot).astype(F32)
    d_hidden, g = layer_backward(upstream, saved, w, block_order)
    in_grads = jnp.where(first, d_hidden, d_hidden.astype(BF16).astype(F32))

    proj_w = weight_grad(saved["activated"], g["dy2"], core)
    fc_w = weight_grad(saved["normed2"], g["d_pre"], core)
    out_w = weight_grad(saved["attended"], g["dy1"], core)
    qkv_w = by_part(weight_grad(saved["normed"], g["d_qkv"], core))

    sums = {n: jnp.sum(g[n].astype(F32), axis=0) for n in ("dy2", "d_pre", "dy1", "d_qkv")}
    d_qkv_sum = by_part(sums["d_qkv"])
    small = (
        g["ln1_gain"],
        g["ln1_bias"],
        jnp.concatenate([d_qkv_sum[:D], d_qkv_sum[2 * D :]]),
        sums["dy1"],
        g["ln2_gain"],
        g["ln2_bias"],
        sums["d_pre"],
        sums["dy2"],
    )
    small = jnp.concatenate([v.reshape(64, -1) for v in small], axis=1)
    small = lax.psum_scatter(small, CTX_FSDP, scatter_dimension=0, tiled=True)
    small = [small[:, a : a + n] for a, n in zip(starts, widths)]
    shape = (1, micro, 1, rows, D)
    return (
        acts.reshape(shape),
        in_grads.reshape(shape),
        small[0],
        small[1],
        qkv_w[None],
        small[2],
        out_w[None],
        small[3],
        small[4],
        small[5],
        fc_w[None],
        small[6],
        proj_w[None],
        small[7],
    )


def solution(mesh):
    torus = Mesh(
        mesh.devices.reshape(mesh.shape["section"], 2, 4, 4, 2),
        ("section", "ctx_0", "ctx_1", "fsdp_0", "fsdp_1"),
    )
    tokens = P(None, FSDP, CTX, None)
    vector = P("section", CTX_FSDP)
    matrix = P("section", CTX_FSDP, None)
    kinds = (vector, vector, matrix, vector, matrix, vector, vector, vector, matrix, vector, matrix, vector)
    results = P("section", None, FSDP, CTX, None)
    return jax.shard_map(
        on_device,
        mesh=torus,
        in_specs=(tokens, tokens, P()) + kinds,
        out_specs=(results, results) + kinds,
        check_vma=False,
    )
```

```python
import functools

import jax
import jax.numpy as jnp
from jax import lax
from jax.experimental import pallas as pl
from jax.experimental.pallas import tpu as pltpu
from jax.sharding import Mesh
from jax.sharding import PartitionSpec as P

D = 1024
HEADS = 16
HEAD_DIM = 64
FF = 4096
PAIRS = 8
PAIR = 128
QUAD = 256
TILE = 256
BLOCK = 64
CTX = ("ctx_0", "ctx_1")
FSDP = ("fsdp_0", "fsdp_1")
CTX_FSDP = CTX + FSDP
Y, Z, X, CORE = CTX_FSDP
EPSILON = 1e-05
MASKED = -1e30
SCALE = HEAD_DIM**-0.5
BF16 = jnp.bfloat16
F32 = jnp.float32
VMEM_LIMIT = 48 * 2**20


def dot(left, right):
    return jnp.dot(left, right, preferred_element_type=F32)


def dot_rows(left, right):
    return lax.dot_general(left, right, (((0,), (0,)), ((), ())), preferred_element_type=F32)


def dot_back(left, right):
    return lax.dot_general(left, right, (((1,), (1,)), ((), ())), preferred_element_type=F32)


def shift(value, axis, by):
    n = lax.axis_size(axis)
    return lax.ppermute(value, axis, [(i, (i + by) % n) for i in range(n)])


def swap_cores(value):
    return shift(value, CORE, 1)


def swap_y(value, section):
    at = 2 * section
    return lax.ppermute(value, ("section", Y), [(at, at + 1), (at + 1, at)])


def half(value, which, dim):
    size = value.shape[dim] // 2
    return lax.dynamic_slice_in_dim(value, which * size, size, dim)


def in_order(which, mine, other, dim):
    return jnp.where(
        which == 0,
        jnp.concatenate([mine, other], axis=dim),
        jnp.concatenate([other, mine], axis=dim),
    )


def spread(rows, first, second):
    both = jnp.stack([rows, shift(rows, Y, 1)])
    ring = jnp.stack([both] + [shift(both, first, k) for k in range(1, 4)])
    return [ring] + [shift(ring, second, k) for k in range(1, 4)]


def assemble_kernel(first, cuts, coords_ref, *refs):
    pieces, outs = refs[:4], refs[4:]
    y, me = coords_ref[0], coords_ref[1] if first == Z else coords_ref[2]
    for m in range(4):

        @pl.when(pl.program_id(0) == m)
        def _():
            for k in range(4):
                place = lax.rem(me + 4 - k, 4)
                for dy in range(2):
                    at_y = lax.rem(y + dy, 2)
                    for (start, width), out in zip(cuts, outs):
                        block = pieces[m][k, dy, :, start : start + width]
                        if first == Z:
                            out[at_y, place, 0] = block
                        else:
                            out[at_y, 0, place] = block


def assemble(coords, first, cuts, pieces):
    rows = pieces[0].shape[2]
    at = 2 if first == Z else 1

    def place(m, coords):
        ring = lax.rem(coords[at] + 4 - m, 4)
        return (0, 0, ring, 0, 0) if first == Z else (0, ring, 0, 0, 0)

    along = (2, 4, 1) if first == Z else (2, 1, 4)
    whole = pl.BlockSpec(pieces[0].shape, lambda m, coords: (0, 0, 0, 0))
    outs = pl.pallas_call(
        functools.partial(assemble_kernel, first, cuts),
        grid_spec=pltpu.PrefetchScalarGridSpec(
            num_scalar_prefetch=1,
            grid=(4,),
            in_specs=[whole] * 4,
            out_specs=[pl.BlockSpec((*along, rows, width), place) for _, width in cuts],
        ),
        out_shape=[jax.ShapeDtypeStruct((2, 4, 4, rows, width), BF16) for _, width in cuts],
        compiler_params=pltpu.CompilerParams(vmem_limit_bytes=VMEM_LIMIT),
    )(coords, *pieces)
    return [out.reshape(32 * rows, out.shape[-1]) for out in outs]


def weight_grad_kernel(n_jobs, first, coords_ref, *refs):
    jobs = [refs[4 * j : 4 * j + 4] for j in range(n_jobs)]
    outs, whole = refs[4 * n_jobs : 4 * n_jobs + 4], refs[-1]
    rows = whole.shape[2]
    at = 0
    for own_left, other_left, own_right, other_right in jobs:
        for start in range(0, own_right.shape[1], 256):
            columns = pl.ds(start, 256)
            grad = dot_rows(own_left[...], own_right[:, columns])
            grad += dot_rows(other_left[...], other_right[:, columns])
            whole[:, :, :, pl.ds(at + start, 256)] = grad.astype(BF16).reshape(4, 4, rows, 256)
        at += own_right.shape[1]
    me = coords_ref[1] if first == Z else coords_ref[2]
    for k in range(4):
        target = lax.rem(me + k, 4)
        outs[k][:, 0] = whole[target] if first == Z else whole[:, target]


def weight_grad(coords, first, jobs):
    rows = jobs[0][0].shape[1] // 32
    tokens = jobs[0][0].shape[0]
    columns = sum(job[5] for job in jobs)
    in_specs, arrays = [], []
    for *job, at, width in jobs:
        left = pl.BlockSpec((tokens, 16 * rows), lambda y, coords: (0, y))
        right = pl.BlockSpec((tokens, width), lambda y, coords, at=at: (0, at))
        in_specs += [left, left, right, right]
        arrays += job
    return pl.pallas_call(
        functools.partial(weight_grad_kernel, len(jobs), first),
        grid_spec=pltpu.PrefetchScalarGridSpec(
            num_scalar_prefetch=1,
            grid=(2,),
            in_specs=in_specs,
            out_specs=[pl.BlockSpec((4, 1, rows, columns), lambda y, coords: (0, y, 0, 0))] * 4,
            scratch_shapes=[pltpu.VMEM((4, 4, rows, columns), BF16)],
        ),
        out_shape=[jax.ShapeDtypeStruct((4, 2, rows, columns), BF16)] * 4,
        compiler_params=pltpu.CompilerParams(vmem_limit_bytes=VMEM_LIMIT),
    )(coords, *arrays)


def total(parts):
    return functools.reduce(lambda a, b: a + b, [p.astype(F32) for p in parts])


def sum_parts(parts, first, second):
    arrived = [shift(parts[k], first, k) for k in (2, 1, 3)]
    part = total([parts[0]] + arrived).astype(BF16)
    me = lax.axis_index(second)
    chunks = [lax.dynamic_index_in_dim(part, (me + k) % 4, 0, keepdims=False) for k in range(4)]
    arrived = [shift(chunks[k], second, k) for k in (2, 1, 3)]
    part = total([chunks[0]] + arrived).astype(BF16)
    y = lax.axis_index(Y)
    mine = lax.dynamic_index_in_dim(part, y, 0, keepdims=False)
    other = lax.dynamic_index_in_dim(part, 1 - y, 0, keepdims=False)
    return total([mine, shift(other, Y, 1)])


def layer_norm(values, gain, bias):
    average = jnp.mean(values, axis=-1, keepdims=True)
    centred = values - average
    spread_of = jnp.mean(centred * centred, axis=-1, keepdims=True)
    inverse = lax.rsqrt(spread_of + EPSILON)
    normal = centred * inverse
    return normal * gain + bias, normal, inverse


def norm_back(upstream, normal, inverse, gain):
    scaled = upstream * gain
    first = jnp.mean(scaled, axis=-1, keepdims=True)
    second = jnp.mean(scaled * normal, axis=-1, keepdims=True)
    return (
        inverse * (scaled - first - normal * second),
        jnp.sum(upstream * normal, axis=0),
        jnp.sum(upstream, axis=0),
    )


def head_lanes(shape, head):
    return lax.broadcasted_iota(jnp.int32, shape, 1) // HEAD_DIM == head


def causal(keys):
    rows = lax.broadcasted_iota(jnp.int32, (keys, TILE), 0)
    columns = lax.broadcasted_iota(jnp.int32, (keys, TILE), 1)
    return rows <= columns + (keys - TILE)


def stored_blocks(order_ref, coords_ref):
    y, c = coords_ref[0], coords_ref[3]
    for dy in range(2):
        for dc in range(2):
            for z in range(4):
                stored = lax.rem(y + dy, 2) * 8 + z * 2 + lax.rem(c + dc, 2)
                at = pl.multiple_of(order_ref[stored] * BLOCK, BLOCK)
                yield dy, dc, slice(z * BLOCK, (z + 1) * BLOCK), pl.ds(at, BLOCK)


def attention_kernel(order_ref, coords_ref, qkv_own, qkv_far, out_own, out_far, lse_ref, q, k, v, out):
    for dy, dc, rows, place in stored_blocks(order_ref, coords_ref):
        ref = (qkv_own, qkv_far)[dy]
        q[place, :] = ref[dc, rows, 0:PAIR]
        k[place, :] = ref[dc, rows, PAIR : 2 * PAIR] * SCALE
        v[place, :] = ref[dc, rows, 2 * PAIR :]
    length = q.shape[0]
    lse_ref[...] = jnp.zeros_like(lse_ref)
    for tile in range(length // TILE):
        keys = (tile + 1) * TILE
        here = pl.ds(tile * TILE, TILE)
        outs = []
        for head in range(2):
            queries = q[here, :]
            queries = jnp.where(head_lanes(queries.shape, head), queries, jnp.zeros_like(queries))
            scores = dot_back(k[0:keys, :], queries)
            scores = jnp.where(causal(keys), scores, MASKED)
            highest = jnp.max(scores, axis=0, keepdims=True)
            probs = jnp.exp(scores - highest)
            total_of = jnp.sum(probs, axis=0, keepdims=True)
            lse_ref[0, head : head + 1, here] = highest + jnp.log(total_of)
            attended = dot_rows(v[0:keys, :], probs.astype(BF16)) / total_of
            outs.append(attended[head * HEAD_DIM : (head + 1) * HEAD_DIM, :])
        out[here, :] = jnp.concatenate(outs, axis=0).T.astype(BF16)
    for dy, dc, rows, place in stored_blocks(order_ref, coords_ref):
        (out_own, out_far)[dy][dc, rows, :] = out[place, :]


def attention_back_kernel(
    order_ref, coords_ref, qkv_own, qkv_far, grad_own, grad_far, lse_ref, out_own, out_far, q, k, v, g, dq, dk, dv
):
    for dy, dc, rows, place in stored_blocks(order_ref, coords_ref):
        ref = (qkv_own, qkv_far)[dy]
        q[place, :] = ref[dc, rows, 0:PAIR]
        k[place, :] = ref[dc, rows, PAIR : 2 * PAIR] * SCALE
        v[place, :] = ref[dc, rows, 2 * PAIR :]
        g[place, :] = (grad_own, grad_far)[dy][dc, rows, :]
    length = q.shape[0]
    dk[...] = jnp.zeros_like(dk)
    dv[...] = jnp.zeros_like(dv)
    for tile in range(length // TILE):
        keys = (tile + 1) * TILE
        here = pl.ds(tile * TILE, TILE)
        outs = []
        for head in range(2):
            lanes = head_lanes((TILE, PAIR), head)
            queries = q[here, :]
            queries = jnp.where(lanes, queries, jnp.zeros_like(queries))
            grads = g[here, :]
            grads = jnp.where(lanes, grads, jnp.zeros_like(grads))
            scores = dot_back(k[0:keys, :], queries)
            probs = jnp.exp(scores - lse_ref[0, head : head + 1, here])
            probs = jnp.where(causal(keys), probs, 0.0)
            grad_probs = dot_back(v[0:keys, :], grads)
            term = jnp.sum(probs * grad_probs, axis=0, keepdims=True)
            grad_scores = (probs * (grad_probs - term)).astype(BF16)
            dv[0:keys, :] += dot(probs.astype(BF16), grads)
            dk[0:keys, :] += dot(grad_scores, queries)
            grad_q = dot_rows(k[0:keys, :], grad_scores)
            outs.append(grad_q[head * HEAD_DIM : (head + 1) * HEAD_DIM, :])
        dq[here, :] = jnp.concatenate(outs, axis=0).T
    for dy, dc, rows, place in stored_blocks(order_ref, coords_ref):
        ref = (out_own, out_far)[dy]
        ref[dc, rows, 0:PAIR] = dq[place, :].astype(BF16)
        ref[dc, rows, PAIR : 2 * PAIR] = (dk[place, :] * SCALE).astype(BF16)
        ref[dc, rows, 2 * PAIR :] = dv[place, :].astype(BF16)


def per_pair(tokens, width):
    return pl.BlockSpec((2, tokens, width), lambda pair, order, coords: (0, 0, pair))


def lse_block(length):
    return pl.BlockSpec((1, 8, length), lambda pair, order, coords: (pair, 0, 0))


def attention(order, coords, own, far):
    tokens = own.shape[1]
    length = 4 * tokens
    return pl.pallas_call(
        attention_kernel,
        grid_spec=pltpu.PrefetchScalarGridSpec(
            num_scalar_prefetch=2,
            grid=(2,),
            in_specs=[per_pair(tokens, 3 * PAIR)] * 2,
            out_specs=[per_pair(tokens, PAIR)] * 2 + [lse_block(length)],
            scratch_shapes=[pltpu.VMEM((length, PAIR), BF16)] * 4,
        ),
        out_shape=[jax.ShapeDtypeStruct((2, tokens, QUAD), BF16)] * 2
        + [jax.ShapeDtypeStruct((2, 8, length), F32)],
        compiler_params=pltpu.CompilerParams(vmem_limit_bytes=VMEM_LIMIT),
    )(order, coords, own, far)


def attention_back(order, coords, own, far, grad_own, grad_far, lse):
    tokens = own.shape[1]
    length = 4 * tokens
    return pl.pallas_call(
        attention_back_kernel,
        grid_spec=pltpu.PrefetchScalarGridSpec(
            num_scalar_prefetch=2,
            grid=(2,),
            in_specs=[per_pair(tokens, 3 * PAIR)] * 2 + [per_pair(tokens, PAIR)] * 2 + [lse_block(length)],
            out_specs=[per_pair(tokens, 3 * PAIR)] * 2,
            scratch_shapes=[pltpu.VMEM((length, PAIR), BF16)] * 4
            + [pltpu.VMEM((length, PAIR), F32)] * 3,
        ),
        out_shape=[jax.ShapeDtypeStruct((2, tokens, 3 * QUAD), BF16)] * 2,
        compiler_params=pltpu.CompilerParams(vmem_limit_bytes=VMEM_LIMIT),
    )(order, coords, own, far, grad_own, grad_far, lse)


def to_heads(mine, other, active, old):
    y = lax.axis_index(Y)
    both = jnp.stack([mine, swap_cores(other)])
    far = swap_y(half(both, 1 - y, 2), active)
    if old is not None:
        far = jnp.where(lax.axis_index("section") == active, far, old)
    return half(both, y, 2), far


def to_tokens(own, far, active, old):
    got = swap_y(far, active)
    if old is not None:
        got = jnp.where(lax.axis_index("section") == active, got, old)
    both = in_order(lax.axis_index(Y), own, got, 2)
    return both[0], swap_cores(both[1]), got


def layer_forward(hidden, w, order, coords, active, old):
    core = coords[3]
    normed, normal1, inverse1 = layer_norm(hidden, w["ln1_gain"], w["ln1_bias"])
    normed = normed.astype(BF16)
    mine, other = (
        jnp.concatenate(
            [
                (dot(normed, quad) + half(w["qkv_bias"][i], j, 0)).astype(BF16)
                for j, quad in enumerate(w["qkv"][i])
            ],
            axis=1,
        )
        for i in range(2)
    )
    own, far = to_heads(mine, other, active, old and old["far"])
    heads_own, heads_far, lse = attention(order, coords, own, far)
    mine, other, got = to_tokens(heads_own, heads_far, active, old and old["got"])
    attended = in_order(core, mine, other, 1)
    added = in_order(core, dot(attended, w["out"][0]), dot(attended, w["out"][1]), 1)
    middle = hidden + (added + w["out_bias"])
    normed2, normal2, inverse2 = layer_norm(middle, w["ln2_gain"], w["ln2_bias"])
    normed2 = normed2.astype(BF16)
    before = [dot(normed2, w["fc"][i]) + w["fc_bias"][i] for i in range(2)]
    activated = [jax.nn.gelu(u, approximate=True).astype(BF16) for u in before]
    added = dot(activated[0], w["proj"][0]) + dot(activated[1], w["proj"][1])
    result = middle + (added + w["proj_bias"])
    saved = dict(
        normed=normed,
        normal1=normal1,
        inverse1=inverse1,
        own=own,
        far=far,
        got=got,
        lse=lse,
        attended=attended,
        normal2=normal2,
        inverse2=inverse2,
        normed2=normed2,
        before=before,
        activated=activated,
    )
    return result, saved


def layer_backward(upstream, s, w, order, coords, active, old):
    core = coords[3]
    dy2 = upstream.astype(BF16)
    d_pre = []
    for i in range(2):
        grad_act = dot_back(dy2, w["proj"][i])
        back = jax.vjp(lambda u: jax.nn.gelu(u, approximate=True), s["before"][i])[1]
        d_pre.append(back(grad_act)[0].astype(BF16))
    d_normed2 = dot_back(d_pre[0], w["fc"][0]) + dot_back(d_pre[1], w["fc"][1])
    through, ln2_gain, ln2_bias = norm_back(d_normed2, s["normal2"], s["inverse2"], w["ln2_gain"])
    d_mid = upstream + through
    dy1 = d_mid.astype(BF16)
    dy1_mine = half(dy1, core, 1)
    dy1_other = half(dy1, 1 - core, 1)
    d_att = (dot_back(dy1_mine, w["out"][0]) + dot_back(dy1_other, w["out"][1])).astype(BF16)
    grad_own, grad_far = to_heads(half(d_att, core, 1), half(d_att, 1 - core, 1), active, old and old["far"])
    back_own, back_far = attention_back(order, coords, s["own"], s["far"], grad_own, grad_far, s["lse"])
    d_qkv_mine, d_qkv_other, got = to_tokens(back_own, back_far, active, old and old["got"])
    d_normed = sum(
        dot_back(half(grad, j, 1), w["qkv"][i][j])
        for i, grad in enumerate((d_qkv_mine, d_qkv_other))
        for j in range(2)
    )
    through, ln1_gain, ln1_bias = norm_back(d_normed, s["normal1"], s["inverse1"], w["ln1_gain"])
    d_hidden = d_mid + through
    return d_hidden, dict(
        far=grad_far,
        got=got,
        dy2=dy2,
        d_pre=d_pre,
        dy1=dy1,
        dy1_mine=dy1_mine,
        dy1_other=dy1_other,
        d_qkv=(d_qkv_mine, d_qkv_other),
        ln1_gain=ln1_gain,
        ln1_bias=ln1_bias,
        ln2_gain=ln2_gain,
        ln2_bias=ln2_bias,
    )


def to_sequence(values, core):
    micro, rows, width = values.shape
    cut = values.reshape(micro, 2, rows // 2, width)
    keep = lax.dynamic_index_in_dim(cut, core, 1)
    got = swap_cores(lax.dynamic_index_in_dim(cut, 1 - core, 1))
    each = in_order(core, keep, got, 1).reshape(2 * micro, rows // 2, width)
    return lax.all_to_all(each, Z, 0, 0, tiled=True).reshape(2 * rows, width)


def from_sequence(values, core):
    tokens, width = values.shape
    back = lax.all_to_all(values.reshape(4, tokens // 4, width), Z, 0, 0, tiled=True)
    each = back.reshape(2, 2, tokens // 4, width)
    keep = lax.dynamic_index_in_dim(each, core, 1)
    got = swap_cores(lax.dynamic_index_in_dim(each, 1 - core, 1))
    return in_order(core, keep, got, 1).reshape(2, tokens // 2, width)


def by_pair(values):
    lead = values.shape[:-1]
    return values.reshape(*lead, 3, PAIRS, PAIR).swapaxes(-2, -3).reshape(*lead, 3 * D)


def by_part(values):
    lead = values.shape[:-1]
    return values.reshape(*lead, PAIRS, 3, PAIR).swapaxes(-2, -3).reshape(*lead, 3 * D)


def by_core(values):
    lead = values.shape[:-1]
    return values.reshape(*lead, 32, 2, 64).swapaxes(-2, -3).reshape(*lead, FF)


def from_core(values):
    lead = values.shape[:-1]
    return values.reshape(*lead, 2, 32, 64).swapaxes(-2, -3).reshape(*lead, FF)


def on_device(
    inputs,
    cotangent,
    block_order,
    ln1_gain,
    ln1_bias,
    qkv_weight,
    qv_bias,
    out_weight,
    out_bias,
    ln2_gain,
    ln2_bias,
    fc_weight,
    fc_bias,
    proj_weight,
    proj_bias,
):
    section = lax.axis_index("section")
    core = lax.axis_index(CORE)
    coords = jnp.stack([lax.axis_index(a) for a in CTX_FSDP]).astype(jnp.int32)
    first = section == 0
    micro, _, rows, _ = inputs.shape

    vectors = (ln1_gain, ln1_bias, qv_bias, out_bias, ln2_gain, ln2_bias, fc_bias, proj_bias)
    widths = [v.shape[-1] for v in vectors]
    starts = [sum(widths[:i]) for i in range(len(widths))]
    packed = jnp.concatenate([v.reshape(-1) for v in vectors])
    packed = jnp.pad(packed, (0, 16 * 128 - packed.shape[0])).reshape(16, 128)

    qkv_cut = by_pair(qkv_weight[0]).reshape(16, 2, 2, 768)
    out_cut = out_weight[0].reshape(16, 2, 2, 256)
    fc_cut = by_core(fc_weight[0]).reshape(16, 2, 2048)
    halves = [
        jnp.concatenate(
            [qkv_cut[:, i, 0], out_cut[:, i, 0], packed, qkv_cut[:, i, 1], out_cut[:, i, 1], fc_cut[:, i]],
            axis=1,
        )
        for i in range(2)
    ]
    mine = jnp.where(core == 0, halves[0], halves[1])
    other = jnp.where(core == 0, halves[1], halves[0])
    blob = in_order(core, mine, swap_cores(other), 0)
    entry = to_sequence(inputs[:, 0], core)

    cuts = ((0, 768), (768, 256))
    qkv_0, out_0, packed = assemble(coords, X, cuts + ((1024, 128),), spread(blob[:, :1152], X, Z))
    qkv_1, out_1 = assemble(coords, Z, cuts, spread(blob[:, 1152:2176], Z, X))
    (fc_own,) = assemble(coords, X, ((0, 2048),), spread(blob[:, 2176:], X, Z))
    (proj_own,) = assemble(coords, Z, ((0, 1024),), spread(proj_weight[0], Z, X))
    out_own = jnp.concatenate([out_0, out_1], axis=1)
    w = {name: (own, swap_cores(own)) for name, own in (("out", out_own), ("fc", fc_own), ("proj", proj_own))}
    w["qkv"] = ((qkv_0, qkv_1), (swap_cores(qkv_0), swap_cores(qkv_1)))
    packed = packed.reshape(32, 2, 16, 128)[:, :, :2].reshape(64, 256)
    names = ("ln1_gain", "ln1_bias", "qv", "out_bias", "ln2_gain", "ln2_bias", "fc", "proj_bias")
    vector = {
        name: packed[:, start : start + width].reshape(-1).astype(F32)
        for name, start, width in zip(names, starts, widths)
    }
    qv, fc_vector = vector.pop("qv"), by_core(vector.pop("fc"))
    qkv_vector = by_pair(jnp.concatenate([qv[:D], jnp.zeros((D,), F32), qv[D:]]))
    w.update(vector)
    w["qkv_bias"] = (half(qkv_vector, core, 0), half(qkv_vector, 1 - core, 0))
    w["fc_bias"] = (half(fc_vector, core, 0), half(fc_vector, 1 - core, 0))

    result, early = layer_forward(entry.astype(F32), w, block_order, coords, 0, None)
    arriving = lax.ppermute(result.astype(BF16), "section", [(0, 1)])
    entry = jnp.where(first, entry, arriving)
    result, saved = layer_forward(entry.astype(F32), w, block_order, coords, 1, early)
    acts = from_sequence(result.astype(BF16), core)

    given = to_sequence(cotangent[:, 0], core)
    d_hidden, early = layer_backward(given.astype(F32), saved, w, block_order, coords, 1, None)
    arriving = lax.ppermute(d_hidden.astype(BF16), "section", [(1, 0)])
    upstream = jnp.where(first, arriving, given).astype(F32)
    d_hidden, g = layer_backward(upstream, saved, w, block_order, coords, 0, early)
    in_grads = jnp.where(first, d_hidden, d_hidden.astype(BF16).astype(F32))
    in_grads = from_sequence(in_grads, core)

    act = saved["activated"]
    jobs = [(act[0], swap_cores(act[1]), g["dy2"], swap_cores(g["dy2"]), 0, 1024)]
    proj_grad = sum_parts(weight_grad(coords, Z, jobs), Z, X)
    jobs = [(saved["normed2"], swap_cores(saved["normed2"]), g["d_pre"][0], swap_cores(g["d_pre"][1]), 0, 2048)]
    fc_grad = sum_parts(weight_grad(coords, X, jobs), X, Z)
    qkv_pair = (saved["normed"], swap_cores(saved["normed"]), g["d_qkv"][0], swap_cores(g["d_qkv"][1]))
    out_pair = (saved["attended"], swap_cores(saved["attended"]), g["dy1_mine"], swap_cores(g["dy1_other"]))
    last = [
        sum_parts(weight_grad(coords, a, [qkv_pair + (i, 768), out_pair + (i, 256)]), a, b)
        for i, (a, b) in enumerate(((Z, X), (X, Z)))
    ]
    grads = jnp.concatenate(
        [last[0][:, :768], last[1][:, :768], last[0][:, 768:], last[1][:, 768:], fc_grad], axis=1
    )
    mine = half(grads, core, 0)
    other = swap_cores(half(grads, 1 - core, 0))
    qkv_grad = by_part(in_order(core, mine[:, :1536], other[:, :1536], 1))
    out_grad = in_order(core, mine[:, 1536:2048], other[:, 1536:2048], 1)
    fc_grad = from_core(in_order(core, mine[:, 2048:], other[:, 2048:], 1))

    sums = {
        n: jnp.sum(g[n].astype(F32), axis=0) for n in ("dy2", "dy1")
    }
    d_pre_sum = from_core(in_order(core, *[jnp.sum(v.astype(F32), axis=0) for v in g["d_pre"]], 0))
    d_qkv_sum = by_part(in_order(core, *[jnp.sum(v.astype(F32), axis=0) for v in g["d_qkv"]], 0))
    small = (
        g["ln1_gain"],
        g["ln1_bias"],
        jnp.concatenate([d_qkv_sum[:D], d_qkv_sum[2 * D :]]),
        sums["dy1"],
        g["ln2_gain"],
        g["ln2_bias"],
        d_pre_sum,
        sums["dy2"],
    )
    small = jnp.concatenate([v.reshape(64, -1) for v in small], axis=1)
    small = jnp.sum(lax.all_to_all(small, CTX_FSDP, 0, 0, tiled=True), axis=0, keepdims=True)
    small = [small[:, a : a + n] for a, n in zip(starts, widths)]
    shape = (1, micro, 1, rows, D)
    return (
        acts.reshape(shape),
        in_grads.reshape(shape),
        small[0],
        small[1],
        qkv_grad[None],
        small[2],
        out_grad[None],
        small[3],
        small[4],
        small[5],
        fc_grad[None],
        small[6],
        proj_grad[None],
        small[7],
    )


def solution(mesh):
    torus = Mesh(
        mesh.devices.reshape(mesh.shape["section"], 2, 4, 4, 2),
        ("section", "ctx_0", "ctx_1", "fsdp_0", "fsdp_1"),
    )
    tokens = P(None, FSDP, CTX, None)
    vector = P("section", CTX_FSDP)
    matrix = P("section", CTX_FSDP, None)
    kinds = (vector, vector, matrix, vector, matrix, vector, vector, vector, matrix, vector, matrix, vector)
    results = P("section", None, FSDP, CTX, None)
    return jax.shard_map(
        on_device,
        mesh=torus,
        in_specs=(tokens, tokens, P()) + kinds,
        out_specs=(results, results) + kinds,
        check_vma=False,
    )
```

```python
import functools

import jax
import jax.numpy as jnp
from jax import lax
from jax.experimental import pallas as pl
from jax.experimental.pallas import tpu as pltpu
from jax.sharding import Mesh
from jax.sharding import PartitionSpec as P

D = 1024
HEADS = 16
HEAD_DIM = 64
FF = 4096
PAIRS = 8
PAIR = 128
QUAD = 256
TILE = 256
BLOCK = 64
CTX = ("ctx_0", "ctx_1")
FSDP = ("fsdp_0", "fsdp_1")
CTX_FSDP = CTX + FSDP
Y, Z, X, CORE = CTX_FSDP
EPSILON = 1e-05
MASKED = -1e30
SCALE = HEAD_DIM**-0.5
BF16 = jnp.bfloat16
F32 = jnp.float32
VMEM_LIMIT = 24 * 2**20
FREE = pl.CostEstimate(flops=0, bytes_accessed=0, transcendentals=0)
SOME = pl.CostEstimate(flops=2 * 10**9, bytes_accessed=8 * 10**6, transcendentals=0)


def dot(left, right):
    return jnp.dot(left, right, preferred_element_type=F32)


def dot_rows(left, right):
    return lax.dot_general(left, right, (((0,), (0,)), ((), ())), preferred_element_type=F32)


def dot_back(left, right):
    return lax.dot_general(left, right, (((1,), (1,)), ((), ())), preferred_element_type=F32)


def shift(value, axis, by):
    n = lax.axis_size(axis)
    return lax.ppermute(value, axis, [(i, (i + by) % n) for i in range(n)])


def swap_cores(value):
    return shift(value, CORE, 1)


def swap_y(value, section):
    at = 2 * section
    return lax.ppermute(value, ("section", Y), [(at, at + 1), (at + 1, at)])


def half(value, which, dim):
    size = value.shape[dim] // 2
    return lax.dynamic_slice_in_dim(value, which * size, size, dim)


def in_order(which, mine, other, dim):
    return jnp.where(
        which == 0,
        jnp.concatenate([mine, other], axis=dim),
        jnp.concatenate([other, mine], axis=dim),
    )


def both_y(rows):
    return jnp.stack([rows, shift(rows, Y, 1)])


def first_ring(both, axis):
    return jnp.stack([both] + [shift(both, axis, k) for k in range(1, 4)])


def second_ring(ring, axis):
    return [ring] + [shift(ring, axis, k) for k in (2, 1, 3)]


def to_neighbours(ring, axis):
    return shift(ring, axis, 1), shift(ring, axis, -1)


def past_neighbours(low, high, axis):
    size = low.shape[0] // 2
    return jnp.concatenate([shift(low[:size], axis, 1), shift(high[size:], axis, -1)])


def assemble_kernel(first, cuts, coords_ref, *refs):
    pieces, outs = refs[:4], refs[4:]
    y, me = coords_ref[0], coords_ref[1] if first == Z else coords_ref[2]
    for m in range(4):

        @pl.when(pl.program_id(0) == m)
        def _():
            for k in range(4):
                place = lax.rem(me + 4 - k, 4)
                for dy in range(2):
                    at_y = lax.rem(y + dy, 2)
                    for start, width, out, row in cuts:
                        block = pieces[m][k, dy, :, start : start + width]
                        rows = pl.ds(row, block.shape[0])
                        if first == Z:
                            outs[out][at_y, place, 0, rows] = block
                        else:
                            outs[out][at_y, 0, place, rows] = block


def assemble(coords, first, cuts, pieces):
    rows = pieces[0].shape[2]
    at = 2 if first == Z else 1
    shapes = {}
    for _, width, out, row in cuts:
        shapes[out] = (row + rows, width)
    shapes = [shapes[out] for out in range(len(shapes))]

    def place(m, coords):
        by = jnp.where(m == 1, 2, jnp.where(m == 2, 1, m))
        ring = lax.rem(coords[at] + 4 - by, 4)
        return (0, 0, ring, 0, 0) if first == Z else (0, ring, 0, 0, 0)

    along = (2, 4, 1) if first == Z else (2, 1, 4)
    whole = pl.BlockSpec(pieces[0].shape, lambda m, coords: (0, 0, 0, 0))
    outs = pl.pallas_call(
        functools.partial(assemble_kernel, first, cuts),
        grid_spec=pltpu.PrefetchScalarGridSpec(
            num_scalar_prefetch=1,
            grid=(4,),
            in_specs=[whole] * 4,
            out_specs=[pl.BlockSpec((*along, *shape), place) for shape in shapes],
        ),
        out_shape=[jax.ShapeDtypeStruct((2, 4, 4, *shape), BF16) for shape in shapes],
        compiler_params=pltpu.CompilerParams(vmem_limit_bytes=VMEM_LIMIT),
        cost_estimate=FREE,
    )(coords, *pieces)
    return [out.reshape(-1, out.shape[-1]) for out in outs]


def weight_grad_kernel(n_jobs, first, coords_ref, *refs):
    jobs = [refs[4 * j : 4 * j + 4] for j in range(n_jobs)]
    outs, whole = refs[4 * n_jobs : 4 * n_jobs + 4], refs[-1]
    rows = whole.shape[2]
    at = 0
    for own_left, other_left, own_right, other_right in jobs:
        for own, other in zip(column_parts(own_right), column_parts(other_right)):
            grad = dot_rows(own_left[...], own()) + dot_rows(other_left[...], other())
            width = grad.shape[1]
            whole[:, :, :, pl.ds(at, width)] = grad.astype(BF16).reshape(4, 4, rows, width)
            at += width
    me = coords_ref[1] if first == Z else coords_ref[2]
    for k in range(4):
        target = lax.rem(me + k, 4)
        outs[k][:, 0] = whole[target] if first == Z else whole[:, target]


def column_parts(ref):
    if len(ref.shape) == 4:
        return [lambda t=t: ref[0, t] for t in range(2)]
    return [lambda at=at: ref[:, pl.ds(at, 256)] for at in range(0, ref.shape[1], 256)]


def weight_grad(coords, first, jobs):
    rows = jobs[0][0].shape[1] // 32
    tokens = jobs[0][0].shape[0]
    columns = 0
    in_specs, arrays = [], []
    for *job, at, width in jobs:
        left = pl.BlockSpec((tokens, 16 * rows), lambda y, coords: (0, y))
        if job[2].ndim == 4:
            shape = (1, *job[2].shape[1:])
            right = pl.BlockSpec(shape, lambda y, coords, at=at: (lax.rem(coords[0] + at, 2), 0, 0, 0))
        else:
            right = pl.BlockSpec((tokens, width), lambda y, coords, at=at: (0, at))
        columns += width
        in_specs += [left, left, right, right]
        arrays += job
    return pl.pallas_call(
        functools.partial(weight_grad_kernel, len(jobs), first),
        grid_spec=pltpu.PrefetchScalarGridSpec(
            num_scalar_prefetch=1,
            grid=(2,),
            in_specs=in_specs,
            out_specs=[pl.BlockSpec((4, 1, rows, columns), lambda y, coords: (0, y, 0, 0))] * 4,
            scratch_shapes=[pltpu.VMEM((4, 4, rows, columns), BF16)],
        ),
        out_shape=[pltpu.HBM((4, 2, rows, columns), BF16)] * 4,
        compiler_params=pltpu.CompilerParams(vmem_limit_bytes=VMEM_LIMIT),
        cost_estimate=SOME if columns == FF // 2 else FREE,
    )(coords, *arrays)


def plain_grad_kernel(own_left, other_left, own_right, other_right, out):
    grad = dot_rows(own_left[...], own_right[...])
    out[...] = (grad + dot_rows(other_left[...], other_right[...])).astype(BF16)


def plain_grad(own_left, other_left, own_right, other_right):
    tokens, rows = own_left.shape
    columns = own_right.shape[1]
    block = 512
    left = pl.BlockSpec((tokens, block), lambda i: (0, i))
    right = pl.BlockSpec((tokens, columns), lambda i: (0, 0))
    return pl.pallas_call(
        plain_grad_kernel,
        grid=(rows // block,),
        in_specs=[left, left, right, right],
        out_specs=pl.BlockSpec((block, columns), lambda i: (i, 0)),
        out_shape=pltpu.HBM((rows, columns), BF16),
        compiler_params=pltpu.CompilerParams(vmem_limit_bytes=VMEM_LIMIT),
        cost_estimate=SOME,
    )(own_left, other_left, own_right, other_right)


def sum_by_axes(parts, axes):
    for axis in axes:
        parts = lax.psum_scatter(parts, axis, scatter_dimension=0, tiled=False)
    return parts


def total(parts):
    return functools.reduce(lambda a, b: a + b, [p.astype(F32) for p in parts])


def start_sum(parts, first):
    return [parts[0]] + [shift(parts[k], first, k) for k in (2, 1, 3)]


def relay_far(parts, axis):
    size = parts[2].shape[0] // 2
    return shift(parts[2][:size], axis, 1), shift(parts[2][size:], axis, -1)


def relay_kernel(up, low, down, high, up_out, down_out):
    up_out[...] = total([up[...], low[...]]).astype(BF16)
    down_out[...] = total([down[...], high[...]]).astype(BF16)


def relay_near(parts, low, high, axis):
    rest = (0,) * (low.ndim - 1)
    first = pl.BlockSpec(low.shape, lambda i: (0, *rest))
    second = pl.BlockSpec(low.shape, lambda i: (1, *rest))
    up, down = pl.pallas_call(
        relay_kernel,
        grid=(1,),
        in_specs=[first, first, second, first],
        out_specs=[first, second],
        out_shape=[pltpu.HBM(parts[1].shape, BF16)] * 2,
        input_output_aliases={0: 0, 2: 1},
        compiler_params=pltpu.CompilerParams(vmem_limit_bytes=VMEM_LIMIT),
        cost_estimate=FREE,
    )(parts[1], low, parts[3], high)
    return shift(up, axis, 1), shift(down, axis, -1)


def second_sum(part, second):
    part = part.astype(BF16)
    me = lax.axis_index(second)
    chunks = [lax.dynamic_index_in_dim(part, (me + k) % 4, 0, keepdims=False) for k in range(4)]
    return [chunks[0]] + [shift(chunks[k], second, k) for k in (2, 1, 3)]


def last_sum(part):
    y = lax.axis_index(Y)
    part = part.astype(BF16)
    mine = lax.dynamic_index_in_dim(part, y, 0, keepdims=False)
    other = lax.dynamic_index_in_dim(part, 1 - y, 0, keepdims=False)
    return total([mine, shift(other, Y, 1)])


def layer_norm(values, gain, bias):
    average = jnp.mean(values, axis=-1, keepdims=True)
    centred = values - average
    spread_of = jnp.mean(centred * centred, axis=-1, keepdims=True)
    inverse = lax.rsqrt(spread_of + EPSILON)
    normal = centred * inverse
    return normal * gain + bias, normal, inverse


def norm_back(upstream, normal, inverse, gain):
    scaled = upstream * gain
    first = jnp.mean(scaled, axis=-1, keepdims=True)
    second = jnp.mean(scaled * normal, axis=-1, keepdims=True)
    return (
        inverse * (scaled - first - normal * second),
        jnp.sum(upstream * normal, axis=0),
        jnp.sum(upstream, axis=0),
    )


def head_lanes(shape, head):
    return lax.broadcasted_iota(jnp.int32, shape, 1) // HEAD_DIM == head


def causal(keys):
    rows = lax.broadcasted_iota(jnp.int32, (keys, TILE), 0)
    columns = lax.broadcasted_iota(jnp.int32, (keys, TILE), 1)
    return rows <= columns + (keys - TILE)


def stored_blocks(order_ref, coords_ref, near, far):
    y, c = coords_ref[0], coords_ref[3]
    for dy in range(2):
        for dc in range(2):
            for z in range(4):
                stored = lax.rem(y + dy, 2) * 8 + z * 2 + lax.rem(c + dc, 2)
                at = pl.multiple_of(order_ref[stored] * BLOCK, BLOCK)
                ref = near[dc] if dy == 0 else far.at[dc]
                yield ref, slice(z * BLOCK, (z + 1) * BLOCK), pl.ds(at, BLOCK)


def attention_kernel(order_ref, coords_ref, own, got, far, out_near, out_far, lse_ref, q, k, v, out):
    near = (own.at[0, 0], got.at[0, 0])
    for ref, rows, place in stored_blocks(order_ref, coords_ref, near, far):
        q[place, :] = ref[rows, 0:PAIR]
        k[place, :] = ref[rows, PAIR : 2 * PAIR] * SCALE
        v[place, :] = ref[rows, 2 * PAIR :]
    length = q.shape[0]
    lse_ref[...] = jnp.zeros_like(lse_ref)
    for tile in range(length // TILE):
        keys = (tile + 1) * TILE
        here = pl.ds(tile * TILE, TILE)
        outs = []
        for head in range(2):
            queries = q[here, :]
            queries = jnp.where(head_lanes(queries.shape, head), queries, jnp.zeros_like(queries))
            scores = dot_back(k[0:keys, :], queries)
            scores = jnp.where(causal(keys), scores, MASKED)
            highest = jnp.max(scores, axis=0, keepdims=True)
            probs = jnp.exp(scores - highest)
            total_of = jnp.sum(probs, axis=0, keepdims=True)
            lse_ref[head : head + 1, here] = highest + jnp.log(total_of)
            attended = dot_rows(v[0:keys, :], probs.astype(BF16)) / total_of
            outs.append(attended[head * HEAD_DIM : (head + 1) * HEAD_DIM, :])
        out[here, :] = jnp.concatenate(outs, axis=0).T.astype(BF16)
    near = (out_near.at[0], out_near.at[1])
    for ref, rows, place in stored_blocks(order_ref, coords_ref, near, out_far):
        ref[rows, :] = out[place, :]


def attention_back_kernel(
    order_ref, coords_ref, own, got, far, grad_own, grad_got, grad_far, lse_ref, out_near, out_far, q, k, v, g, dq, dk, dv
):
    near = (own.at[0, 0], got.at[0, 0])
    for ref, rows, place in stored_blocks(order_ref, coords_ref, near, far):
        q[place, :] = ref[rows, 0:PAIR]
        k[place, :] = ref[rows, PAIR : 2 * PAIR] * SCALE
        v[place, :] = ref[rows, 2 * PAIR :]
    near = (grad_own.at[0, 0], grad_got.at[0, 0])
    for ref, rows, place in stored_blocks(order_ref, coords_ref, near, grad_far):
        g[place, :] = ref[rows, :]
    length = q.shape[0]
    dk[...] = jnp.zeros_like(dk)
    dv[...] = jnp.zeros_like(dv)
    for tile in range(length // TILE):
        keys = (tile + 1) * TILE
        here = pl.ds(tile * TILE, TILE)
        outs = []
        for head in range(2):
            lanes = head_lanes((TILE, PAIR), head)
            queries = q[here, :]
            queries = jnp.where(lanes, queries, jnp.zeros_like(queries))
            grads = g[here, :]
            grads = jnp.where(lanes, grads, jnp.zeros_like(grads))
            scores = dot_back(k[0:keys, :], queries)
            probs = jnp.exp(scores - lse_ref[head : head + 1, here])
            probs = jnp.where(causal(keys), probs, 0.0)
            grad_probs = dot_back(v[0:keys, :], grads)
            term = jnp.sum(probs * grad_probs, axis=0, keepdims=True)
            grad_scores = (probs * (grad_probs - term)).astype(BF16)
            dv[0:keys, :] += dot(probs.astype(BF16), grads)
            dk[0:keys, :] += dot(grad_scores, queries)
            grad_q = dot_rows(k[0:keys, :], grad_scores)
            outs.append(grad_q[head * HEAD_DIM : (head + 1) * HEAD_DIM, :])
        dq[here, :] = jnp.concatenate(outs, axis=0).T
    near = (out_near.at[0], out_near.at[1])
    for ref, rows, place in stored_blocks(order_ref, coords_ref, near, out_far):
        ref[rows, 0:PAIR] = dq[place, :].astype(BF16)
        ref[rows, PAIR : 2 * PAIR] = (dk[place, :] * SCALE).astype(BF16)
        ref[rows, 2 * PAIR :] = dv[place, :].astype(BF16)


def own_pair(tokens, width, pair):
    return pl.BlockSpec((1, 1, tokens, width), lambda i, order, coords: (0, pair, 0, 0))


def all_of(shape):
    return pl.BlockSpec(shape, lambda i, *scalars: (0,) * len(shape))


def attention(order, coords, own, got, far, pair):
    tokens = far.shape[1]
    length = 4 * tokens
    out = (2, tokens, PAIR)
    return pl.pallas_call(
        attention_kernel,
        grid_spec=pltpu.PrefetchScalarGridSpec(
            num_scalar_prefetch=2,
            grid=(1,),
            in_specs=[own_pair(tokens, 3 * PAIR, pair)] * 2 + [all_of(far.shape)],
            out_specs=[all_of(out)] * 2 + [all_of((8, length))],
            scratch_shapes=[pltpu.VMEM((length, PAIR), BF16)] * 4,
        ),
        out_shape=[jax.ShapeDtypeStruct(out, BF16)] * 2 + [jax.ShapeDtypeStruct((8, length), F32)],
        compiler_params=pltpu.CompilerParams(vmem_limit_bytes=VMEM_LIMIT),
        cost_estimate=FREE,
    )(order, coords, own, got, far)


def attention_back(order, coords, own, got, far, grad_own, grad_got, grad_far, lse, pair):
    tokens = far.shape[1]
    length = 4 * tokens
    out = (2, tokens, 3 * PAIR)
    return pl.pallas_call(
        attention_back_kernel,
        grid_spec=pltpu.PrefetchScalarGridSpec(
            num_scalar_prefetch=2,
            grid=(1,),
            in_specs=[own_pair(tokens, 3 * PAIR, pair)] * 2
            + [all_of(far.shape)]
            + [own_pair(tokens, PAIR, pair)] * 2
            + [all_of(grad_far.shape), all_of(lse.shape)],
            out_specs=[all_of(out)] * 2,
            scratch_shapes=[pltpu.VMEM((length, PAIR), BF16)] * 4
            + [pltpu.VMEM((length, PAIR), F32)] * 3,
        ),
        out_shape=[jax.ShapeDtypeStruct(out, BF16)] * 2,
        compiler_params=pltpu.CompilerParams(vmem_limit_bytes=VMEM_LIMIT),
        cost_estimate=FREE,
    )(order, coords, own, got, far, grad_own, grad_got, grad_far, lse)


def streamed(value):
    return pltpu.with_memory_space_constraint(value, pltpu.HBM)


K_STEPS = 4
K_BLOCK = D // K_STEPS


def qkv_kernel(coords_ref, entry, gain, bias, *refs):
    weights, biases, outs, normed_out, blocks, acc = refs[:4], refs[4:8], refs[8:10], refs[10], refs[11], refs[12]
    step = pl.program_id(0)

    @pl.when(step == 0)
    def _():
        normed = layer_norm(entry[...].astype(F32), gain[...], bias[...])[0].astype(BF16)
        normed_out[...] = normed
        for b in range(K_STEPS):
            blocks[b] = normed[:, b * K_BLOCK : (b + 1) * K_BLOCK]
        acc[...] = jnp.zeros_like(acc)

    for quad in range(4):
        acc[quad] += dot(blocks[step], weights[quad][...])

    @pl.when(step == K_STEPS - 1)
    def _():
        for quad in range(4):
            core, y = quad // 2, quad % 2
            value = (acc[quad] + biases[quad][...]).astype(BF16)
            for pair in range(2):
                outs[core][lax.rem(coords_ref[0] + y, 2), pair] = value[:, pair * 3 * PAIR : (pair + 1) * 3 * PAIR]


def qkv_forward(coords, entry, w):
    tokens = entry.shape[0]
    weights = [streamed(w["qkv"][i][j]) for i in range(2) for j in range(2)]
    biases = [w["qkv_bias"][i][:, j * 768 : (j + 1) * 768] for i in range(2) for j in range(2)]
    wide, row = all_of((tokens, D)), all_of((1, D))
    heads = (2, 2, tokens, 3 * PAIR)
    return pl.pallas_call(
        qkv_kernel,
        grid_spec=pltpu.PrefetchScalarGridSpec(
            num_scalar_prefetch=1,
            grid=(K_STEPS,),
            in_specs=[wide, row, row]
            + [pl.BlockSpec((K_BLOCK, 768), lambda j, coords: (j, 0))] * 4
            + [all_of((1, 768))] * 4,
            out_specs=[all_of(heads)] * 2 + [wide],
            scratch_shapes=[pltpu.VMEM((K_STEPS, tokens, K_BLOCK), BF16), pltpu.VMEM((4, tokens, 768), F32)],
        ),
        out_shape=[jax.ShapeDtypeStruct(heads, BF16)] * 2 + [jax.ShapeDtypeStruct((tokens, D), BF16)],
        compiler_params=pltpu.CompilerParams(vmem_limit_bytes=VMEM_LIMIT),
        cost_estimate=FREE,
    )(coords, entry, w["ln1_gain"], w["ln1_bias"], *weights, *biases)


def qkv_back_kernel(coords_ref, mine, other, entry, gain, d_mid, *refs):
    weights, d_entry, ln_gain, ln_bias, sums, blocks = refs[:4], refs[4], refs[5], refs[6], refs[7:9], refs[9]
    step = pl.program_id(0)
    grad = jnp.zeros(blocks.shape[1:], F32)
    for quad in range(4):
        ref = (mine, other)[quad // 2]
        rel = lax.rem(coords_ref[0] + quad % 2, 2)
        for pair in range(2):
            columns = slice(pair * 3 * PAIR, (pair + 1) * 3 * PAIR)
            grad += dot_back(ref[rel, pair], weights[quad][:, columns])
    blocks[step] = grad

    @pl.when(step == K_STEPS - 1)
    def _():
        for quad in range(4):
            ref = (mine, other)[quad // 2]
            rel = lax.rem(coords_ref[0] + quad % 2, 2)
            for pair in range(2):
                columns = slice(pair * 3 * PAIR, (pair + 1) * 3 * PAIR)
                values = ref[rel, pair].astype(F32)
                sums[quad // 2][quad % 2 : quad % 2 + 1, columns] = jnp.sum(values, axis=0, keepdims=True)
        whole = jnp.concatenate([blocks[b] for b in range(K_STEPS)], axis=1)
        _, normal, inverse = layer_norm(entry[...].astype(F32), gain[...], 0.0)
        through, d_gain, d_bias = norm_back(whole, normal, inverse, gain[...])
        ln_gain[...] = d_gain.reshape(1, D)
        ln_bias[...] = d_bias.reshape(1, D)
        d_entry[...] = (d_mid[...] + through).astype(BF16)


def qkv_back(coords, mine, other, entry, d_mid, w):
    tokens = entry.shape[0]
    weights = [streamed(w["qkv"][i][j]) for i in range(2) for j in range(2)]
    wide, row = all_of((tokens, D)), all_of((1, D))
    line = jax.ShapeDtypeStruct((1, D), F32)
    return pl.pallas_call(
        qkv_back_kernel,
        grid_spec=pltpu.PrefetchScalarGridSpec(
            num_scalar_prefetch=1,
            grid=(K_STEPS,),
            in_specs=[all_of(mine.shape)] * 2
            + [wide, row, wide]
            + [pl.BlockSpec((K_BLOCK, 768), lambda j, coords: (j, 0))] * 4,
            out_specs=[wide, row, row] + [all_of((2, 768))] * 2,
            scratch_shapes=[pltpu.VMEM((K_STEPS, tokens, K_BLOCK), F32)],
        ),
        out_shape=[jax.ShapeDtypeStruct((tokens, D), BF16), line, line]
        + [jax.ShapeDtypeStruct((2, 768), F32)] * 2,
        compiler_params=pltpu.CompilerParams(vmem_limit_bytes=VMEM_LIMIT),
        cost_estimate=FREE,
    )(coords, mine, other, entry, w["ln1_gain"], d_mid, *weights)


def head_columns(coords_ref, core, y, pair):
    quad = lax.rem(coords_ref[3] + core, 2) * 2 + lax.rem(coords_ref[0] + y, 2)
    return pl.multiple_of((quad * 2 + pair) * PAIR, PAIR)


def half_columns(coords_ref, core):
    return pl.ds(pl.multiple_of(lax.rem(coords_ref[3] + core, 2) * (D // 2), D // 2), D // 2)


def out_kernel(coords_ref, entry, near_0, near_1, got_0, got_1, other, own_weight, other_weight, bias, mid, att):
    for pair, (near, got) in enumerate(((near_0, got_0), (near_1, got_1))):
        att[:, pl.ds(head_columns(coords_ref, 0, 0, pair), PAIR)] = near[0]
        att[:, pl.ds(head_columns(coords_ref, 0, 1, pair), PAIR)] = got[0]
        for y in range(2):
            att[:, pl.ds(head_columns(coords_ref, 1, y, pair), PAIR)] = other[y, pair]
    for core, weight in enumerate((own_weight, other_weight)):
        columns = half_columns(coords_ref, core)
        mid[:, columns] = entry[:, columns].astype(F32) + (dot(att[...], weight[...]) + bias[:, columns])


def out_forward(coords, entry, near, got, other, w):
    tokens = entry.shape[0]
    arrays = [entry, *near, *got, other, *w["out"], w["out_bias"]]
    return pl.pallas_call(
        out_kernel,
        grid_spec=pltpu.PrefetchScalarGridSpec(
            num_scalar_prefetch=1,
            grid=(1,),
            in_specs=[all_of(a.shape) for a in arrays],
            out_specs=[all_of((tokens, D))] * 2,
        ),
        out_shape=[jax.ShapeDtypeStruct((tokens, D), t) for t in (F32, BF16)],
        compiler_params=pltpu.CompilerParams(vmem_limit_bytes=VMEM_LIMIT),
        cost_estimate=FREE,
    )(coords, *arrays)


FF_BLOCK = 1024
FF_STEPS = FF // FF_BLOCK
CURVE = 0.044715
ROOT = (2.0 / jnp.pi) ** 0.5


def feed_up_kernel(first, *refs):
    if first:
        mid, gain, bias, fc, fc_bias, normed, act, slope = refs

        @pl.when(pl.program_id(0) == 0)
        def _():
            normed[...] = layer_norm(mid[...], gain[...], bias[...])[0].astype(BF16)
    else:
        normed, fc, fc_bias, act, slope = refs
    before = dot(normed[...], fc[...]) + fc_bias[...]
    square = before * before
    bent = jnp.tanh(ROOT * before * (1.0 + CURVE * square))
    act[...] = (0.5 * before * (1.0 + bent)).astype(BF16)
    slope[...] = (
        0.5 * (1.0 + bent) + 0.5 * ROOT * before * (1.0 - bent * bent) * (1.0 + 3.0 * CURVE * square)
    ).astype(BF16)


def feed_up_half(first, given, fc, fc_bias):
    tokens = given[0].shape[0]
    row, wide = all_of((1, D)), all_of((tokens, D))
    along = lambda rows: pl.BlockSpec((rows, FF_BLOCK), lambda j: (0, j))
    outs = [(wide, jax.ShapeDtypeStruct((tokens, D), BF16))] if first else []
    outs += [(along(tokens), jax.ShapeDtypeStruct((tokens, FF // 2), BF16))] * 2
    return pl.pallas_call(
        functools.partial(feed_up_kernel, first),
        grid=(FF_STEPS // 2,),
        in_specs=([wide, row, row] if first else [wide]) + [along(D), along(1)],
        out_specs=[spec for spec, _ in outs],
        out_shape=[shape for _, shape in outs],
        compiler_params=pltpu.CompilerParams(vmem_limit_bytes=VMEM_LIMIT),
        cost_estimate=FREE,
    )(*given, fc, fc_bias)


def feed_up(middle, w):
    given = (middle, w["ln2_gain"], w["ln2_bias"])
    normed, act_own, slope_own = feed_up_half(True, given, w["fc"][0], w["fc_bias"][0])
    act_other, slope_other = feed_up_half(False, (normed,), w["fc"][1], w["fc_bias"][1])
    return normed, (act_own, act_other), (slope_own, slope_other)


def ff_at(i):
    count = FF_STEPS // 2
    return (lambda j: jnp.minimum(j, count - 1)) if i == 0 else (lambda j: jnp.maximum(j - count, 0))


def ff_specs(rows, axis):
    def one(i):
        at = ff_at(i)
        if axis == 1:
            return pl.BlockSpec((rows, FF_BLOCK), lambda j, *scalars: (0, at(j)))
        return pl.BlockSpec((FF_BLOCK, rows), lambda j, *scalars: (at(j), 0))

    return [one(0), one(1)]


def feed_down_kernel(mid, bias, act_own, act_other, proj_own, proj_other, result, acc):
    step = pl.program_id(0)

    @pl.when(step == 0)
    def _():
        acc[...] = mid[...] + bias[...]

    for i, (act, proj) in enumerate(((act_own, proj_own), (act_other, proj_other))):

        @pl.when(step // (FF_STEPS // 2) == i)
        def _():
            acc[...] += dot(act[...], proj[...])

    @pl.when(step == FF_STEPS - 1)
    def _():
        result[...] = acc[...].astype(BF16)


def feed_down(middle, act, w):
    tokens = middle.shape[0]
    wide = all_of((tokens, D))
    return pl.pallas_call(
        feed_down_kernel,
        grid=(FF_STEPS,),
        in_specs=[wide, all_of((1, D))] + ff_specs(tokens, 1) + ff_specs(D, 0),
        out_specs=wide,
        out_shape=jax.ShapeDtypeStruct((tokens, D), BF16),
        scratch_shapes=[pltpu.VMEM((tokens, D), F32)],
        compiler_params=pltpu.CompilerParams(vmem_limit_bytes=VMEM_LIMIT),
        cost_estimate=FREE,
    )(middle, w["proj_bias"], *act, *w["proj"])


def feed_back_kernel(coords_ref, *refs):
    upstream, mid, gain, fc, proj, slope, out_weights = refs[0], refs[1], refs[2], refs[3:5], refs[5:7], refs[7:9], refs[9:11]
    refs = refs[11:]
    d_mid, dy1, d_pre, fc_sum, ln_gain, ln_bias, proj_sum, heads, acc = (
        refs[0],
        refs[1],
        refs[2:4],
        refs[4:6],
        refs[6],
        refs[7],
        refs[8],
        refs[9:11],
        refs[11],
    )
    step = pl.program_id(0)

    @pl.when(step == 0)
    def _():
        acc[...] = jnp.zeros_like(acc)
        proj_sum[...] = jnp.sum(upstream[...].astype(F32), axis=0, keepdims=True)

    for i in range(2):

        @pl.when(step // (FF_STEPS // 2) == i)
        def _():
            grad = (slope[i][...].astype(F32) * dot_back(upstream[...], proj[i][...])).astype(BF16)
            d_pre[i][...] = grad
            fc_sum[i][...] = jnp.sum(grad.astype(F32), axis=0, keepdims=True)
            acc[...] += dot_back(grad, fc[i][...])

    @pl.when(step == FF_STEPS - 1)
    def _():
        _, normal, inverse = layer_norm(mid[...], gain[...], 0.0)
        through, d_gain, d_bias = norm_back(acc[...], normal, inverse, gain[...])
        ln_gain[...] = d_gain.reshape(1, D)
        ln_bias[...] = d_bias.reshape(1, D)
        d_mid[...] = upstream[...].astype(F32) + through
        dy1[...] = d_mid[...].astype(BF16)
        grads = [dy1[:, half_columns(coords_ref, core)] for core in range(2)]
        for core in range(2):
            for y in range(2):
                for pair in range(2):
                    rows = pl.ds(head_columns(coords_ref, core, y, pair), PAIR)
                    value = dot_back(grads[0], out_weights[0][rows, :]) + dot_back(grads[1], out_weights[1][rows, :])
                    heads[core][y, pair] = value.astype(BF16)


def feed_back(coords, upstream, middle, slope, w):
    tokens = upstream.shape[0]
    row, wide = all_of((1, D)), all_of((tokens, D))
    line = jax.ShapeDtypeStruct((1, D), F32)
    heads = (2, 2, tokens, PAIR)
    return pl.pallas_call(
        feed_back_kernel,
        grid_spec=pltpu.PrefetchScalarGridSpec(
            num_scalar_prefetch=1,
            grid=(FF_STEPS,),
            in_specs=[wide, wide, row]
            + ff_specs(D, 1)
            + ff_specs(D, 0)
            + ff_specs(tokens, 1)
            + [all_of((D, D // 2))] * 2,
            out_specs=[wide, wide] + ff_specs(tokens, 1) + ff_specs(1, 1) + [row] * 3 + [all_of(heads)] * 2,
            scratch_shapes=[pltpu.VMEM((tokens, D), F32)],
        ),
        out_shape=[
            jax.ShapeDtypeStruct((tokens, D), F32),
            jax.ShapeDtypeStruct((tokens, D), BF16),
            *[jax.ShapeDtypeStruct((tokens, FF // 2), BF16)] * 2,
            *[jax.ShapeDtypeStruct((1, FF // 2), F32)] * 2,
            line,
            line,
            line,
            *[jax.ShapeDtypeStruct(heads, BF16)] * 2,
        ],
        compiler_params=pltpu.CompilerParams(vmem_limit_bytes=VMEM_LIMIT),
        cost_estimate=FREE,
    )(coords, upstream, middle, w["ln2_gain"], *w["fc"], *w["proj"], *slope, *w["out"])


def together(first, *others):
    return lax.optimization_barrier((first, *others))


def over_y(values, active, old):
    arrived = [swap_y(value, active) for value in values]
    if old is not None:
        here = lax.axis_index("section") == active
        arrived = [jnp.where(here, new, was) for new, was in zip(arrived, old)]
    return arrived


def to_heads(mine, other, active, old):
    got = swap_cores(other)
    far = over_y([jnp.stack([mine[1, pair], got[1, pair]]) for pair in range(2)], active, old)
    return got, far


def to_tokens(near, got):
    mine, send = (
        jnp.stack([jnp.stack([v[core] for v in near]), jnp.stack([v[core] for v in got])]) for core in range(2)
    )
    return mine, swap_cores(send)


def layer_forward(entry, w, order, coords, active, old, late=None):
    mine, other, normed = qkv_forward(coords, entry, w)
    got, far = to_heads(mine, other, active, old and old["far"])
    if late is not None:
        next(late)
        far[1] = late.send(far[1])
    near, back, lse = [], [], []
    for pair in range(2):
        heads, heads_far, pair_lse = attention(order, coords, mine, got, far[pair], pair)
        near.append(heads)
        back += over_y([heads_far], active, old and [old["back"][pair]])
        lse.append(pair_lse)
    send = jnp.stack([jnp.stack([v[1] for v in near]), jnp.stack([v[1] for v in back])])
    middle, attended = out_forward(coords, entry, near, back, swap_cores(send), w)
    if late is not None:
        middle = late.send(middle)
    normed2, act, slope = feed_up(middle, w)
    return dict(
        entry=entry,
        normed=normed,
        qkv=(mine, got),
        far=far,
        back=back,
        lse=lse,
        attended=attended,
        middle=middle,
        normed2=normed2,
        act=act,
        slope=slope,
    )


def layer_backward(upstream, s, w, order, coords, active, old):
    g = {}
    last = old is not None
    d_mid, dy1, d_pre_own, d_pre_other, *sums, mine, other = feed_back(
        coords, upstream, s["middle"], s["slope"], w
    )
    got, far = to_heads(mine, other, active, old and old["far"])
    if last:
        jobs = [(s["normed2"], swap_cores(s["normed2"]), d_pre_own, swap_cores(d_pre_other), 0, FF // 2)]
        grad = plain_grad(s["act"][0], swap_cores(s["act"][1]), upstream, swap_cores(upstream))
        far[0], far[1], parts, grad = together(far[0], far[1], weight_grad(coords, Z, jobs), grad)
        relay = relay_far(parts, Z)
        proj_part = sum_by_axes(grad.reshape(4, 4, 2, -1, D), (X,))
    near, back = [], []
    for pair in range(2):
        args = (*s["qkv"], s["far"][pair], mine, got, far[pair], s["lse"][pair], pair)
        own, heads_far = attention_back(order, coords, *args)
        if last and pair == 1:
            own, heads_far, relay = together(own, heads_far, relay)
            relay = relay_near(parts, *relay, Z)
        near.append(own)
        back += over_y([heads_far], active, old and [old["back"][pair]])
    d_mine, d_other = to_tokens(near, back)
    if last:
        lefts = (s["normed"], swap_cores(s["normed"]))
        lefts_out = (s["attended"], swap_cores(s["attended"]))
        core = coords[3]
        rights_out = (half(dy1, core, 1), swap_cores(half(dy1, 1 - core, 1)))
        qkv_parts = [
            weight_grad(
                coords,
                axis,
                [(*lefts, d_mine, swap_cores(d_other), i, 768), (*lefts_out, *rights_out, i, 256)],
            )
            for i, axis in enumerate((Z, X))
        ]
        d_mine, d_other, qkv_parts, proj_part, relay, dy1, sums = together(
            d_mine, d_other, qkv_parts, proj_part, relay, dy1, sums
        )
        g["proj"] = sum_by_axes(proj_part, (Z,))
        along_z, along_x = start_sum(qkv_parts[0], Z), start_sum(qkv_parts[1], X)
        along_z, relay, g["proj"] = together(along_z, relay, g["proj"])
        g["proj"] = sum_by_axes(g["proj"], (Y,))
        both = jnp.concatenate([total([parts[0], *relay]), total(along_z)], axis=-1)
        g["rest"] = [second_sum(both, X), second_sum(total(along_x), Z)]
    d_entry, ln1_gain, ln1_bias, *qkv_sums = qkv_back(coords, d_mine, d_other, s["entry"], d_mid, w)
    g.update(
        far=far,
        back=back,
        dy1=dy1,
        qkv_sum=[v.reshape(-1) for v in qkv_sums],
        ln1_gain=ln1_gain,
        ln1_bias=ln1_bias,
        fc_sum=sums[0:2],
        ln2_gain=sums[2],
        ln2_bias=sums[3],
        proj_sum=sums[4],
    )
    return d_entry, g


def to_sequence(values, core):
    micro, rows, width = values.shape
    cut = values.reshape(micro, 2, rows // 2, width)
    keep = lax.dynamic_index_in_dim(cut, core, 1)
    got = swap_cores(lax.dynamic_index_in_dim(cut, 1 - core, 1))
    each = in_order(core, keep, got, 1).reshape(2 * micro, rows // 2, width)
    return lax.all_to_all(each, Z, 0, 0, tiled=True).reshape(2 * rows, width)


def from_sequence(values):
    tokens, width = values.shape
    return lax.all_to_all(values.reshape(4, tokens // 4, width), Z, 0, 0, tiled=True)


def own_rows(values, core):
    _, rows, width = values.shape
    each = values.reshape(2, 2, rows, width)
    keep = lax.dynamic_index_in_dim(each, core, 1)
    got = swap_cores(lax.dynamic_index_in_dim(each, 1 - core, 1))
    return in_order(core, keep, got, 1).reshape(2, 2 * rows, width)


def by_pair(values):
    lead = values.shape[:-1]
    return values.reshape(*lead, 3, PAIRS, PAIR).swapaxes(-2, -3).reshape(*lead, 3 * D)


def by_part(values):
    lead = values.shape[:-1]
    return values.reshape(*lead, PAIRS, 3, PAIR).swapaxes(-2, -3).reshape(*lead, 3 * D)


def by_core(values):
    lead = values.shape[:-1]
    return jnp.moveaxis(values.reshape(*lead, 2, 4, 4, 2, 64), (-2, -3, -4, -5), (-5, -4, -3, -2)).reshape(*lead, FF)


def from_core(values):
    lead = values.shape[:-1]
    return jnp.moveaxis(values.reshape(*lead, 2, 4, 4, 2, 64), (-5, -4, -3, -2), (-2, -3, -4, -5)).reshape(*lead, FF)


def on_device(
    inputs,
    cotangent,
    block_order,
    ln1_gain,
    ln1_bias,
    qkv_weight,
    qv_bias,
    out_weight,
    out_bias,
    ln2_gain,
    ln2_bias,
    fc_weight,
    fc_bias,
    proj_weight,
    proj_bias,
):
    section = lax.axis_index("section")
    core = lax.axis_index(CORE)
    coords = jnp.stack([lax.axis_index(a) for a in CTX_FSDP]).astype(jnp.int32)
    first = section == 0
    micro, _, rows, _ = inputs.shape

    vectors = (ln1_gain, ln1_bias, qv_bias, out_bias, ln2_gain, ln2_bias, fc_bias, proj_bias)
    widths = [v.shape[-1] for v in vectors]
    starts = [sum(widths[:i]) for i in range(len(widths))]
    packed = jnp.concatenate([v.reshape(-1) for v in vectors])
    packed = jnp.pad(packed, (0, 16 * 128 - packed.shape[0])).reshape(16, 128)

    qkv_cut = by_pair(qkv_weight[0]).reshape(16, 2, 2, 768)
    out_cut = out_weight[0].reshape(16, 2, 2, 256)
    fc_cut = by_core(fc_weight[0]).reshape(16, 2, 2048)
    halves = [
        jnp.concatenate(
            [qkv_cut[:, i, 0], out_cut[:, i, 0], packed, fc_cut[:, i], qkv_cut[:, i, 1], out_cut[:, i, 1]],
            axis=1,
        )
        for i in range(2)
    ]
    mine = jnp.where(core == 0, halves[0], halves[1])
    other = jnp.where(core == 0, halves[1], halves[0])
    blob = in_order(core, mine, swap_cores(other), 0)
    proj_own = in_order(coords[0], proj_weight[0], shift(proj_weight[0], Y, 1), 0)
    proj_own = lax.all_gather(proj_own, Z, axis=0, tiled=True)
    ring_x = first_ring(both_y(blob[:, :3200]), X)
    ring_z = first_ring(both_y(blob[:, 3200:]), Z)
    tokens = to_sequence(jnp.concatenate([inputs[:, 0], cotangent[:, 0]], axis=-1), core)
    ring_x, ring_z, tokens = together(ring_x, ring_z, tokens)
    entry, given = tokens[:, :D], tokens[:, D:]
    pieces_x = second_ring(ring_x[..., :1152], Z)
    pieces_z = second_ring(ring_z, X)
    (pieces_x, pieces_z), fc_ring, proj_own = together((pieces_x, pieces_z), ring_x[..., 1152:], proj_own)
    proj_own = lax.all_gather(proj_own, X, axis=0, tiled=True)
    cuts = ((0, 768, 0, 0), (768, 256, 1, 0))
    qkv_0, out_0, packed = assemble(coords, X, cuts + ((1024, 128, 2, 0),), pieces_x)
    qkv_1, out_1 = assemble(coords, Z, cuts, pieces_z)
    out_own = jnp.concatenate([out_0, out_1], axis=1)
    w = {
        "qkv": ((qkv_0, qkv_1), (swap_cores(qkv_0), swap_cores(qkv_1))),
        "out": (out_own, swap_cores(out_own)),
    }

    def late_weights():
        value = yield
        value, low, high = together(value, *to_neighbours(fc_ring, Z))
        far = past_neighbours(low, high, Z)
        value = yield value
        value, *pieces = together(value, fc_ring, far, low, high)
        (fc_own,) = assemble(coords, X, ((0, 2048, 0, 0),), pieces)
        w["fc"] = (fc_own, swap_cores(fc_own))
        w["proj"] = (proj_own, swap_cores(proj_own))
        yield value

    packed = packed.reshape(32, 2, 16, 128)[:, :, :2].reshape(64, 256)
    names = ("ln1_gain", "ln1_bias", "qv", "out_bias", "ln2_gain", "ln2_bias", "fc", "proj_bias")
    vector = {
        name: packed[:, start : start + width].reshape(1, -1).astype(F32)
        for name, start, width in zip(names, starts, widths)
    }
    qv, fc_vector = vector.pop("qv"), by_core(vector.pop("fc"))
    qkv_vector = by_pair(jnp.concatenate([qv[:, :D], jnp.zeros((1, D), F32), qv[:, D:]], axis=1))
    w.update(vector)
    w["qkv_bias"] = (half(qkv_vector, core, 1), half(qkv_vector, 1 - core, 1))
    w["fc_bias"] = (half(fc_vector, core, 1), half(fc_vector, 1 - core, 1))

    early = layer_forward(entry, w, block_order, coords, 0, None, late_weights())
    result = feed_down(early["middle"], early["act"], w)
    arriving = lax.ppermute(result, "section", [(0, 1)])
    entry = jnp.where(first, entry, arriving)
    saved = layer_forward(entry, w, block_order, coords, 1, early)

    d_entry, early = layer_backward(given, saved, w, block_order, coords, 1, None)
    arriving = lax.ppermute(d_entry, "section", [(1, 0)])
    middle, _ = together(saved["middle"], d_entry)
    arriving, result = together(arriving, feed_down(middle, saved["act"], w))
    upstream = jnp.where(first, arriving, given)
    d_entry, g = layer_backward(upstream, saved, w, block_order, coords, 0, early)
    returned = from_sequence(jnp.concatenate([result, d_entry], axis=1))

    rest = g["rest"]
    d_pre_sum = from_core(in_order(core, *[v[0] for v in g["fc_sum"]], 0))
    d_qkv_sum = by_part(in_order(core, *g["qkv_sum"], 0))
    small = (
        g["ln1_gain"],
        g["ln1_bias"],
        jnp.concatenate([d_qkv_sum[:D], d_qkv_sum[2 * D :]]),
        jnp.sum(g["dy1"].astype(F32), axis=0),
        g["ln2_gain"],
        g["ln2_bias"],
        d_pre_sum,
        g["proj_sum"],
    )
    small = jnp.concatenate([v.reshape(64, -1) for v in small], axis=1)
    small, returned, rest[0] = together(small, returned, rest[0])
    returned = own_rows(returned, core)
    acts, in_grads = returned[..., :D], returned[..., D:].astype(F32)
    small = jnp.sum(lax.all_to_all(small, CTX_FSDP, 0, 0, tiled=True), axis=0, keepdims=True)
    grads = last_sum(jnp.concatenate([total(part) for part in rest], axis=-1))
    fc_part, z_part, x_part = grads[:, :2048], grads[:, 2048:3072], grads[:, 3072:]
    grads = jnp.concatenate([z_part[:, :768], x_part[:, :768], z_part[:, 768:], x_part[:, 768:], fc_part], axis=1)
    mine = half(grads, core, 0)
    other = swap_cores(half(grads, 1 - core, 0))
    qkv_grad = by_part(in_order(core, mine[:, :1536], other[:, :1536], 1))
    out_grad = in_order(core, mine[:, 1536:2048], other[:, 1536:2048], 1)
    fc_grad = from_core(in_order(core, mine[:, 2048:], other[:, 2048:], 1))
    proj_grad = g["proj"].astype(F32)

    small = [small[:, a : a + n] for a, n in zip(starts, widths)]
    shape = (1, micro, 1, rows, D)
    return (
        acts.reshape(shape),
        in_grads.reshape(shape),
        small[0],
        small[1],
        qkv_grad[None],
        small[2],
        out_grad[None],
        small[3],
        small[4],
        small[5],
        fc_grad[None],
        small[6],
        proj_grad[None],
        small[7],
    )


def solution(mesh):
    torus = Mesh(
        mesh.devices.reshape(mesh.shape["section"], 2, 4, 4, 2),
        ("section", "ctx_0", "ctx_1", "fsdp_0", "fsdp_1"),
    )
    tokens = P(None, FSDP, CTX, None)
    vector = P("section", CTX_FSDP)
    matrix = P("section", CTX_FSDP, None)
    kinds = (vector, vector, matrix, vector, matrix, vector, vector, vector, matrix, vector, matrix, vector)
    results = P("section", None, FSDP, CTX, None)
    return jax.shard_map(
        on_device,
        mesh=torus,
        in_specs=(tokens, tokens, P()) + kinds,
        out_specs=(results, results) + kinds,
        check_vma=False,
    )
```

```python
import functools

import jax
import jax.numpy as jnp
from jax import lax
from jax.experimental import pallas as pl
from jax.experimental.pallas import tpu as pltpu
from jax.sharding import Mesh
from jax.sharding import PartitionSpec as P

D = 1024
HEADS = 16
HEAD_DIM = 64
FF = 4096
PAIRS = 8
PAIR = 128
QUAD = 256
TILE = 256
BLOCK = 64
CTX = ("ctx_0", "ctx_1")
FSDP = ("fsdp_0", "fsdp_1")
CTX_FSDP = CTX + FSDP
Y, Z, X, CORE = CTX_FSDP
EPSILON = 1e-05
MASKED = -1e30
SCALE = HEAD_DIM**-0.5
BF16 = jnp.bfloat16
F32 = jnp.float32
VMEM_LIMIT = 24 * 2**20
FREE = pl.CostEstimate(flops=0, bytes_accessed=0, transcendentals=0)
SOME = pl.CostEstimate(flops=2 * 10**9, bytes_accessed=8 * 10**6, transcendentals=0)


def dot(left, right):
    return jnp.dot(left, right, preferred_element_type=F32)


def dot_rows(left, right):
    return lax.dot_general(left, right, (((0,), (0,)), ((), ())), preferred_element_type=F32)


def dot_back(left, right):
    return lax.dot_general(left, right, (((1,), (1,)), ((), ())), preferred_element_type=F32)


def shift(value, axis, by):
    n = lax.axis_size(axis)
    return lax.ppermute(value, axis, [(i, (i + by) % n) for i in range(n)])


def swap_cores(value):
    return shift(value, CORE, 1)


def swap_y(value, section):
    at = 2 * section
    return lax.ppermute(value, ("section", Y), [(at, at + 1), (at + 1, at)])


def half(value, which, dim):
    size = value.shape[dim] // 2
    return lax.dynamic_slice_in_dim(value, which * size, size, dim)


def in_order(which, mine, other, dim):
    return jnp.where(
        which == 0,
        jnp.concatenate([mine, other], axis=dim),
        jnp.concatenate([other, mine], axis=dim),
    )


def both_y(rows):
    return jnp.stack([rows, shift(rows, Y, 1)])


def first_ring(both, axis):
    return jnp.stack([both] + [shift(both, axis, k) for k in range(1, 4)])


def second_ring(ring, axis):
    return [ring] + [shift(ring, axis, k) for k in (2, 1, 3)]


def to_neighbours(halves, axis):
    return [shift(v, axis, by) for v, by in zip(halves, (1, -1))]


def assemble_kernel(first, cuts, count, coords_ref, *refs):
    outs = refs[4 * count :]
    pieces = [[refs[m * count + k * count // 4].at[k % (4 // count)] for k in range(4)] for m in range(4)]
    y, me = coords_ref[0], coords_ref[1] if first == Z else coords_ref[2]
    for m in range(4):

        @pl.when(pl.program_id(0) == m)
        def _():
            for k in range(4):
                place = lax.rem(me + 4 - k, 4)
                for dy in range(2):
                    at_y = lax.rem(y + dy, 2)
                    for start, width, out, row in cuts:
                        block = pieces[m][k][dy, :, start : start + width]
                        rows = pl.ds(row, block.shape[0])
                        if first == Z:
                            outs[out][at_y, place, 0, rows] = block
                        else:
                            outs[out][at_y, 0, place, rows] = block


def assemble(coords, first, cuts, pieces):
    pieces = [p if isinstance(p, (tuple, list)) else (p,) for p in pieces]
    count = len(pieces[0])
    one = pieces[0][0].shape
    rows = one[2]
    at = 2 if first == Z else 1
    shapes = {}
    for _, width, out, row in cuts:
        shapes[out] = (row + rows, width)
    shapes = [shapes[out] for out in range(len(shapes))]

    def place(m, coords):
        by = jnp.where(m == 1, 2, jnp.where(m == 2, 1, m))
        ring = lax.rem(coords[at] + 4 - by, 4)
        return (0, 0, ring, 0, 0) if first == Z else (0, ring, 0, 0, 0)

    along = (2, 4, 1) if first == Z else (2, 1, 4)
    whole = pl.BlockSpec(one, lambda m, coords: (0, 0, 0, 0))
    outs = pl.pallas_call(
        functools.partial(assemble_kernel, first, cuts, count),
        grid_spec=pltpu.PrefetchScalarGridSpec(
            num_scalar_prefetch=1,
            grid=(4,),
            in_specs=[whole] * (4 * count),
            out_specs=[pl.BlockSpec((*along, *shape), place) for shape in shapes],
        ),
        out_shape=[jax.ShapeDtypeStruct((2, 4, 4, *shape), BF16) for shape in shapes],
        compiler_params=pltpu.CompilerParams(vmem_limit_bytes=VMEM_LIMIT),
        cost_estimate=FREE,
    )(coords, *[streamed(part) for piece in pieces for part in piece])
    return [out.reshape(-1, out.shape[-1]) for out in outs]


def weight_grad_kernel(n_jobs, ring, coords_ref, *refs):
    jobs = [refs[4 * j : 4 * j + 4] for j in range(n_jobs)]
    extra = () if ring else (refs[4 * n_jobs],)
    outs, whole = refs[4 * n_jobs + len(extra) : -1], refs[-1]
    rows = whole.shape[2]
    at = 0
    for own_left, other_left, own_right, other_right in jobs:
        for own, other in zip(column_parts(own_right), column_parts(other_right)):
            grad = dot_rows(own_left[...], own()) + dot_rows(other_left[...], other())
            width = grad.shape[1]
            whole[:, :, :, pl.ds(at, width)] = grad.astype(BF16).reshape(4, 4, rows, width)
            at += width
    if not ring:
        for x in range(4):
            whole[:, x, :, pl.ds(at, 128)] = extra[0][:, 0]
        outs[0][:, :, 0] = whole[...]
        return
    own, up, down, up_later, down_later = outs
    part = [whole.at[lax.rem(coords_ref[1] + k, 4)] for k in range(4)]
    own[:, 0] = part[0][...]
    up[0, :, 0], up[1, :, 0] = part[2][0:2], part[1][2:4]
    down[0, :, 0], down[1, :, 0] = part[2][2:4], part[3][0:2]
    up_later[:, 0] = part[1][0:2]
    down_later[:, 0] = part[3][2:4]


def column_parts(ref):
    if len(ref.shape) == 4:
        return [lambda t=t: ref[0, t] for t in range(2)]
    return [lambda at=at: ref[:, pl.ds(at, 256)] for at in range(0, ref.shape[1], 256)]


def weight_grad(coords, ring, jobs, extra=None):
    rows = jobs[0][0].shape[1] // 32
    tokens = jobs[0][0].shape[0]
    columns = 0
    in_specs, arrays = [], []
    for *job, at, width in jobs:
        left = pl.BlockSpec((tokens, 16 * rows), lambda y, coords: (0, y))
        if job[2].ndim == 4:
            shape = (1, *job[2].shape[1:])
            right = pl.BlockSpec(shape, lambda y, coords, at=at: (lax.rem(coords[0] + at, 2), 0, 0, 0))
        elif at is None:
            right = pl.BlockSpec((tokens, width), lambda y, coords: (0, coords[3]))
        else:
            right = pl.BlockSpec((tokens, width), lambda y, coords, at=at: (0, at))
        columns += width
        in_specs += [left, left, right, right]
        arrays += [streamed(v) for v in job]
    if extra is not None:
        in_specs.append(pl.BlockSpec((4, 1, rows, 128), lambda y, coords: (0, y, 0, 0)))
        arrays.append(extra)
        columns += 128
    leads = [(4,), (2, 2), (2, 2), (2,), (2,)] if ring else [(4, 4)]

    def along_y(lead):
        return pl.BlockSpec((*lead, 1, rows, columns), lambda y, coords: (*(0,) * len(lead), y, 0, 0))

    return pl.pallas_call(
        functools.partial(weight_grad_kernel, len(jobs), ring),
        grid_spec=pltpu.PrefetchScalarGridSpec(
            num_scalar_prefetch=1,
            grid=(2,),
            in_specs=in_specs,
            out_specs=[along_y(lead) for lead in leads],
            scratch_shapes=[pltpu.VMEM((4, 4, rows, columns), BF16)],
        ),
        out_shape=[pltpu.HBM((*lead, 2, rows, columns), BF16) for lead in leads],
        compiler_params=pltpu.CompilerParams(vmem_limit_bytes=VMEM_LIMIT),
        cost_estimate=SOME if ring else FREE,
    )(coords, *arrays)


def plain_grad_kernel(own_left, other_left, own_right, other_right, out):
    grad = dot_rows(own_left[...], own_right[...])
    out[...] = (grad + dot_rows(other_left[...], other_right[...])).astype(BF16)


def plain_grad(own_left, other_left, own_right, other_right):
    tokens, rows = own_left.shape
    columns = own_right.shape[1]
    block = 512
    left = pl.BlockSpec((tokens, block), lambda i: (0, i))
    right = pl.BlockSpec((tokens, columns), lambda i: (0, 0))
    return pl.pallas_call(
        plain_grad_kernel,
        grid=(rows // block,),
        in_specs=[left, left, right, right],
        out_specs=pl.BlockSpec((block, columns), lambda i: (i, 0)),
        out_shape=pltpu.HBM((rows, columns), BF16),
        compiler_params=pltpu.CompilerParams(vmem_limit_bytes=VMEM_LIMIT),
        cost_estimate=SOME,
    )(*[streamed(v) for v in (own_left, other_left, own_right, other_right)])


def sum_by_axes(parts, axes):
    for axis in axes:
        parts = lax.psum_scatter(parts, axis, scatter_dimension=0, tiled=False)
    return parts


def total(parts):
    return functools.reduce(lambda a, b: a + b, [p.astype(F32) for p in parts])


def start_sum(parts, first):
    return [parts[0]] + [shift(parts[k], first, k) for k in (2, 1, 3)]


def relay_kernel(coords_ref, up, low, down, high, up_out, down_out):
    up_out[...] = total([up[...], low[0]]).astype(BF16)
    down_out[...] = total([down[...], high[0]]).astype(BF16)


def relay(coords, parts, low, high):
    shape = pltpu.HBM(parts[3].shape, BF16)
    up, down = small_kernel(relay_kernel, coords, [parts[3], low, parts[4], high], [shape] * 2)
    return shift(up, Z, 1), shift(down, Z, -1)


def layer_norm(values, gain, bias):
    average = jnp.mean(values, axis=-1, keepdims=True)
    centred = values - average
    spread_of = jnp.mean(centred * centred, axis=-1, keepdims=True)
    inverse = lax.rsqrt(spread_of + EPSILON)
    normal = centred * inverse
    return normal * gain + bias, normal, inverse


def norm_back(upstream, normal, inverse, gain):
    scaled = upstream * gain
    first = jnp.mean(scaled, axis=-1, keepdims=True)
    second = jnp.mean(scaled * normal, axis=-1, keepdims=True)
    return (
        inverse * (scaled - first - normal * second),
        jnp.sum(upstream * normal, axis=0),
        jnp.sum(upstream, axis=0),
    )


def head_lanes(shape, head):
    return lax.broadcasted_iota(jnp.int32, shape, 1) // HEAD_DIM == head


def causal(keys):
    rows = lax.broadcasted_iota(jnp.int32, (keys, TILE), 0)
    columns = lax.broadcasted_iota(jnp.int32, (keys, TILE), 1)
    return rows <= columns + (keys - TILE)


def stored_blocks(order_ref, coords_ref):
    y, c = coords_ref[0], coords_ref[3]
    for dy in range(2):
        for dc in range(2):
            for z in range(4):
                stored = lax.rem(y + dy, 2) * 8 + z * 2 + lax.rem(c + dc, 2)
                at = pl.multiple_of(order_ref[stored] * BLOCK, BLOCK)
                yield dy, dc, slice(z * BLOCK, (z + 1) * BLOCK), pl.ds(at, BLOCK)


def chosen(coords_ref, active, refs, index):
    if len(refs) == 1:
        return refs[0][index]
    return jnp.where(coords_ref[4] == active, refs[0][index], refs[1][index])


def attention_kernel(active, order_ref, coords_ref, own, got, *refs):
    far, (out_near, out_far, lse_ref, q, k, v, out) = refs[:-7], refs[-7:]
    for dy, dc, rows, place in stored_blocks(order_ref, coords_ref):
        if dy == 0:
            block = (own, got)[dc][0, 0, rows, :]
        else:
            block = chosen(coords_ref, active, far, (dc, rows, slice(None)))
        q[place, :] = block[:, 0:PAIR]
        k[place, :] = block[:, PAIR : 2 * PAIR] * SCALE
        v[place, :] = block[:, 2 * PAIR :]
    length = q.shape[0]
    lse_ref[...] = jnp.zeros_like(lse_ref)
    for tile in range(length // TILE):
        keys = (tile + 1) * TILE
        here = pl.ds(tile * TILE, TILE)
        outs = []
        for head in range(2):
            queries = q[here, :]
            queries = jnp.where(head_lanes(queries.shape, head), queries, jnp.zeros_like(queries))
            scores = dot_back(k[0:keys, :], queries)
            scores = jnp.where(causal(keys), scores, MASKED)
            highest = jnp.max(scores, axis=0, keepdims=True)
            probs = jnp.exp(scores - highest)
            total_of = jnp.sum(probs, axis=0, keepdims=True)
            lse_ref[head : head + 1, here] = highest + jnp.log(total_of)
            attended = dot_rows(v[0:keys, :], probs.astype(BF16)) / total_of
            outs.append(attended[head * HEAD_DIM : (head + 1) * HEAD_DIM, :])
        out[here, :] = jnp.concatenate(outs, axis=0).T.astype(BF16)
    for dy, dc, rows, place in stored_blocks(order_ref, coords_ref):
        (out_near, out_far)[dy][dc, rows, :] = out[place, :]


def attention_back_kernel(actives, n_far, n_grad, order_ref, coords_ref, *refs):
    own, got = refs[:2]
    far = refs[2 : 2 + n_far]
    grad_own, grad_got = refs[2 + n_far : 4 + n_far]
    grad_far = refs[4 + n_far : 4 + n_far + n_grad]
    lse_ref, out_near, out_far, q, k, v, g, dq, dk, dv = refs[4 + n_far + n_grad :]
    for dy, dc, rows, place in stored_blocks(order_ref, coords_ref):
        if dy == 0:
            block = (own, got)[dc][0, 0, rows, :]
            grads = (grad_own, grad_got)[dc][0, 0, rows, :]
        else:
            block = chosen(coords_ref, actives[0], far, (dc, rows, slice(None)))
            grads = chosen(coords_ref, actives[1], grad_far, (dc, rows, slice(None)))
        q[place, :] = block[:, 0:PAIR]
        k[place, :] = block[:, PAIR : 2 * PAIR] * SCALE
        v[place, :] = block[:, 2 * PAIR :]
        g[place, :] = grads
    length = q.shape[0]
    dk[...] = jnp.zeros_like(dk)
    dv[...] = jnp.zeros_like(dv)
    for tile in range(length // TILE):
        keys = (tile + 1) * TILE
        here = pl.ds(tile * TILE, TILE)
        outs = []
        for head in range(2):
            lanes = head_lanes((TILE, PAIR), head)
            queries = q[here, :]
            queries = jnp.where(lanes, queries, jnp.zeros_like(queries))
            grads = g[here, :]
            grads = jnp.where(lanes, grads, jnp.zeros_like(grads))
            scores = dot_back(k[0:keys, :], queries)
            probs = jnp.exp(scores - lse_ref[head : head + 1, here])
            probs = jnp.where(causal(keys), probs, 0.0)
            grad_probs = dot_back(v[0:keys, :], grads)
            term = jnp.sum(probs * grad_probs, axis=0, keepdims=True)
            grad_scores = (probs * (grad_probs - term)).astype(BF16)
            dv[0:keys, :] += dot(probs.astype(BF16), grads)
            dk[0:keys, :] += dot(grad_scores, queries)
            grad_q = dot_rows(k[0:keys, :], grad_scores)
            outs.append(grad_q[head * HEAD_DIM : (head + 1) * HEAD_DIM, :])
        dq[here, :] = jnp.concatenate(outs, axis=0).T
    for dy, dc, rows, place in stored_blocks(order_ref, coords_ref):
        ref = (out_near, out_far)[dy]
        ref[dc, rows, 0:PAIR] = dq[place, :].astype(BF16)
        ref[dc, rows, PAIR : 2 * PAIR] = (dk[place, :] * SCALE).astype(BF16)
        ref[dc, rows, 2 * PAIR :] = dv[place, :].astype(BF16)


def own_pair(tokens, width, pair):
    return pl.BlockSpec((1, 1, tokens, width), lambda i, order, coords: (0, pair, 0, 0))


def all_of(shape):
    return pl.BlockSpec(shape, lambda i, *scalars: (0,) * len(shape))


def attention(order, coords, own, got, far, active, pair):
    tokens = far[0].shape[1]
    length = 4 * tokens
    out = (2, tokens, PAIR)
    return pl.pallas_call(
        functools.partial(attention_kernel, active),
        grid_spec=pltpu.PrefetchScalarGridSpec(
            num_scalar_prefetch=2,
            grid=(1,),
            in_specs=[own_pair(tokens, 3 * PAIR, pair)] * 2 + [all_of(f.shape) for f in far],
            out_specs=[all_of(out)] * 2 + [all_of((8, length))],
            scratch_shapes=[pltpu.VMEM((length, PAIR), BF16)] * 4,
        ),
        out_shape=[jax.ShapeDtypeStruct(out, BF16)] * 2 + [jax.ShapeDtypeStruct((8, length), F32)],
        compiler_params=pltpu.CompilerParams(vmem_limit_bytes=VMEM_LIMIT),
        cost_estimate=FREE,
    )(order, coords, own, got, *far)


def attention_back(order, coords, own, got, far, grad_own, grad_got, grad_far, lse, actives, pair):
    tokens = far[0].shape[1]
    length = 4 * tokens
    out = (2, tokens, 3 * PAIR)
    return pl.pallas_call(
        functools.partial(attention_back_kernel, actives, len(far), len(grad_far)),
        grid_spec=pltpu.PrefetchScalarGridSpec(
            num_scalar_prefetch=2,
            grid=(1,),
            in_specs=[own_pair(tokens, 3 * PAIR, pair)] * 2
            + [all_of(f.shape) for f in far]
            + [own_pair(tokens, PAIR, pair)] * 2
            + [all_of(f.shape) for f in grad_far]
            + [all_of(lse.shape)],
            out_specs=[all_of(out)] * 2,
            scratch_shapes=[pltpu.VMEM((length, PAIR), BF16)] * 4
            + [pltpu.VMEM((length, PAIR), F32)] * 3,
        ),
        out_shape=[jax.ShapeDtypeStruct(out, BF16)] * 2,
        compiler_params=pltpu.CompilerParams(vmem_limit_bytes=VMEM_LIMIT),
        cost_estimate=FREE,
    )(order, coords, own, got, *far, grad_own, grad_got, *grad_far, lse)


def small_kernel(kernel, coords, arrays, out_shape):
    return pl.pallas_call(
        kernel,
        grid_spec=pltpu.PrefetchScalarGridSpec(
            num_scalar_prefetch=1,
            grid=(1,),
            in_specs=[all_of(a.shape) for a in arrays],
            out_specs=[all_of(o.shape) for o in out_shape],
        ),
        out_shape=out_shape,
        compiler_params=pltpu.CompilerParams(vmem_limit_bytes=VMEM_LIMIT),
        cost_estimate=FREE,
    )(coords, *arrays)


def leaving_kernel(coords_ref, mine, got, *outs):
    for pair in range(2):
        outs[pair][0] = mine[1, pair]
        outs[pair][1] = got[1, pair]


def collect_kernel(active, coords_ref, *refs):
    near, new, old, (mine, send) = refs[:2], refs[2:4], refs[4:-2], refs[-2:]
    for pair in range(2):
        here = (new[pair], old[pair]) if old else (new[pair],)
        for dc, out in enumerate((mine, send)):
            out[0, pair] = near[pair][dc]
            out[1, pair] = chosen(coords_ref, active, here, dc)


def streamed(value):
    return pltpu.with_memory_space_constraint(value, pltpu.HBM)


K_STEPS = 4
K_BLOCK = D // K_STEPS


def qkv_kernel(coords_ref, entry, gain, bias, *refs):
    weights, biases, outs, normed_out, blocks, acc = refs[:4], refs[4:8], refs[8:10], refs[10], refs[11], refs[12]
    step = pl.program_id(0)

    @pl.when(step == 0)
    def _():
        normed = layer_norm(entry[...].astype(F32), gain[...], bias[...])[0].astype(BF16)
        normed_out[...] = normed
        for b in range(K_STEPS):
            blocks[b] = normed[:, b * K_BLOCK : (b + 1) * K_BLOCK]
        acc[...] = jnp.zeros_like(acc)

    for quad in range(4):
        acc[quad] += dot(blocks[step], weights[quad][...])

    @pl.when(step == K_STEPS - 1)
    def _():
        for quad in range(4):
            core, y = quad // 2, quad % 2
            value = (acc[quad] + biases[quad][...]).astype(BF16)
            for pair in range(2):
                outs[core][lax.rem(coords_ref[0] + y, 2), pair] = value[:, pair * 3 * PAIR : (pair + 1) * 3 * PAIR]


def qkv_forward(coords, entry, w):
    tokens = entry.shape[0]
    weights = [streamed(w["qkv"][i][j]) for i in range(2) for j in range(2)]
    biases = [w["qkv_bias"][i][:, j * 768 : (j + 1) * 768] for i in range(2) for j in range(2)]
    wide, row = all_of((tokens, D)), all_of((1, D))
    heads = (2, 2, tokens, 3 * PAIR)
    return pl.pallas_call(
        qkv_kernel,
        grid_spec=pltpu.PrefetchScalarGridSpec(
            num_scalar_prefetch=1,
            grid=(K_STEPS,),
            in_specs=[wide, row, row]
            + [pl.BlockSpec((K_BLOCK, 768), lambda j, coords: (j, 0))] * 4
            + [all_of((1, 768))] * 4,
            out_specs=[all_of(heads)] * 2 + [wide],
            scratch_shapes=[pltpu.VMEM((K_STEPS, tokens, K_BLOCK), BF16), pltpu.VMEM((4, tokens, 768), F32)],
        ),
        out_shape=[jax.ShapeDtypeStruct(heads, BF16), pltpu.HBM(heads, BF16), pltpu.HBM((tokens, D), BF16)],
        compiler_params=pltpu.CompilerParams(vmem_limit_bytes=VMEM_LIMIT),
        cost_estimate=FREE,
    )(coords, entry, w["ln1_gain"], w["ln1_bias"], *weights, *biases)


def qkv_back_kernel(coords_ref, mine, other, entry, gain, d_mid, *refs):
    weights, d_entry, ln_gain, ln_bias, sums, blocks = refs[:4], refs[4], refs[5], refs[6], refs[7:9], refs[9]
    step = pl.program_id(0)
    grad = jnp.zeros(blocks.shape[1:], F32)
    for quad in range(4):
        ref = (mine, other)[quad // 2]
        rel = lax.rem(coords_ref[0] + quad % 2, 2)
        for pair in range(2):
            columns = slice(pair * 3 * PAIR, (pair + 1) * 3 * PAIR)
            grad += dot_back(ref[rel, pair], weights[quad][:, columns])
    blocks[step] = grad

    @pl.when(step == K_STEPS - 1)
    def _():
        for quad in range(4):
            ref = (mine, other)[quad // 2]
            rel = lax.rem(coords_ref[0] + quad % 2, 2)
            for pair in range(2):
                columns = slice(pair * 3 * PAIR, (pair + 1) * 3 * PAIR)
                values = ref[rel, pair].astype(F32)
                sums[quad // 2][quad % 2 : quad % 2 + 1, columns] = jnp.sum(values, axis=0, keepdims=True)
        whole = jnp.concatenate([blocks[b] for b in range(K_STEPS)], axis=1)
        _, normal, inverse = layer_norm(entry[...].astype(F32), gain[...], 0.0)
        through, d_gain, d_bias = norm_back(whole, normal, inverse, gain[...])
        ln_gain[...] = d_gain.reshape(1, D)
        ln_bias[...] = d_bias.reshape(1, D)
        d_entry[...] = (d_mid[...] + through).astype(BF16)


def qkv_back(coords, mine, other, entry, d_mid, w):
    tokens = entry.shape[0]
    weights = [streamed(w["qkv"][i][j]) for i in range(2) for j in range(2)]
    wide, row = all_of((tokens, D)), all_of((1, D))
    line = jax.ShapeDtypeStruct((1, D), F32)
    return pl.pallas_call(
        qkv_back_kernel,
        grid_spec=pltpu.PrefetchScalarGridSpec(
            num_scalar_prefetch=1,
            grid=(K_STEPS,),
            in_specs=[all_of(mine.shape)] * 2
            + [wide, row, wide]
            + [pl.BlockSpec((K_BLOCK, 768), lambda j, coords: (j, 0))] * 4,
            out_specs=[wide, row, row] + [all_of((2, 768))] * 2,
            scratch_shapes=[pltpu.VMEM((K_STEPS, tokens, K_BLOCK), F32)],
        ),
        out_shape=[jax.ShapeDtypeStruct((tokens, D), BF16), line, line]
        + [jax.ShapeDtypeStruct((2, 768), F32)] * 2,
        compiler_params=pltpu.CompilerParams(vmem_limit_bytes=VMEM_LIMIT),
        cost_estimate=FREE,
    )(coords, mine, other, entry, w["ln1_gain"], d_mid, *weights)


def head_columns(coords_ref, core, y, pair):
    quad = lax.rem(coords_ref[3] + core, 2) * 2 + lax.rem(coords_ref[0] + y, 2)
    return pl.multiple_of((quad * 2 + pair) * PAIR, PAIR)


def half_columns(coords_ref, core):
    return pl.ds(pl.multiple_of(lax.rem(coords_ref[3] + core, 2) * (D // 2), D // 2), D // 2)


def out_kernel(coords_ref, entry, mine, other, own_weight, other_weight, bias, mid, att):
    for core, ref in enumerate((mine, other)):
        for y in range(2):
            for pair in range(2):
                att[:, pl.ds(head_columns(coords_ref, core, y, pair), PAIR)] = ref[y, pair]
    for core, weight in enumerate((own_weight, other_weight)):
        columns = half_columns(coords_ref, core)
        mid[:, columns] = entry[:, columns].astype(F32) + (dot(att[...], weight[...]) + bias[:, columns])


def out_forward(coords, entry, mine, other, w):
    shape = entry.shape
    arrays = [entry, mine, other, *w["out"], w["out_bias"]]
    return small_kernel(out_kernel, coords, arrays, [jax.ShapeDtypeStruct(shape, F32), pltpu.HBM(shape, BF16)])


FF_BLOCK = 1024
FF_STEPS = FF // FF_BLOCK
CURVE = 0.044715
ROOT = (2.0 / jnp.pi) ** 0.5


def feed_up_kernel(first, *refs):
    if first:
        mid, gain, bias, fc, fc_bias, normed, act, slope = refs

        @pl.when(pl.program_id(0) == 0)
        def _():
            normed[...] = layer_norm(mid[...], gain[...], bias[...])[0].astype(BF16)
    else:
        normed, fc, fc_bias, act, slope = refs
    before = dot(normed[...], fc[...]) + fc_bias[...]
    square = before * before
    bent = jnp.tanh(ROOT * before * (1.0 + CURVE * square))
    act[...] = (0.5 * before * (1.0 + bent)).astype(BF16)
    slope[...] = (
        0.5 * (1.0 + bent) + 0.5 * ROOT * before * (1.0 - bent * bent) * (1.0 + 3.0 * CURVE * square)
    ).astype(BF16)


def feed_up_half(first, given, fc, fc_bias):
    tokens = given[0].shape[0]
    row, wide = all_of((1, D)), all_of((tokens, D))
    along = lambda rows: pl.BlockSpec((rows, FF_BLOCK), lambda j: (0, j))
    outs = [(wide, jax.ShapeDtypeStruct((tokens, D), BF16))] if first else []
    outs += [(along(tokens), jax.ShapeDtypeStruct((tokens, FF // 2), BF16))] * 2
    return pl.pallas_call(
        functools.partial(feed_up_kernel, first),
        grid=(FF_STEPS // 2,),
        in_specs=([wide, row, row] if first else [wide]) + [along(D), along(1)],
        out_specs=[spec for spec, _ in outs],
        out_shape=[shape for _, shape in outs],
        compiler_params=pltpu.CompilerParams(vmem_limit_bytes=VMEM_LIMIT),
        cost_estimate=FREE,
    )(*given, fc, fc_bias)


def feed_up(middle, w):
    given = (middle, w["ln2_gain"], w["ln2_bias"])
    normed, act_own, slope_own = feed_up_half(True, given, w["fc"][0], w["fc_bias"][0])
    act_other, slope_other = feed_up_half(False, (normed,), w["fc"][1], w["fc_bias"][1])
    return normed, (act_own, act_other), (slope_own, slope_other)


def ff_at(i):
    count = FF_STEPS // 2
    return (lambda j: jnp.minimum(j, count - 1)) if i == 0 else (lambda j: jnp.maximum(j - count, 0))


def ff_specs(rows, axis):
    def one(i):
        at = ff_at(i)
        if axis == 1:
            return pl.BlockSpec((rows, FF_BLOCK), lambda j, *scalars: (0, at(j)))
        return pl.BlockSpec((FF_BLOCK, rows), lambda j, *scalars: (at(j), 0))

    return [one(0), one(1)]


def feed_down_kernel(mid, bias, act_own, act_other, proj_own, proj_other, result, acc):
    step = pl.program_id(0)

    @pl.when(step == 0)
    def _():
        acc[...] = mid[...] + bias[...]

    for i, (act, proj) in enumerate(((act_own, proj_own), (act_other, proj_other))):

        @pl.when(step // (FF_STEPS // 2) == i)
        def _():
            acc[...] += dot(act[...], proj[...])

    @pl.when(step == FF_STEPS - 1)
    def _():
        result[...] = acc[...].astype(BF16)


def feed_down(middle, act, w):
    tokens = middle.shape[0]
    wide = all_of((tokens, D))
    return pl.pallas_call(
        feed_down_kernel,
        grid=(FF_STEPS,),
        in_specs=[wide, all_of((1, D))] + ff_specs(tokens, 1) + ff_specs(D, 0),
        out_specs=wide,
        out_shape=jax.ShapeDtypeStruct((tokens, D), BF16),
        scratch_shapes=[pltpu.VMEM((tokens, D), F32)],
        compiler_params=pltpu.CompilerParams(vmem_limit_bytes=VMEM_LIMIT),
        cost_estimate=FREE,
    )(middle, w["proj_bias"], *act, *w["proj"])


def feed_back_kernel(coords_ref, *refs):
    upstream, mid, gain, fc, proj, slope, out_weights = refs[0], refs[1], refs[2], refs[3:5], refs[5:7], refs[7:9], refs[9:11]
    refs = refs[11:]
    d_mid, dy1, d_pre, fc_sum, ln_gain, ln_bias, proj_sum, heads, acc = (
        refs[0],
        refs[1],
        refs[2:4],
        refs[4:6],
        refs[6],
        refs[7],
        refs[8],
        refs[9:11],
        refs[11],
    )
    step = pl.program_id(0)

    @pl.when(step == 0)
    def _():
        acc[...] = jnp.zeros_like(acc)
        proj_sum[...] = jnp.sum(upstream[...].astype(F32), axis=0, keepdims=True)

    for i in range(2):

        @pl.when(step // (FF_STEPS // 2) == i)
        def _():
            grad = (slope[i][...].astype(F32) * dot_back(upstream[...], proj[i][...])).astype(BF16)
            d_pre[i][...] = grad
            fc_sum[i][...] = jnp.sum(grad.astype(F32), axis=0, keepdims=True)
            acc[...] += dot_back(grad, fc[i][...])

    @pl.when(step == FF_STEPS - 1)
    def _():
        _, normal, inverse = layer_norm(mid[...], gain[...], 0.0)
        through, d_gain, d_bias = norm_back(acc[...], normal, inverse, gain[...])
        ln_gain[...] = d_gain.reshape(1, D)
        ln_bias[...] = d_bias.reshape(1, D)
        d_mid[...] = upstream[...].astype(F32) + through
        dy1[...] = d_mid[...].astype(BF16)
        grads = [dy1[:, half_columns(coords_ref, core)] for core in range(2)]
        for core in range(2):
            for y in range(2):
                for pair in range(2):
                    rows = pl.ds(head_columns(coords_ref, core, y, pair), PAIR)
                    value = dot_back(grads[0], out_weights[0][rows, :]) + dot_back(grads[1], out_weights[1][rows, :])
                    heads[core][y, pair] = value.astype(BF16)


def feed_back(coords, upstream, middle, slope, w):
    tokens = upstream.shape[0]
    row, wide = all_of((1, D)), all_of((tokens, D))
    line = jax.ShapeDtypeStruct((1, D), F32)
    heads = (2, 2, tokens, PAIR)
    return pl.pallas_call(
        feed_back_kernel,
        grid_spec=pltpu.PrefetchScalarGridSpec(
            num_scalar_prefetch=1,
            grid=(FF_STEPS,),
            in_specs=[wide, wide, row]
            + ff_specs(D, 1)
            + ff_specs(D, 0)
            + ff_specs(tokens, 1)
            + [all_of((D, D // 2))] * 2,
            out_specs=[wide, wide] + ff_specs(tokens, 1) + ff_specs(1, 1) + [row] * 3 + [all_of(heads)] * 2,
            scratch_shapes=[pltpu.VMEM((tokens, D), F32)],
        ),
        out_shape=[
            pltpu.HBM((tokens, D), F32),
            pltpu.HBM((tokens, D), BF16),
            *[pltpu.HBM((tokens, FF // 2), BF16)] * 2,
            *[jax.ShapeDtypeStruct((1, FF // 2), F32)] * 2,
            line,
            line,
            line,
            *[jax.ShapeDtypeStruct(heads, BF16)] * 2,
        ],
        compiler_params=pltpu.CompilerParams(vmem_limit_bytes=VMEM_LIMIT),
        cost_estimate=FREE,
    )(coords, upstream, middle, w["ln2_gain"], *w["fc"], *w["proj"], *slope, *w["out"])


def together(first, *others):
    return lax.optimization_barrier((first, *others))


def to_heads(coords, mine, other, active):
    got = swap_cores(other)
    shape = pltpu.HBM((2, *mine.shape[2:]), BF16)
    return got, [swap_y(v, active) for v in small_kernel(leaving_kernel, coords, [mine, got], [shape] * 2)]


def to_tokens(coords, near, back, old, active):
    shape = (2, *near[0].shape)
    outs = [jax.ShapeDtypeStruct(shape, BF16), pltpu.HBM(shape, BF16)]
    mine, send = small_kernel(functools.partial(collect_kernel, active), coords, [*near, *back, *old], outs)
    return mine, swap_cores(send)


def layer_forward(entry, w, order, coords, active, old, late=None):
    mine, other, normed = qkv_forward(coords, entry, w)
    if late is not None:
        next(late)
        other = late.send(other)
    got, far = to_heads(coords, mine, other, active)
    if late is not None:
        far[1] = late.send(far[1])
    far = [(v, old["far"][pair][0]) if old else (v,) for pair, v in enumerate(far)]
    near, back, lse = [], [], []
    for pair in range(2):
        heads, heads_far, pair_lse = attention(order, coords, mine, got, far[pair], active, pair)
        near.append(heads)
        back.append(swap_y(heads_far, active))
        lse.append(pair_lse)
    middle, attended = out_forward(
        coords, entry, *to_tokens(coords, near, back, old["back"] if old else [], active), w
    )
    if late is not None:
        middle = late.send(middle)
    normed2, act, slope = feed_up(middle, w)
    return dict(
        entry=entry,
        normed=normed,
        qkv=(mine, got),
        far=far,
        back=back,
        lse=lse,
        attended=attended,
        middle=middle,
        normed2=normed2,
        act=act,
        slope=slope,
    )


def layer_backward(upstream, s, w, order, coords, active, old):
    g = {}
    last = old is not None
    d_mid, dy1, d_pre_own, d_pre_other, *sums, mine, other = feed_back(
        coords, upstream, s["middle"], s["slope"], w
    )
    got, far = to_heads(coords, mine, other, active)
    if last:
        jobs = [
            (s["normed2"], s["swapped"][1], d_pre_own, swap_cores(d_pre_other), 0, FF // 2),
            (s["attended"], s["swapped"][3], dy1, swap_cores(dy1), None, D // 2),
        ]
        grad = plain_grad(s["act"][0], s["swapped"][0], upstream, swap_cores(upstream))
        far[0], far[1], parts, grad = together(far[0], far[1], weight_grad(coords, True, jobs), grad)
        arrived = [shift(parts[1], Z, 1), shift(parts[2], Z, -1)]
        proj_part = sum_by_axes(grad.reshape(4, 4, 2, -1, D), (X,))
    far = [(v, old["far"][pair][0]) if old else (v,) for pair, v in enumerate(far)]
    near, back = [], []
    for pair in range(2):
        args = (*s["qkv"], s["far"][pair], mine, got, far[pair], s["lse"][pair], (1, active), pair)
        own, heads_far = attention_back(order, coords, *args)
        near.append(own)
        back.append(swap_y(heads_far, active))
    if last:
        back[1], arrived = together(back[1], arrived)
        later = relay(coords, parts, *arrived)
    d_mine, d_other = to_tokens(coords, near, back, old["back"] if old else [], active)
    d_entry, ln1_gain, ln1_bias, *qkv_sums = qkv_back(coords, d_mine, d_other, s["entry"], d_mid, w)
    if last:
        small = pack(coords, [ln1_gain, ln1_bias, dy1, *sums[2:5], *qkv_sums, *sums[0:2]])
        lefts = (s["normed"], s["swapped"][2])
        other = swap_cores(d_other)
        (qkv_part,) = weight_grad(coords, False, [(*lefts, d_mine, other, i, 768) for i in range(2)], small)
        d_entry, qkv_part, proj_part, later = together(d_entry, qkv_part, proj_part, later)
        g["qkv"] = lax.all_to_all(qkv_part.reshape(16, *qkv_part.shape[2:]), (Z, X), 0, 0, tiled=True)
        g["proj"] = sum_by_axes(proj_part, (Z,))
        shape = pltpu.HBM((2, *parts[0].shape[2:]), BF16)
        chunks = small_kernel(chunks_kernel, coords, [parts[0], *arrived, *later], [shape] * 4)
        g["fc"] = [chunks[0]] + [shift(chunks[k], X, k) for k in (1, 2, 3)]
    g.update(far=far, back=back)
    return d_entry, g


SMALL_ROWS = 12


def pack_kernel(
    coords_ref, ln1_gain, ln1_bias, dy1, ln2_gain, ln2_bias, proj, qkv_own, qkv_other, fc_own, fc_other, out
):
    first = coords_ref[3] == 0
    out_bias = jnp.sum(dy1[...].astype(F32), axis=0, keepdims=True)
    whole = [ln1_gain[...], ln1_bias[...], out_bias, ln2_gain[...], ln2_bias[...], proj[...]]
    fc = [jnp.where(first, fc_own[...], fc_other[...]), jnp.where(first, fc_other[...], fc_own[...])]
    qkv = [jnp.where(first, qkv_own[...], qkv_other[...]), jnp.where(first, qkv_other[...], qkv_own[...])]
    out[...] = jnp.zeros_like(out)
    for z in range(4):
        for y in range(2):
            blocks = [v[:, y * 512 + z * 128 : y * 512 + (z + 1) * 128] for v in whole]
            quad = qkv[z // 2][z % 2 : z % 2 + 1]
            for pair in range(2):
                at = pair * 3 * PAIR + y * 2 * PAIR
                blocks.append(quad[:, at : at + PAIR])
            for x in range(4):
                at = ((x * 4 + z) * 2 + y) * 64
                blocks.append(jnp.concatenate([v[:, at : at + 64] for v in fc], axis=1))
            rows = jnp.concatenate(blocks, axis=0).astype(BF16)
            for core in range(2):
                out[z, y, core * 16 : core * 16 + SMALL_ROWS] = rows


def pack(coords, sums):
    return small_kernel(pack_kernel, coords, sums, [jax.ShapeDtypeStruct((4, 2, 32, 128), BF16)])[0]


def chunks_kernel(coords_ref, own, up, down, up_later, down_later, *outs):
    for k in range(4):
        x = lax.rem(coords_ref[2] + k, 4)
        low, place = x < 2, lax.rem(x, 2)
        below = jnp.where(low, up_later[place], up[1, place]).astype(F32)
        above = jnp.where(low, down[1, place], down_later[place]).astype(F32)
        outs[k][...] = (own[x].astype(F32) + below + above).astype(BF16)


def y_kernel(coords_ref, *refs):
    parts, qkv, mine, send = refs[:4], refs[4], refs[5], refs[6]
    columns = parts[0].shape[2]
    for dy, out in enumerate((mine, send)):
        y = lax.rem(coords_ref[0] + dy, 2)
        out[:, 0:columns] = total([part[y] for part in parts]).astype(out.dtype)
        out[:, columns:] = total([qkv[i, y] for i in range(16)]).astype(out.dtype)


def core_kernel(coords_ref, mine, got, keep, send):
    rows = keep.shape[0]
    for core, out in enumerate((keep, send)):
        here = pl.ds(pl.multiple_of(lax.rem(coords_ref[3] + core, 2) * rows, rows), rows)
        out[...] = mine[here, :] + got[here, :].astype(F32)


def final_kernel(coords_ref, keep, got, qkv, out, fc, ln1_gain, ln1_bias, qv, out_bias, ln2_gain, ln2_bias, fc_bias, proj):
    first = coords_ref[3] == 0
    halves = [jnp.where(first, keep[...], got[...]), jnp.where(first, got[...], keep[...])]
    half_fc, half_out, small = FF // 2, D // 2, 128
    for core in range(2):
        out[:, core * half_out : (core + 1) * half_out] = halves[core][:, half_fc : half_fc + half_out]
        for pair in range(4):
            for part in range(3):
                at = half_fc + half_out + (pair * 3 + part) * PAIR
                to = part * D + (core * 4 + pair) * PAIR
                qkv[:, to : to + PAIR] = halves[core][:, at : at + PAIR]
    for y in range(2):
        for z in range(4):
            for x in range(4):
                at = ((x * 4 + z) * 2 + y) * 64
                to = ((y * 4 + z) * 4 + x) * 128
                fc[:, to : to + 128] = jnp.concatenate([v[:, at : at + 64] for v in halves], axis=1)
    at = half_fc + half_out + 3 * half_out
    rows = keep[:, at : at + small] + got[:, at : at + small]
    x, c = coords_ref[2], coords_ref[3]
    part = x * 2 + c
    number = lax.broadcasted_iota(jnp.int32, rows.shape, 0)

    def one(at, count, width):
        per_row = small // width
        row = at + part // per_row
        line = jnp.sum(jnp.where(number == row, rows, 0.0), axis=0, keepdims=True)
        lane = (part % per_row) * width
        line = pltpu.roll(jnp.broadcast_to(line, (8, small)), lax.rem(small - lane, small), 1)
        return line[0:1, 0:width]

    for i, ref in enumerate((ln1_gain, ln1_bias, out_bias, ln2_gain, ln2_bias, proj)):
        ref[...] = one(i, 1, 16)
    qv[...] = one(6, 2, 32)
    fc_bias[...] = one(8, 4, 64)


def to_sequence(values, core):
    micro, rows, width = values.shape
    cut = values.reshape(micro, 2, rows // 2, width)
    keep = lax.dynamic_index_in_dim(cut, core, 1)
    got = swap_cores(lax.dynamic_index_in_dim(cut, 1 - core, 1))
    each = in_order(core, keep, got, 1).reshape(2 * micro, rows // 2, width)
    return lax.all_to_all(each, Z, 0, 0, tiled=True).reshape(2 * rows, width)


def to_z_kernel(coords_ref, first, second, *outs):
    rows = outs[0].shape[1]
    for k in range(4):
        z = lax.rem(coords_ref[1] + k, 4)
        for i, values in enumerate((first, second)):
            outs[k][i] = values[pl.ds(pl.multiple_of(z * rows, rows), rows), :]


def to_rows_of_z(coords, first, second):
    shape = pltpu.HBM((2, first.shape[0] // 4, D), BF16)
    chunks = small_kernel(to_z_kernel, coords, [first, second], [shape] * 4)
    return [chunks[0]] + [shift(chunks[k], Z, k) for k in (1, 2, 3)]


def by_sequence_kernel(coords_ref, *refs):
    arrived, (keep, send, blocks) = refs[:4], refs[4:]
    for i in range(2):
        for k in range(4):
            blocks[i, lax.rem(coords_ref[1] + 4 - k, 4)] = arrived[k][i]
    for i in range(2):
        for micro in range(2):
            keep[i, micro] = blocks[i, micro * 2 + coords_ref[3]]
            send[i, micro] = blocks[i, micro * 2 + 1 - coords_ref[3]]


def rows_kernel(coords_ref, keep, got, acts, in_grads):
    rows = keep.shape[2]
    for core, ref in enumerate((keep, got)):
        here = pl.ds(pl.multiple_of(lax.rem(coords_ref[3] + core, 2) * rows, rows), rows)
        for micro in range(2):
            acts[micro, here, :] = ref[0, micro]
            in_grads[micro, here, :] = ref[1, micro].astype(F32)


def own_rows(coords, arrays):
    rows = arrays[0].shape[1]
    shape = (2, 2, rows, D)
    keep, send = pl.pallas_call(
        by_sequence_kernel,
        grid_spec=pltpu.PrefetchScalarGridSpec(
            num_scalar_prefetch=1,
            grid=(1,),
            in_specs=[all_of(a.shape) for a in arrays],
            out_specs=[all_of(shape)] * 2,
            scratch_shapes=[pltpu.VMEM((2, 4, rows, D), BF16)],
        ),
        out_shape=[jax.ShapeDtypeStruct(shape, BF16), pltpu.HBM(shape, BF16)],
        compiler_params=pltpu.CompilerParams(vmem_limit_bytes=VMEM_LIMIT),
        cost_estimate=FREE,
    )(coords, *arrays)
    outs = [pltpu.HBM((2, 2 * rows, D), t) for t in (BF16, F32)]
    return small_kernel(rows_kernel, coords, [keep, swap_cores(send)], outs)


def by_pair(values):
    lead = values.shape[:-1]
    return values.reshape(*lead, 3, PAIRS, PAIR).swapaxes(-2, -3).reshape(*lead, 3 * D)


def by_core(values):
    lead = values.shape[:-1]
    return jnp.moveaxis(values.reshape(*lead, 2, 4, 4, 2, 64), (-2, -3, -4, -5), (-5, -4, -3, -2)).reshape(*lead, FF)


def on_device(
    inputs,
    cotangent,
    block_order,
    ln1_gain,
    ln1_bias,
    qkv_weight,
    qv_bias,
    out_weight,
    out_bias,
    ln2_gain,
    ln2_bias,
    fc_weight,
    fc_bias,
    proj_weight,
    proj_bias,
):
    section = lax.axis_index("section")
    core = lax.axis_index(CORE)
    coords = jnp.stack([lax.axis_index(a) for a in (*CTX_FSDP, "section")]).astype(jnp.int32)
    first = section == 0
    micro, _, rows, _ = inputs.shape

    vectors = (ln1_gain, ln1_bias, qv_bias, out_bias, ln2_gain, ln2_bias, fc_bias, proj_bias)
    widths = [v.shape[-1] for v in vectors]
    starts = [sum(widths[:i]) for i in range(len(widths))]
    packed = jnp.concatenate([v.reshape(-1) for v in vectors])
    packed = jnp.pad(packed, (0, 16 * 128 - packed.shape[0])).reshape(16, 128)

    qkv_cut = by_pair(qkv_weight[0]).reshape(16, 2, 2, 768)
    out_cut = out_weight[0].reshape(16, 2, 2, 256)
    fc_cut = by_core(fc_weight[0]).reshape(16, 2, 2048)
    halves = [
        jnp.concatenate(
            [qkv_cut[:, i, 0], out_cut[:, i, 0], packed, fc_cut[:, i], qkv_cut[:, i, 1], out_cut[:, i, 1]],
            axis=1,
        )
        for i in range(2)
    ]
    mine = jnp.where(core == 0, halves[0], halves[1])
    other = jnp.where(core == 0, halves[1], halves[0])
    blob = in_order(core, mine, swap_cores(other), 0)
    proj_own = in_order(coords[0], proj_weight[0], shift(proj_weight[0], Y, 1), 0)
    proj_own = lax.all_gather(proj_own, Z, axis=0, tiled=True)
    ring_x = first_ring(both_y(blob[:, :3200]), X)
    ring_z = first_ring(both_y(blob[:, 3200:]), Z)
    tokens = to_sequence(jnp.concatenate([inputs[:, 0], cotangent[:, 0]], axis=-1), core)
    ring_x, ring_z, tokens = together(ring_x, ring_z, tokens)
    entry, given = tokens[:, :D], tokens[:, D:]
    pieces_x = second_ring(ring_x[..., :1152], Z)
    pieces_z = second_ring(ring_z, X)
    fc_halves = (ring_x[:2, ..., 1152:], ring_x[2:, ..., 1152:])
    (pieces_x, pieces_z), fc_halves, proj_own, entry = together((pieces_x, pieces_z), fc_halves, proj_own, entry)
    proj_own = lax.all_gather(proj_own, X, axis=0, tiled=True)
    cuts = ((0, 768, 0, 0), (768, 256, 1, 0))
    qkv_0, out_0, packed = assemble(coords, X, cuts + ((1024, 128, 2, 0),), pieces_x)
    qkv_1, out_1 = assemble(coords, Z, cuts, pieces_z)
    out_own = jnp.concatenate([out_0, out_1], axis=1)
    w = {
        "qkv": ((qkv_0, qkv_1), (swap_cores(qkv_0), swap_cores(qkv_1))),
        "out": (out_own, swap_cores(out_own)),
    }

    def late_weights():
        value = yield
        low, high = to_neighbours(fc_halves, Z)
        value, low, high = together(value, low, high)
        far = to_neighbours((low, high), Z)
        value = yield value
        value, low_late, high_late = together(value, *to_neighbours(fc_halves[::-1], Z))
        value = yield value
        pieces = [fc_halves, far, (low, low_late), (high_late, high)]
        value, pieces = together(value, pieces)
        (fc_own,) = assemble(coords, X, ((0, 2048, 0, 0),), pieces)
        w["fc"] = (fc_own, swap_cores(fc_own))
        w["proj"] = (proj_own, swap_cores(proj_own))
        yield value

    packed = packed.reshape(32, 2, 16, 128)[:, :, :2].reshape(64, 256)
    names = ("ln1_gain", "ln1_bias", "qv", "out_bias", "ln2_gain", "ln2_bias", "fc", "proj_bias")
    vector = {
        name: packed[:, start : start + width].reshape(1, -1).astype(F32)
        for name, start, width in zip(names, starts, widths)
    }
    qv, fc_vector = vector.pop("qv"), by_core(vector.pop("fc"))
    qkv_vector = by_pair(jnp.concatenate([qv[:, :D], jnp.zeros((1, D), F32), qv[:, D:]], axis=1))
    w.update(vector)
    w["qkv_bias"] = (half(qkv_vector, core, 1), half(qkv_vector, 1 - core, 1))
    w["fc_bias"] = (half(fc_vector, core, 1), half(fc_vector, 1 - core, 1))

    early = layer_forward(entry, w, block_order, coords, 0, None, late_weights())
    result = feed_down(early["middle"], early["act"], w)
    arriving = lax.ppermute(result, "section", [(0, 1)])
    entry = jnp.where(first, entry, arriving)
    saved = layer_forward(entry, w, block_order, coords, 1, early)

    d_entry, early = layer_backward(given, saved, w, block_order, coords, 1, None)
    arriving = lax.ppermute(d_entry, "section", [(1, 0)])
    middle, act_other, normed2, normed, attended, _ = together(
        saved["middle"], saved["act"][1], saved["normed2"], saved["normed"], saved["attended"], d_entry
    )
    swapped = [swap_cores(v) for v in (act_other, normed2, normed, attended)]
    result = feed_down(middle, saved["act"], w)
    arriving, result, saved["swapped"] = together(arriving, result, swapped)
    upstream = jnp.where(first, arriving, given)
    d_entry, g = layer_backward(upstream, saved, w, block_order, coords, 0, early)
    tokens = to_rows_of_z(coords, result, d_entry)
    g["fc"], proj_part = together(g["fc"], g["proj"])
    proj_grad = sum_by_axes(proj_part, (Y,)).astype(F32)
    parts = [streamed(v) for v in (*g["fc"], g["qkv"])]
    columns = parts[0].shape[2] + g["qkv"].shape[3]
    outs = [jax.ShapeDtypeStruct((32, columns), F32), pltpu.HBM((32, columns), BF16)]
    mine, send = small_kernel(y_kernel, coords, parts, outs)
    mine, tokens = together(mine, tokens)
    acts, in_grads = own_rows(coords, tokens)
    outs = [jax.ShapeDtypeStruct((16, columns), F32), pltpu.HBM((16, columns), F32)]
    keep, send = small_kernel(core_kernel, coords, [mine, shift(send, Y, 1)], outs)
    widths = (3 * D, D, FF, 16, 16, 32, 16, 16, 16, 64, 16)
    outs = [pltpu.HBM((16 if n >= D else 1, n), F32) for n in widths]
    qkv_grad, out_grad, fc_grad, *small = small_kernel(final_kernel, coords, [keep, swap_cores(send)], outs)
    shape = (1, micro, 1, rows, D)
    return (
        acts.reshape(shape),
        in_grads.reshape(shape),
        small[0],
        small[1],
        qkv_grad[None],
        small[2],
        out_grad[None],
        small[3],
        small[4],
        small[5],
        fc_grad[None],
        small[6],
        proj_grad[None],
        small[7],
    )


def solution(mesh):
    torus = Mesh(
        mesh.devices.reshape(mesh.shape["section"], 2, 4, 4, 2),
        ("section", "ctx_0", "ctx_1", "fsdp_0", "fsdp_1"),
    )
    tokens = P(None, FSDP, CTX, None)
    vector = P("section", CTX_FSDP)
    matrix = P("section", CTX_FSDP, None)
    kinds = (vector, vector, matrix, vector, matrix, vector, vector, vector, matrix, vector, matrix, vector)
    results = P("section", None, FSDP, CTX, None)
    return jax.shard_map(
        on_device,
        mesh=torus,
        in_specs=(tokens, tokens, P()) + kinds,
        out_specs=(results, results) + kinds,
        check_vma=False,
    )
```

```python
import functools

import jax
import jax.numpy as jnp
from jax import lax
from jax.experimental import pallas as pl
from jax.experimental.pallas import tpu as pltpu
from jax.sharding import Mesh
from jax.sharding import PartitionSpec as P

D = 1024
HEADS = 16
HEAD_DIM = 64
FF = 4096
PAIRS = 8
PAIR = 128
QUAD = 256
TILE = 256
BLOCK = 64
CTX = ("ctx_0", "ctx_1")
FSDP = ("fsdp_0", "fsdp_1")
CTX_FSDP = CTX + FSDP
Y, Z, X, CORE = CTX_FSDP
EPSILON = 1e-05
MASKED = -1e30
SCALE = HEAD_DIM**-0.5
BF16 = jnp.bfloat16
F32 = jnp.float32
VMEM_LIMIT = 24 * 2**20
FREE = pl.CostEstimate(flops=0, bytes_accessed=0, transcendentals=0)
SOME = pl.CostEstimate(flops=2 * 10**9, bytes_accessed=8 * 10**6, transcendentals=0)


def dot(left, right):
    return jnp.dot(left, right, preferred_element_type=F32)


def dot_rows(left, right):
    return lax.dot_general(left, right, (((0,), (0,)), ((), ())), preferred_element_type=F32)


def dot_back(left, right):
    return lax.dot_general(left, right, (((1,), (1,)), ((), ())), preferred_element_type=F32)


def shift(value, axis, by):
    n = lax.axis_size(axis)
    return lax.ppermute(value, axis, [(i, (i + by) % n) for i in range(n)])


def swap_cores(value):
    return shift(value, CORE, 1)


def swap_y(value, section):
    at = 2 * section
    return lax.ppermute(value, ("section", Y), [(at, at + 1), (at + 1, at)])


def half(value, which, dim):
    size = value.shape[dim] // 2
    return lax.dynamic_slice_in_dim(value, which * size, size, dim)


def in_order(which, mine, other, dim):
    return jnp.where(
        which == 0,
        jnp.concatenate([mine, other], axis=dim),
        jnp.concatenate([other, mine], axis=dim),
    )


def both_y(rows):
    return jnp.stack([rows, shift(rows, Y, 1)])


def first_ring(both, axis):
    return jnp.stack([both] + [shift(both, axis, k) for k in range(1, 4)])


def second_ring(ring, axis):
    return [ring] + [shift(ring, axis, k) for k in (2, 1, 3)]


def to_neighbours(halves, axis):
    return [shift(v, axis, by) for v, by in zip(halves, (1, -1))]


def assemble_kernel(first, cuts, count, coords_ref, *refs):
    outs = refs[4 * count :]
    pieces = [[refs[m * count + k * count // 4].at[k % (4 // count)] for k in range(4)] for m in range(4)]
    y, me = coords_ref[0], coords_ref[1] if first == Z else coords_ref[2]
    for m in range(4):

        @pl.when(pl.program_id(0) == m)
        def _():
            for k in range(4):
                place = lax.rem(me + 4 - k, 4)
                for dy in range(2):
                    at_y = lax.rem(y + dy, 2)
                    for start, width, out, row in cuts:
                        block = pieces[m][k][dy, :, start : start + width]
                        rows = pl.ds(row, block.shape[0])
                        if first == Z:
                            outs[out][at_y, place, 0, rows] = block
                        else:
                            outs[out][at_y, 0, place, rows] = block


def assemble(coords, first, cuts, pieces):
    pieces = [p if isinstance(p, (tuple, list)) else (p,) for p in pieces]
    count = len(pieces[0])
    one = pieces[0][0].shape
    rows = one[2]
    at = 2 if first == Z else 1
    shapes = {}
    for _, width, out, row in cuts:
        shapes[out] = (row + rows, width)
    shapes = [shapes[out] for out in range(len(shapes))]

    def place(m, coords):
        by = jnp.where(m == 1, 2, jnp.where(m == 2, 1, m))
        ring = lax.rem(coords[at] + 4 - by, 4)
        return (0, 0, ring, 0, 0) if first == Z else (0, ring, 0, 0, 0)

    along = (2, 4, 1) if first == Z else (2, 1, 4)
    whole = pl.BlockSpec(one, lambda m, coords: (0, 0, 0, 0))
    outs = pl.pallas_call(
        functools.partial(assemble_kernel, first, cuts, count),
        grid_spec=pltpu.PrefetchScalarGridSpec(
            num_scalar_prefetch=1,
            grid=(4,),
            in_specs=[whole] * (4 * count),
            out_specs=[pl.BlockSpec((*along, *shape), place) for shape in shapes],
        ),
        out_shape=[jax.ShapeDtypeStruct((2, 4, 4, *shape), BF16) for shape in shapes],
        compiler_params=pltpu.CompilerParams(vmem_limit_bytes=VMEM_LIMIT),
        cost_estimate=FREE,
    )(coords, *[streamed(part) for piece in pieces for part in piece])
    return [out.reshape(-1, out.shape[-1]) for out in outs]


def weight_grad_kernel(n_jobs, ring, coords_ref, *refs):
    jobs = [refs[4 * j : 4 * j + 4] for j in range(n_jobs)]
    extra = () if ring else (refs[4 * n_jobs],)
    outs, whole = refs[4 * n_jobs + len(extra) : -1], refs[-1]
    rows = whole.shape[2]
    at = 0
    for own_left, other_left, own_right, other_right in jobs:
        for own, other in zip(column_parts(own_right), column_parts(other_right)):
            grad = dot_rows(own_left[...], own()) + dot_rows(other_left[...], other())
            width = grad.shape[1]
            whole[:, :, :, pl.ds(at, width)] = grad.astype(BF16).reshape(4, 4, rows, width)
            at += width
    if not ring:
        for x in range(4):
            whole[:, x, :, pl.ds(at, 128)] = extra[0][:, 0]
        outs[0][:, :, 0] = whole[...]
        return
    own, up, down, up_later, down_later = outs
    part = [whole.at[lax.rem(coords_ref[1] + k, 4)] for k in range(4)]
    own[:, 0] = part[0][...]
    up[0, :, 0], up[1, :, 0] = part[2][0:2], part[1][2:4]
    down[0, :, 0], down[1, :, 0] = part[2][2:4], part[3][0:2]
    up_later[:, 0] = part[1][0:2]
    down_later[:, 0] = part[3][2:4]


def column_parts(ref):
    if len(ref.shape) == 4:
        return [lambda t=t: ref[0, t] for t in range(2)]
    return [lambda at=at: ref[:, pl.ds(at, 256)] for at in range(0, ref.shape[1], 256)]


def weight_grad(coords, ring, jobs, extra=None):
    rows = jobs[0][0].shape[1] // 32
    tokens = jobs[0][0].shape[0]
    columns = 0
    in_specs, arrays = [], []
    for *job, at, width in jobs:
        left = pl.BlockSpec((tokens, 16 * rows), lambda y, coords: (0, y))
        if job[2].ndim == 4:
            shape = (1, *job[2].shape[1:])
            right = pl.BlockSpec(shape, lambda y, coords, at=at: (lax.rem(coords[0] + at, 2), 0, 0, 0))
        elif at is None:
            right = pl.BlockSpec((tokens, width), lambda y, coords: (0, coords[3]))
        else:
            right = pl.BlockSpec((tokens, width), lambda y, coords, at=at: (0, at))
        columns += width
        in_specs += [left, left, right, right]
        arrays += [streamed(v) for v in job]
    if extra is not None:
        in_specs.append(pl.BlockSpec((4, 1, rows, 128), lambda y, coords: (0, y, 0, 0)))
        arrays.append(extra)
        columns += 128
    leads = [(4,), (2, 2), (2, 2), (2,), (2,)] if ring else [(4, 4)]

    def along_y(lead):
        return pl.BlockSpec((*lead, 1, rows, columns), lambda y, coords: (*(0,) * len(lead), y, 0, 0))

    return pl.pallas_call(
        functools.partial(weight_grad_kernel, len(jobs), ring),
        grid_spec=pltpu.PrefetchScalarGridSpec(
            num_scalar_prefetch=1,
            grid=(2,),
            in_specs=in_specs,
            out_specs=[along_y(lead) for lead in leads],
            scratch_shapes=[pltpu.VMEM((4, 4, rows, columns), BF16)],
        ),
        out_shape=[pltpu.HBM((*lead, 2, rows, columns), BF16) for lead in leads],
        compiler_params=pltpu.CompilerParams(vmem_limit_bytes=VMEM_LIMIT),
        cost_estimate=SOME if ring else FREE,
    )(coords, *arrays)


def plain_grad_kernel(own_left, other_left, own_right, other_right, out):
    grad = dot_rows(own_left[...], own_right[...])
    grad = (grad + dot_rows(other_left[...], other_right[...])).astype(BF16)
    for z in range(4):
        for y in range(2):
            out[(y * 4 + z) * 64 : (y * 4 + z + 1) * 64, :] = grad[(z * 2 + y) * 64 : (z * 2 + y + 1) * 64, :]


def plain_grad(own_left, other_left, own_right, other_right):
    tokens, rows = own_left.shape
    columns = own_right.shape[1]
    block = 512
    left = pl.BlockSpec((tokens, block), lambda i: (0, i))
    right = pl.BlockSpec((tokens, columns), lambda i: (0, 0))
    return pl.pallas_call(
        plain_grad_kernel,
        grid=(rows // block,),
        in_specs=[left, left, right, right],
        out_specs=pl.BlockSpec((block, columns), lambda i: (i, 0)),
        out_shape=pltpu.HBM((rows, columns), BF16),
        compiler_params=pltpu.CompilerParams(vmem_limit_bytes=VMEM_LIMIT),
        cost_estimate=SOME,
    )(*[streamed(v) for v in (own_left, other_left, own_right, other_right)])


def sum_by_axes(parts, axes):
    for axis in axes:
        parts = lax.psum_scatter(parts, axis, scatter_dimension=0, tiled=False)
    return parts


def total(parts):
    return functools.reduce(lambda a, b: a + b, [p.astype(F32) for p in parts])


def start_sum(parts, first):
    return [parts[0]] + [shift(parts[k], first, k) for k in (2, 1, 3)]


def relay_kernel(coords_ref, up, low, down, high, up_out, down_out):
    up_out[...] = total([up[...], low[0]]).astype(BF16)
    down_out[...] = total([down[...], high[0]]).astype(BF16)


def relay(coords, parts, low, high):
    shape = pltpu.HBM(parts[3].shape, BF16)
    up, down = small_kernel(relay_kernel, coords, [parts[3], low, parts[4], high], [shape] * 2)
    return shift(up, Z, 1), shift(down, Z, -1)


def layer_norm(values, gain, bias):
    average = jnp.mean(values, axis=-1, keepdims=True)
    centred = values - average
    spread_of = jnp.mean(centred * centred, axis=-1, keepdims=True)
    inverse = lax.rsqrt(spread_of + EPSILON)
    normal = centred * inverse
    return normal * gain + bias, normal, inverse


def norm_back(upstream, normal, inverse, gain):
    scaled = upstream * gain
    first = jnp.mean(scaled, axis=-1, keepdims=True)
    second = jnp.mean(scaled * normal, axis=-1, keepdims=True)
    return (
        inverse * (scaled - first - normal * second),
        jnp.sum(upstream * normal, axis=0),
        jnp.sum(upstream, axis=0),
    )


def head_lanes(shape, head):
    return lax.broadcasted_iota(jnp.int32, shape, 1) // HEAD_DIM == head


def causal(keys):
    rows = lax.broadcasted_iota(jnp.int32, (keys, TILE), 0)
    columns = lax.broadcasted_iota(jnp.int32, (keys, TILE), 1)
    return rows <= columns + (keys - TILE)


def stored_blocks(order_ref, coords_ref):
    y, c = coords_ref[0], coords_ref[3]
    for dy in range(2):
        for dc in range(2):
            for z in range(4):
                stored = lax.rem(y + dy, 2) * 8 + z * 2 + lax.rem(c + dc, 2)
                at = pl.multiple_of(order_ref[stored] * BLOCK, BLOCK)
                yield dy, dc, slice(z * BLOCK, (z + 1) * BLOCK), pl.ds(at, BLOCK)


def chosen(coords_ref, active, refs, index):
    if len(refs) == 1:
        return refs[0][index]
    return jnp.where(coords_ref[4] == active, refs[0][index], refs[1][index])


def attention_kernel(active, order_ref, coords_ref, own, got, *refs):
    far, (out_near, out_far, lse_ref, q, k, v, out) = refs[:-7], refs[-7:]
    for dy, dc, rows, place in stored_blocks(order_ref, coords_ref):
        if dy == 0:
            block = (own, got)[dc][0, 0, rows, :]
        else:
            block = chosen(coords_ref, active, far, (dc, rows, slice(None)))
        q[place, :] = block[:, 0:PAIR]
        k[place, :] = block[:, PAIR : 2 * PAIR] * SCALE
        v[place, :] = block[:, 2 * PAIR :]
    length = q.shape[0]
    lse_ref[...] = jnp.zeros_like(lse_ref)
    for tile in range(length // TILE):
        keys = (tile + 1) * TILE
        here = pl.ds(tile * TILE, TILE)
        outs = []
        for head in range(2):
            queries = q[here, :]
            queries = jnp.where(head_lanes(queries.shape, head), queries, jnp.zeros_like(queries))
            scores = dot_back(k[0:keys, :], queries)
            scores = jnp.where(causal(keys), scores, MASKED)
            highest = jnp.max(scores, axis=0, keepdims=True)
            probs = jnp.exp(scores - highest)
            total_of = jnp.sum(probs, axis=0, keepdims=True)
            lse_ref[head : head + 1, here] = highest + jnp.log(total_of)
            attended = dot_rows(v[0:keys, :], probs.astype(BF16)) / total_of
            outs.append(attended[head * HEAD_DIM : (head + 1) * HEAD_DIM, :])
        out[here, :] = jnp.concatenate(outs, axis=0).T.astype(BF16)
    for dy, dc, rows, place in stored_blocks(order_ref, coords_ref):
        (out_near, out_far)[dy][dc, rows, :] = out[place, :]


def attention_back_kernel(actives, n_far, n_grad, order_ref, coords_ref, *refs):
    own, got = refs[:2]
    far = refs[2 : 2 + n_far]
    grad_own, grad_got = refs[2 + n_far : 4 + n_far]
    grad_far = refs[4 + n_far : 4 + n_far + n_grad]
    lse_ref, out_near, out_far, q, k, v, g, dq, dk, dv = refs[4 + n_far + n_grad :]
    for dy, dc, rows, place in stored_blocks(order_ref, coords_ref):
        if dy == 0:
            block = (own, got)[dc][0, 0, rows, :]
            grads = (grad_own, grad_got)[dc][0, 0, rows, :]
        else:
            block = chosen(coords_ref, actives[0], far, (dc, rows, slice(None)))
            grads = chosen(coords_ref, actives[1], grad_far, (dc, rows, slice(None)))
        q[place, :] = block[:, 0:PAIR]
        k[place, :] = block[:, PAIR : 2 * PAIR] * SCALE
        v[place, :] = block[:, 2 * PAIR :]
        g[place, :] = grads
    length = q.shape[0]
    dk[...] = jnp.zeros_like(dk)
    dv[...] = jnp.zeros_like(dv)
    for tile in range(length // TILE):
        keys = (tile + 1) * TILE
        here = pl.ds(tile * TILE, TILE)
        outs = []
        for head in range(2):
            lanes = head_lanes((TILE, PAIR), head)
            queries = q[here, :]
            queries = jnp.where(lanes, queries, jnp.zeros_like(queries))
            grads = g[here, :]
            grads = jnp.where(lanes, grads, jnp.zeros_like(grads))
            scores = dot_back(k[0:keys, :], queries)
            probs = jnp.exp(scores - lse_ref[head : head + 1, here])
            probs = jnp.where(causal(keys), probs, 0.0)
            grad_probs = dot_back(v[0:keys, :], grads)
            term = jnp.sum(probs * grad_probs, axis=0, keepdims=True)
            grad_scores = (probs * (grad_probs - term)).astype(BF16)
            dv[0:keys, :] += dot(probs.astype(BF16), grads)
            dk[0:keys, :] += dot(grad_scores, queries)
            grad_q = dot_rows(k[0:keys, :], grad_scores)
            outs.append(grad_q[head * HEAD_DIM : (head + 1) * HEAD_DIM, :])
        dq[here, :] = jnp.concatenate(outs, axis=0).T
    for dy, dc, rows, place in stored_blocks(order_ref, coords_ref):
        ref = (out_near, out_far)[dy]
        ref[dc, rows, 0:PAIR] = dq[place, :].astype(BF16)
        ref[dc, rows, PAIR : 2 * PAIR] = (dk[place, :] * SCALE).astype(BF16)
        ref[dc, rows, 2 * PAIR :] = dv[place, :].astype(BF16)


def own_pair(tokens, width, pair):
    return pl.BlockSpec((1, 1, tokens, width), lambda i, order, coords: (0, pair, 0, 0))


def all_of(shape):
    return pl.BlockSpec(shape, lambda i, *scalars: (0,) * len(shape))


def attention(order, coords, own, got, far, active, pair):
    tokens = far[0].shape[1]
    length = 4 * tokens
    out = (2, tokens, PAIR)
    return pl.pallas_call(
        functools.partial(attention_kernel, active),
        grid_spec=pltpu.PrefetchScalarGridSpec(
            num_scalar_prefetch=2,
            grid=(1,),
            in_specs=[own_pair(tokens, 3 * PAIR, pair)] * 2 + [all_of(f.shape) for f in far],
            out_specs=[all_of(out)] * 2 + [all_of((8, length))],
            scratch_shapes=[pltpu.VMEM((length, PAIR), BF16)] * 4,
        ),
        out_shape=[jax.ShapeDtypeStruct(out, BF16)] * 2 + [jax.ShapeDtypeStruct((8, length), F32)],
        compiler_params=pltpu.CompilerParams(vmem_limit_bytes=VMEM_LIMIT),
        cost_estimate=FREE,
    )(order, coords, own, got, *far)


def attention_back(order, coords, own, got, far, grad_own, grad_got, grad_far, lse, actives, pair):
    tokens = far[0].shape[1]
    length = 4 * tokens
    out = (2, tokens, 3 * PAIR)
    return pl.pallas_call(
        functools.partial(attention_back_kernel, actives, len(far), len(grad_far)),
        grid_spec=pltpu.PrefetchScalarGridSpec(
            num_scalar_prefetch=2,
            grid=(1,),
            in_specs=[own_pair(tokens, 3 * PAIR, pair)] * 2
            + [all_of(f.shape) for f in far]
            + [own_pair(tokens, PAIR, pair)] * 2
            + [all_of(f.shape) for f in grad_far]
            + [all_of(lse.shape)],
            out_specs=[all_of(out)] * 2,
            scratch_shapes=[pltpu.VMEM((length, PAIR), BF16)] * 4
            + [pltpu.VMEM((length, PAIR), F32)] * 3,
        ),
        out_shape=[jax.ShapeDtypeStruct(out, BF16)] * 2,
        compiler_params=pltpu.CompilerParams(vmem_limit_bytes=VMEM_LIMIT),
        cost_estimate=FREE,
    )(order, coords, own, got, *far, grad_own, grad_got, *grad_far, lse)


def small_kernel(kernel, coords, arrays, out_shape):
    return pl.pallas_call(
        kernel,
        grid_spec=pltpu.PrefetchScalarGridSpec(
            num_scalar_prefetch=1,
            grid=(1,),
            in_specs=[all_of(a.shape) for a in arrays],
            out_specs=[all_of(o.shape) for o in out_shape],
        ),
        out_shape=out_shape,
        compiler_params=pltpu.CompilerParams(vmem_limit_bytes=VMEM_LIMIT),
        cost_estimate=FREE,
    )(coords, *arrays)


def leaving_kernel(coords_ref, mine, got, *outs):
    for pair in range(2):
        outs[pair][0] = mine[1, pair]
        outs[pair][1] = got[1, pair]


def collect_kernel(active, coords_ref, *refs):
    near, new, old, (mine, send) = refs[:2], refs[2:4], refs[4:-2], refs[-2:]
    for pair in range(2):
        here = (new[pair], old[pair]) if old else (new[pair],)
        for dc, out in enumerate((mine, send)):
            out[0, pair] = near[pair][dc]
            out[1, pair] = chosen(coords_ref, active, here, dc)


def streamed(value):
    return pltpu.with_memory_space_constraint(value, pltpu.HBM)


K_STEPS = 4
K_BLOCK = D // K_STEPS


def qkv_kernel(coords_ref, entry, gain, bias, *refs):
    weights, biases, outs, normed_out, blocks, acc = refs[:4], refs[4:8], refs[8:10], refs[10], refs[11], refs[12]
    step = pl.program_id(0)

    @pl.when(step == 0)
    def _():
        normed = layer_norm(entry[...].astype(F32), gain[...], bias[...])[0].astype(BF16)
        normed_out[...] = normed
        for b in range(K_STEPS):
            blocks[b] = normed[:, b * K_BLOCK : (b + 1) * K_BLOCK]
        acc[...] = jnp.zeros_like(acc)

    for quad in range(4):
        acc[quad] += dot(blocks[step], weights[quad][...])

    @pl.when(step == K_STEPS - 1)
    def _():
        for quad in range(4):
            core, y = quad // 2, quad % 2
            value = (acc[quad] + biases[quad][...]).astype(BF16)
            for pair in range(2):
                outs[core][lax.rem(coords_ref[0] + y, 2), pair] = value[:, pair * 3 * PAIR : (pair + 1) * 3 * PAIR]


def qkv_forward(coords, entry, w):
    tokens = entry.shape[0]
    weights = [streamed(w["qkv"][i][j]) for i in range(2) for j in range(2)]
    biases = [w["qkv_bias"][i][:, j * 768 : (j + 1) * 768] for i in range(2) for j in range(2)]
    wide, row = all_of((tokens, D)), all_of((1, D))
    heads = (2, 2, tokens, 3 * PAIR)
    return pl.pallas_call(
        qkv_kernel,
        grid_spec=pltpu.PrefetchScalarGridSpec(
            num_scalar_prefetch=1,
            grid=(K_STEPS,),
            in_specs=[wide, row, row]
            + [pl.BlockSpec((K_BLOCK, 768), lambda j, coords: (j, 0))] * 4
            + [all_of((1, 768))] * 4,
            out_specs=[all_of(heads)] * 2 + [wide],
            scratch_shapes=[pltpu.VMEM((K_STEPS, tokens, K_BLOCK), BF16), pltpu.VMEM((4, tokens, 768), F32)],
        ),
        out_shape=[jax.ShapeDtypeStruct(heads, BF16), pltpu.HBM(heads, BF16), pltpu.HBM((tokens, D), BF16)],
        compiler_params=pltpu.CompilerParams(vmem_limit_bytes=VMEM_LIMIT),
        cost_estimate=FREE,
    )(coords, entry, w["ln1_gain"], w["ln1_bias"], *weights, *biases)


def qkv_back_kernel(coords_ref, mine, other, entry, gain, d_mid, *refs):
    weights, d_entry, ln_gain, ln_bias, sums, blocks = refs[:4], refs[4], refs[5], refs[6], refs[7:9], refs[9]
    step = pl.program_id(0)
    grad = jnp.zeros(blocks.shape[1:], F32)
    for quad in range(4):
        ref = (mine, other)[quad // 2]
        rel = lax.rem(coords_ref[0] + quad % 2, 2)
        for pair in range(2):
            columns = slice(pair * 3 * PAIR, (pair + 1) * 3 * PAIR)
            grad += dot_back(ref[rel, pair], weights[quad][:, columns])
    blocks[step] = grad

    @pl.when(step == K_STEPS - 1)
    def _():
        for quad in range(4):
            ref = (mine, other)[quad // 2]
            rel = lax.rem(coords_ref[0] + quad % 2, 2)
            for pair in range(2):
                columns = slice(pair * 3 * PAIR, (pair + 1) * 3 * PAIR)
                values = ref[rel, pair].astype(F32)
                sums[quad // 2][quad % 2 : quad % 2 + 1, columns] = jnp.sum(values, axis=0, keepdims=True)
        whole = jnp.concatenate([blocks[b] for b in range(K_STEPS)], axis=1)
        _, normal, inverse = layer_norm(entry[...].astype(F32), gain[...], 0.0)
        through, d_gain, d_bias = norm_back(whole, normal, inverse, gain[...])
        ln_gain[...] = d_gain.reshape(1, D)
        ln_bias[...] = d_bias.reshape(1, D)
        d_entry[...] = (d_mid[...] + through).astype(BF16)


def qkv_back(coords, mine, other, entry, d_mid, w):
    tokens = entry.shape[0]
    weights = [streamed(w["qkv"][i][j]) for i in range(2) for j in range(2)]
    wide, row = all_of((tokens, D)), all_of((1, D))
    line = jax.ShapeDtypeStruct((1, D), F32)
    return pl.pallas_call(
        qkv_back_kernel,
        grid_spec=pltpu.PrefetchScalarGridSpec(
            num_scalar_prefetch=1,
            grid=(K_STEPS,),
            in_specs=[all_of(mine.shape)] * 2
            + [wide, row, wide]
            + [pl.BlockSpec((K_BLOCK, 768), lambda j, coords: (j, 0))] * 4,
            out_specs=[wide, row, row] + [all_of((2, 768))] * 2,
            scratch_shapes=[pltpu.VMEM((K_STEPS, tokens, K_BLOCK), F32)],
        ),
        out_shape=[jax.ShapeDtypeStruct((tokens, D), BF16), line, line]
        + [jax.ShapeDtypeStruct((2, 768), F32)] * 2,
        compiler_params=pltpu.CompilerParams(vmem_limit_bytes=VMEM_LIMIT),
        cost_estimate=FREE,
    )(coords, mine, other, entry, w["ln1_gain"], d_mid, *weights)


def head_columns(coords_ref, core, y, pair):
    quad = lax.rem(coords_ref[3] + core, 2) * 2 + lax.rem(coords_ref[0] + y, 2)
    return pl.multiple_of((quad * 2 + pair) * PAIR, PAIR)


def half_columns(coords_ref, core):
    return pl.ds(pl.multiple_of(lax.rem(coords_ref[3] + core, 2) * (D // 2), D // 2), D // 2)


def out_kernel(coords_ref, entry, mine, other, own_weight, other_weight, bias, mid, att):
    for core, ref in enumerate((mine, other)):
        for y in range(2):
            for pair in range(2):
                att[:, pl.ds(head_columns(coords_ref, core, y, pair), PAIR)] = ref[y, pair]
    for core, weight in enumerate((own_weight, other_weight)):
        columns = half_columns(coords_ref, core)
        mid[:, columns] = entry[:, columns].astype(F32) + (dot(att[...], weight[...]) + bias[:, columns])


def out_forward(coords, entry, mine, other, w):
    shape = entry.shape
    arrays = [entry, mine, other, *w["out"], w["out_bias"]]
    return small_kernel(out_kernel, coords, arrays, [jax.ShapeDtypeStruct(shape, F32), pltpu.HBM(shape, BF16)])


FF_BLOCK = 1024
FF_STEPS = FF // FF_BLOCK
CURVE = 0.044715
ROOT = (2.0 / jnp.pi) ** 0.5


def feed_up_kernel(first, *refs):
    if first:
        mid, gain, bias, fc, fc_bias, normed, act, slope = refs

        @pl.when(pl.program_id(0) == 0)
        def _():
            normed[...] = layer_norm(mid[...], gain[...], bias[...])[0].astype(BF16)
    else:
        normed, fc, fc_bias, act, slope = refs
    before = dot(normed[...], fc[...]) + fc_bias[...]
    square = before * before
    bent = jnp.tanh(ROOT * before * (1.0 + CURVE * square))
    act[...] = (0.5 * before * (1.0 + bent)).astype(BF16)
    slope[...] = (
        0.5 * (1.0 + bent) + 0.5 * ROOT * before * (1.0 - bent * bent) * (1.0 + 3.0 * CURVE * square)
    ).astype(BF16)


def feed_up_half(first, given, fc, fc_bias):
    tokens = given[0].shape[0]
    row, wide = all_of((1, D)), all_of((tokens, D))
    along = lambda rows: pl.BlockSpec((rows, FF_BLOCK), lambda j: (0, j))
    outs = [(wide, jax.ShapeDtypeStruct((tokens, D), BF16))] if first else []
    outs += [(along(tokens), jax.ShapeDtypeStruct((tokens, FF // 2), BF16))] * 2
    return pl.pallas_call(
        functools.partial(feed_up_kernel, first),
        grid=(FF_STEPS // 2,),
        in_specs=([wide, row, row] if first else [wide]) + [along(D), along(1)],
        out_specs=[spec for spec, _ in outs],
        out_shape=[shape for _, shape in outs],
        compiler_params=pltpu.CompilerParams(vmem_limit_bytes=VMEM_LIMIT),
        cost_estimate=FREE,
    )(*given, fc, fc_bias)


def feed_up(middle, w):
    given = (middle, w["ln2_gain"], w["ln2_bias"])
    normed, act_own, slope_own = feed_up_half(True, given, w["fc"][0], w["fc_bias"][0])
    act_other, slope_other = feed_up_half(False, (normed,), w["fc"][1], w["fc_bias"][1])
    return normed, (act_own, act_other), (slope_own, slope_other)


def copy_kernel(value, out):
    out[...] = value[...]


def held(value):
    rows, columns = value.shape
    block = pl.BlockSpec((rows // 4, columns), lambda i: (i, 0))
    return pl.pallas_call(
        copy_kernel,
        grid=(4,),
        in_specs=[block],
        out_specs=block,
        out_shape=pltpu.VMEM(value.shape, BF16),
        compiler_params=pltpu.CompilerParams(vmem_limit_bytes=8 * 2**20),
        cost_estimate=FREE,
    )(value)


def ff_at(i):
    count = FF_STEPS // 2
    return (lambda j: jnp.minimum(j, count - 1)) if i == 0 else (lambda j: jnp.maximum(j - count, 0))


def ff_specs(rows, axis):
    def one(i):
        at = ff_at(i)
        if axis == 1:
            return pl.BlockSpec((rows, FF_BLOCK), lambda j, *scalars: (0, at(j)))
        return pl.BlockSpec((FF_BLOCK, rows), lambda j, *scalars: (at(j), 0))

    return [one(0), one(1)]


def feed_down_kernel(mid, bias, act_own, act_other, proj_own, proj_other, result, acc):
    step = pl.program_id(0)

    @pl.when(step == 0)
    def _():
        acc[...] = mid[...] + bias[...]

    for i, (act, proj) in enumerate(((act_own, proj_own), (act_other, proj_other))):

        @pl.when(step // (FF_STEPS // 2) == i)
        def _():
            acc[...] += dot(act[...], proj[...])

    @pl.when(step == FF_STEPS - 1)
    def _():
        result[...] = acc[...].astype(BF16)


def feed_down(middle, act, w):
    tokens = middle.shape[0]
    wide = all_of((tokens, D))
    return pl.pallas_call(
        feed_down_kernel,
        grid=(FF_STEPS,),
        in_specs=[wide, all_of((1, D))] + ff_specs(tokens, 1) + ff_specs(D, 0),
        out_specs=wide,
        out_shape=jax.ShapeDtypeStruct((tokens, D), BF16),
        scratch_shapes=[pltpu.VMEM((tokens, D), F32)],
        compiler_params=pltpu.CompilerParams(vmem_limit_bytes=VMEM_LIMIT),
        cost_estimate=FREE,
    )(middle, w["proj_bias"], *act, *w["proj"])


def feed_back_kernel(coords_ref, *refs):
    upstream, mid, gain, fc, proj, slope, out_weights = refs[0], refs[1], refs[2], refs[3:5], refs[5:7], refs[7:9], refs[9:11]
    refs = refs[11:]
    d_mid, dy1, d_pre, fc_sum, ln_gain, ln_bias, proj_sum, heads, acc = (
        refs[0],
        refs[1],
        refs[2:4],
        refs[4:6],
        refs[6],
        refs[7],
        refs[8],
        refs[9:11],
        refs[11],
    )
    step = pl.program_id(0)

    @pl.when(step == 0)
    def _():
        acc[...] = jnp.zeros_like(acc)
        proj_sum[...] = jnp.sum(upstream[...].astype(F32), axis=0, keepdims=True)

    for i in range(2):

        @pl.when(step // (FF_STEPS // 2) == i)
        def _():
            grad = (slope[i][...].astype(F32) * dot_back(upstream[...], proj[i][...])).astype(BF16)
            d_pre[i][...] = grad
            fc_sum[i][...] = jnp.sum(grad.astype(F32), axis=0, keepdims=True)
            acc[...] += dot_back(grad, fc[i][...])

    @pl.when(step == FF_STEPS - 1)
    def _():
        _, normal, inverse = layer_norm(mid[...], gain[...], 0.0)
        through, d_gain, d_bias = norm_back(acc[...], normal, inverse, gain[...])
        ln_gain[...] = d_gain.reshape(1, D)
        ln_bias[...] = d_bias.reshape(1, D)
        d_mid[...] = upstream[...].astype(F32) + through
        dy1[...] = d_mid[...].astype(BF16)
        grads = [dy1[:, half_columns(coords_ref, core)] for core in range(2)]
        for core in range(2):
            for y in range(2):
                for pair in range(2):
                    rows = pl.ds(head_columns(coords_ref, core, y, pair), PAIR)
                    value = dot_back(grads[0], out_weights[0][rows, :]) + dot_back(grads[1], out_weights[1][rows, :])
                    heads[core][y, pair] = value.astype(BF16)


def feed_back(coords, upstream, middle, slope, w):
    tokens = upstream.shape[0]
    row, wide = all_of((1, D)), all_of((tokens, D))
    line = jax.ShapeDtypeStruct((1, D), F32)
    heads = (2, 2, tokens, PAIR)
    return pl.pallas_call(
        feed_back_kernel,
        grid_spec=pltpu.PrefetchScalarGridSpec(
            num_scalar_prefetch=1,
            grid=(FF_STEPS,),
            in_specs=[wide, wide, row]
            + ff_specs(D, 1)
            + ff_specs(D, 0)
            + ff_specs(tokens, 1)
            + [all_of((D, D // 2))] * 2,
            out_specs=[wide, wide] + ff_specs(tokens, 1) + ff_specs(1, 1) + [row] * 3 + [all_of(heads)] * 2,
            scratch_shapes=[pltpu.VMEM((tokens, D), F32)],
        ),
        out_shape=[
            pltpu.HBM((tokens, D), F32),
            pltpu.HBM((tokens, D), BF16),
            *[pltpu.HBM((tokens, FF // 2), BF16)] * 2,
            *[jax.ShapeDtypeStruct((1, FF // 2), F32)] * 2,
            line,
            line,
            line,
            *[jax.ShapeDtypeStruct(heads, BF16)] * 2,
        ],
        compiler_params=pltpu.CompilerParams(vmem_limit_bytes=VMEM_LIMIT),
        cost_estimate=FREE,
    )(coords, upstream, middle, w["ln2_gain"], *w["fc"], *w["proj"], *slope, *w["out"])


def together(first, *others):
    return lax.optimization_barrier((first, *others))


def to_heads(coords, mine, other, active):
    got = swap_cores(other)
    shape = pltpu.HBM((2, *mine.shape[2:]), BF16)
    return got, [swap_y(v, active) for v in small_kernel(leaving_kernel, coords, [mine, got], [shape] * 2)]


def to_tokens(coords, near, back, old, active):
    shape = (2, *near[0].shape)
    outs = [jax.ShapeDtypeStruct(shape, BF16), pltpu.HBM(shape, BF16)]
    mine, send = small_kernel(functools.partial(collect_kernel, active), coords, [*near, *back, *old], outs)
    return mine, swap_cores(send)


def layer_forward(entry, w, order, coords, active, old, late=None):
    mine, other, normed = qkv_forward(coords, entry, w)
    if late is not None:
        next(late)
        other = late.send(other)
    got, far = to_heads(coords, mine, other, active)
    if late is not None:
        far[1] = late.send(far[1])
    far = [(v, old["far"][pair][0]) if old else (v,) for pair, v in enumerate(far)]
    near, back, lse = [], [], []
    for pair in range(2):
        heads, heads_far, pair_lse = attention(order, coords, mine, got, far[pair], active, pair)
        near.append(heads)
        back.append(swap_y(heads_far, active))
        lse.append(pair_lse)
    middle, attended = out_forward(
        coords, entry, *to_tokens(coords, near, back, old["back"] if old else [], active), w
    )
    if late is not None:
        middle = late.send(middle)
    normed2, act, slope = feed_up(middle, w)
    return dict(
        entry=entry,
        normed=normed,
        qkv=(mine, got),
        far=far,
        back=back,
        lse=lse,
        attended=attended,
        middle=middle,
        normed2=normed2,
        act=act,
        slope=slope,
    )


def layer_backward(upstream, s, w, order, coords, active, old):
    g = {}
    last = old is not None
    d_mid, dy1, d_pre_own, d_pre_other, *sums, mine, other = feed_back(
        coords, upstream, s["middle"], s["slope"], w
    )
    got, far = to_heads(coords, mine, other, active)
    if last:
        jobs = [
            (s["normed2"], s["swapped"][1], d_pre_own, swap_cores(d_pre_other), 0, FF // 2),
            (s["attended"], s["swapped"][3], dy1, swap_cores(dy1), None, D // 2),
        ]
        grad = plain_grad(s["act"][0], s["swapped"][0], upstream, swap_cores(upstream))
        far[0], far[1], parts, grad = together(far[0], far[1], weight_grad(coords, True, jobs), grad)
        arrived = [shift(parts[1], Z, 1), shift(parts[2], Z, -1)]
        proj_part = sum_by_axes(grad.reshape(4, 2, 4, -1, D), (X,))
    far = [(v, old["far"][pair][0]) if old else (v,) for pair, v in enumerate(far)]
    near, back = [], []
    for pair in range(2):
        args = (*s["qkv"], s["far"][pair], mine, got, far[pair], s["lse"][pair], (1, active), pair)
        own, heads_far = attention_back(order, coords, *args)
        near.append(own)
        back.append(swap_y(heads_far, active))
    if last:
        back[1], arrived = together(back[1], arrived)
        later = relay(coords, parts, *arrived)
    d_mine, d_other = to_tokens(coords, near, back, old["back"] if old else [], active)
    d_entry, ln1_gain, ln1_bias, *qkv_sums = qkv_back(coords, d_mine, d_other, s["entry"], d_mid, w)
    if last:
        small = pack(coords, [ln1_gain, ln1_bias, dy1, *sums[2:5], *qkv_sums, *sums[0:2]])
        lefts = (s["normed"], s["swapped"][2])
        other = swap_cores(d_other)
        (qkv_part,) = weight_grad(coords, False, [(*lefts, d_mine, other, i, 768) for i in range(2)], small)
        d_entry, qkv_part, proj_part, later = together(d_entry, qkv_part, proj_part, later)
        g["qkv"] = lax.all_to_all(qkv_part.reshape(16, *qkv_part.shape[2:]), (Z, X), 0, 0, tiled=True)
        g["proj"] = sum_by_axes(proj_part, (Y,))
        shape = pltpu.HBM((2, *parts[0].shape[2:]), BF16)
        chunks = small_kernel(chunks_kernel, coords, [parts[0], *arrived, *later], [shape] * 4)
        g["fc"] = [chunks[0]] + [shift(chunks[k], X, k) for k in (1, 2, 3)]
    g.update(far=far, back=back)
    return d_entry, g


SMALL_ROWS = 12


def pack_kernel(
    coords_ref, ln1_gain, ln1_bias, dy1, ln2_gain, ln2_bias, proj, qkv_own, qkv_other, fc_own, fc_other, out
):
    first = coords_ref[3] == 0
    out_bias = jnp.sum(dy1[...].astype(F32), axis=0, keepdims=True)
    whole = [ln1_gain[...], ln1_bias[...], out_bias, ln2_gain[...], ln2_bias[...], proj[...]]
    fc = [jnp.where(first, fc_own[...], fc_other[...]), jnp.where(first, fc_other[...], fc_own[...])]
    qkv = [jnp.where(first, qkv_own[...], qkv_other[...]), jnp.where(first, qkv_other[...], qkv_own[...])]
    out[...] = jnp.zeros_like(out)
    for z in range(4):
        for y in range(2):
            blocks = [v[:, y * 512 + z * 128 : y * 512 + (z + 1) * 128] for v in whole]
            quad = qkv[z // 2][z % 2 : z % 2 + 1]
            for pair in range(2):
                at = pair * 3 * PAIR + y * 2 * PAIR
                blocks.append(quad[:, at : at + PAIR])
            for x in range(4):
                at = ((x * 4 + z) * 2 + y) * 64
                blocks.append(jnp.concatenate([v[:, at : at + 64] for v in fc], axis=1))
            rows = jnp.concatenate(blocks, axis=0).astype(BF16)
            for core in range(2):
                out[z, y, core * 16 : core * 16 + SMALL_ROWS] = rows


def pack(coords, sums):
    return small_kernel(pack_kernel, coords, sums, [jax.ShapeDtypeStruct((4, 2, 32, 128), BF16)])[0]


def chunks_kernel(coords_ref, own, up, down, up_later, down_later, *outs):
    for k in range(4):
        x = lax.rem(coords_ref[2] + k, 4)
        low, place = x < 2, lax.rem(x, 2)
        below = jnp.where(low, up_later[place], up[1, place]).astype(F32)
        above = jnp.where(low, down[1, place], down_later[place]).astype(F32)
        outs[k][...] = (own[x].astype(F32) + below + above).astype(BF16)


def y_kernel(coords_ref, *refs):
    parts, qkv, mine, send = refs[:4], refs[4], refs[5], refs[6]
    columns = parts[0].shape[2]
    for dy, out in enumerate((mine, send)):
        y = lax.rem(coords_ref[0] + dy, 2)
        out[:, 0:columns] = total([part[y] for part in parts]).astype(out.dtype)
        out[:, columns:] = total([qkv[i, y] for i in range(16)]).astype(out.dtype)


def core_kernel(coords_ref, mine, got, keep, send):
    rows = keep.shape[0]
    for core, out in enumerate((keep, send)):
        here = pl.ds(pl.multiple_of(lax.rem(coords_ref[3] + core, 2) * rows, rows), rows)
        out[...] = mine[here, :] + got[here, :].astype(F32)


def final_kernel(coords_ref, keep, got, qkv, out, fc, ln1_gain, ln1_bias, qv, out_bias, ln2_gain, ln2_bias, fc_bias, proj):
    first = coords_ref[3] == 0
    halves = [jnp.where(first, keep[...], got[...]), jnp.where(first, got[...], keep[...])]
    half_fc, half_out, small = FF // 2, D // 2, 128
    for core in range(2):
        out[:, core * half_out : (core + 1) * half_out] = halves[core][:, half_fc : half_fc + half_out]
        for pair in range(4):
            for part in range(3):
                at = half_fc + half_out + (pair * 3 + part) * PAIR
                to = part * D + (core * 4 + pair) * PAIR
                qkv[:, to : to + PAIR] = halves[core][:, at : at + PAIR]
    for y in range(2):
        for z in range(4):
            for x in range(4):
                at = ((x * 4 + z) * 2 + y) * 64
                to = ((y * 4 + z) * 4 + x) * 128
                fc[:, to : to + 128] = jnp.concatenate([v[:, at : at + 64] for v in halves], axis=1)
    at = half_fc + half_out + 3 * half_out
    rows = keep[:, at : at + small] + got[:, at : at + small]
    x, c = coords_ref[2], coords_ref[3]
    part = x * 2 + c
    number = lax.broadcasted_iota(jnp.int32, rows.shape, 0)

    def one(at, count, width):
        per_row = small // width
        row = at + part // per_row
        line = jnp.sum(jnp.where(number == row, rows, 0.0), axis=0, keepdims=True)
        lane = (part % per_row) * width
        line = pltpu.roll(jnp.broadcast_to(line, (8, small)), lax.rem(small - lane, small), 1)
        return line[0:1, 0:width]

    for i, ref in enumerate((ln1_gain, ln1_bias, out_bias, ln2_gain, ln2_bias, proj)):
        ref[...] = one(i, 1, 16)
    qv[...] = one(6, 2, 32)
    fc_bias[...] = one(8, 4, 64)


def to_sequence(values, core):
    micro, rows, width = values.shape
    cut = values.reshape(micro, 2, rows // 2, width)
    keep = lax.dynamic_index_in_dim(cut, core, 1)
    got = swap_cores(lax.dynamic_index_in_dim(cut, 1 - core, 1))
    each = in_order(core, keep, got, 1).reshape(2 * micro, rows // 2, width)
    return lax.all_to_all(each, Z, 0, 0, tiled=True).reshape(2 * rows, width)


def to_z_kernel(coords_ref, first, second, *outs):
    rows = outs[0].shape[1]
    for k in range(4):
        z = lax.rem(coords_ref[1] + k, 4)
        for i, values in enumerate((first, second)):
            outs[k][i] = values[pl.ds(pl.multiple_of(z * rows, rows), rows), :]


def to_rows_of_z(coords, first, second):
    shape = pltpu.HBM((2, first.shape[0] // 4, D), BF16)
    chunks = small_kernel(to_z_kernel, coords, [first, second], [shape] * 4)
    return [chunks[0]] + [shift(chunks[k], Z, k) for k in (1, 2, 3)]


def by_sequence_kernel(coords_ref, *refs):
    arrived, (keep, send, blocks) = refs[:4], refs[4:]
    for i in range(2):
        for k in range(4):
            blocks[i, lax.rem(coords_ref[1] + 4 - k, 4)] = arrived[k][i]
    for i in range(2):
        for micro in range(2):
            keep[i, micro] = blocks[i, micro * 2 + coords_ref[3]]
            send[i, micro] = blocks[i, micro * 2 + 1 - coords_ref[3]]


def rows_kernel(coords_ref, keep, got, acts, in_grads):
    rows = keep.shape[2]
    for core, ref in enumerate((keep, got)):
        here = pl.ds(pl.multiple_of(lax.rem(coords_ref[3] + core, 2) * rows, rows), rows)
        for micro in range(2):
            acts[micro, here, :] = ref[0, micro]
            in_grads[micro, here, :] = ref[1, micro].astype(F32)


def own_rows(coords, arrays):
    rows = arrays[0].shape[1]
    shape = (2, 2, rows, D)
    keep, send = pl.pallas_call(
        by_sequence_kernel,
        grid_spec=pltpu.PrefetchScalarGridSpec(
            num_scalar_prefetch=1,
            grid=(1,),
            in_specs=[all_of(a.shape) for a in arrays],
            out_specs=[all_of(shape)] * 2,
            scratch_shapes=[pltpu.VMEM((2, 4, rows, D), BF16)],
        ),
        out_shape=[jax.ShapeDtypeStruct(shape, BF16), pltpu.HBM(shape, BF16)],
        compiler_params=pltpu.CompilerParams(vmem_limit_bytes=VMEM_LIMIT),
        cost_estimate=FREE,
    )(coords, *arrays)
    outs = [pltpu.HBM((2, 2 * rows, D), t) for t in (BF16, F32)]
    return small_kernel(rows_kernel, coords, [keep, swap_cores(send)], outs)


def by_pair(values):
    lead = values.shape[:-1]
    return values.reshape(*lead, 3, PAIRS, PAIR).swapaxes(-2, -3).reshape(*lead, 3 * D)


def by_core(values):
    lead = values.shape[:-1]
    return jnp.moveaxis(values.reshape(*lead, 2, 4, 4, 2, 64), (-2, -3, -4, -5), (-5, -4, -3, -2)).reshape(*lead, FF)


def on_device(
    inputs,
    cotangent,
    block_order,
    ln1_gain,
    ln1_bias,
    qkv_weight,
    qv_bias,
    out_weight,
    out_bias,
    ln2_gain,
    ln2_bias,
    fc_weight,
    fc_bias,
    proj_weight,
    proj_bias,
):
    section = lax.axis_index("section")
    core = lax.axis_index(CORE)
    coords = jnp.stack([lax.axis_index(a) for a in (*CTX_FSDP, "section")]).astype(jnp.int32)
    first = section == 0
    micro, _, rows, _ = inputs.shape

    vectors = (ln1_gain, ln1_bias, qv_bias, out_bias, ln2_gain, ln2_bias, fc_bias, proj_bias)
    widths = [v.shape[-1] for v in vectors]
    starts = [sum(widths[:i]) for i in range(len(widths))]
    packed = jnp.concatenate([v.reshape(-1) for v in vectors])
    packed = jnp.pad(packed, (0, 16 * 128 - packed.shape[0])).reshape(16, 128)

    qkv_cut = by_pair(qkv_weight[0]).reshape(16, 2, 2, 768)
    out_cut = out_weight[0].reshape(16, 2, 2, 256)
    fc_cut = by_core(fc_weight[0]).reshape(16, 2, 2048)
    halves = [
        jnp.concatenate(
            [qkv_cut[:, i, 0], out_cut[:, i, 0], packed, fc_cut[:, i], qkv_cut[:, i, 1], out_cut[:, i, 1]],
            axis=1,
        )
        for i in range(2)
    ]
    mine = jnp.where(core == 0, halves[0], halves[1])
    other = jnp.where(core == 0, halves[1], halves[0])
    blob = in_order(core, mine, swap_cores(other), 0)
    proj_own = in_order(coords[0], proj_weight[0], shift(proj_weight[0], Y, 1), 0)
    proj_own = lax.all_gather(proj_own, Z, axis=0, tiled=True)
    ring_x = first_ring(both_y(blob[:, :3200]), X)
    ring_z = first_ring(both_y(blob[:, 3200:]), Z)
    tokens = to_sequence(jnp.concatenate([inputs[:, 0], cotangent[:, 0]], axis=-1), core)
    ring_x, ring_z, tokens = together(ring_x, ring_z, tokens)
    entry, given = tokens[:, :D], tokens[:, D:]
    pieces_x = second_ring(ring_x[..., :1152], Z)
    pieces_z = second_ring(ring_z, X)
    fc_halves = (ring_x[:2, ..., 1152:], ring_x[2:, ..., 1152:])
    (pieces_x, pieces_z), fc_halves, proj_own, entry = together((pieces_x, pieces_z), fc_halves, proj_own, entry)
    proj_own = lax.all_gather(proj_own, X, axis=0, tiled=True)
    cuts = ((0, 768, 0, 0), (768, 256, 1, 0))
    qkv_0, out_0, packed = assemble(coords, X, cuts + ((1024, 128, 2, 0),), pieces_x)
    qkv_1, out_1 = assemble(coords, Z, cuts, pieces_z)
    out_own = jnp.concatenate([out_0, out_1], axis=1)
    w = {
        "qkv": ((qkv_0, qkv_1), (swap_cores(qkv_0), swap_cores(qkv_1))),
        "out": (out_own, swap_cores(out_own)),
    }

    def late_weights():
        value = yield
        low, high = to_neighbours(fc_halves, Z)
        value, low, high = together(value, low, high)
        far = to_neighbours((low, high), Z)
        value = yield value
        value, low_late, high_late = together(value, *to_neighbours(fc_halves[::-1], Z))
        value = yield value
        pieces = [fc_halves, far, (low, low_late), (high_late, high)]
        value, pieces = together(value, pieces)
        (fc_own,) = assemble(coords, X, ((0, 2048, 0, 0),), pieces)
        w["fc"] = (fc_own, swap_cores(fc_own))
        w["proj"] = (proj_own, swap_cores(proj_own))
        yield value

    packed = packed.reshape(32, 2, 16, 128)[:, :, :2].reshape(64, 256)
    names = ("ln1_gain", "ln1_bias", "qv", "out_bias", "ln2_gain", "ln2_bias", "fc", "proj_bias")
    vector = {
        name: packed[:, start : start + width].reshape(1, -1).astype(F32)
        for name, start, width in zip(names, starts, widths)
    }
    qv, fc_vector = vector.pop("qv"), by_core(vector.pop("fc"))
    qkv_vector = by_pair(jnp.concatenate([qv[:, :D], jnp.zeros((1, D), F32), qv[:, D:]], axis=1))
    w.update(vector)
    w["qkv_bias"] = (half(qkv_vector, core, 1), half(qkv_vector, 1 - core, 1))
    w["fc_bias"] = (half(fc_vector, core, 1), half(fc_vector, 1 - core, 1))

    early = layer_forward(entry, w, block_order, coords, 0, None, late_weights())
    result = feed_down(early["middle"], early["act"], w)
    arriving = lax.ppermute(result, "section", [(0, 1)])
    heavy, result = together((w["fc"], w["proj"]), result)
    heavy = jax.tree.map(held, heavy)
    arriving, (w["fc"], w["proj"]) = together(arriving, heavy)
    entry = jnp.where(first, entry, arriving)
    saved = layer_forward(entry, w, block_order, coords, 1, early)

    d_entry, early = layer_backward(given, saved, w, block_order, coords, 1, None)
    arriving = lax.ppermute(d_entry, "section", [(1, 0)])
    middle, act_other, normed2, normed, attended, _ = together(
        saved["middle"], saved["act"][1], saved["normed2"], saved["normed"], saved["attended"], d_entry
    )
    swapped = [swap_cores(v) for v in (act_other, normed2, normed, attended)]
    result = feed_down(middle, saved["act"], w)
    arriving, result, saved["swapped"] = together(arriving, result, swapped)
    upstream = jnp.where(first, arriving, given)
    d_entry, g = layer_backward(upstream, saved, w, block_order, coords, 0, early)
    d_entry, proj_part = together(d_entry, g["proj"])
    proj_grad = sum_by_axes(proj_part, (Z,)).astype(F32)
    tokens = to_rows_of_z(coords, result, d_entry)
    parts = [streamed(v) for v in (*g["fc"], g["qkv"])]
    columns = parts[0].shape[2] + g["qkv"].shape[3]
    outs = [jax.ShapeDtypeStruct((32, columns), F32), pltpu.HBM((32, columns), BF16)]
    mine, send = small_kernel(y_kernel, coords, parts, outs)
    mine, tokens = together(mine, tokens)
    acts, in_grads = own_rows(coords, tokens)
    outs = [jax.ShapeDtypeStruct((16, columns), F32), pltpu.HBM((16, columns), F32)]
    keep, send = small_kernel(core_kernel, coords, [mine, shift(send, Y, 1)], outs)
    widths = (3 * D, D, FF, 16, 16, 32, 16, 16, 16, 64, 16)
    outs = [pltpu.HBM((16 if n >= D else 1, n), F32) for n in widths]
    qkv_grad, out_grad, fc_grad, *small = small_kernel(final_kernel, coords, [keep, swap_cores(send)], outs)
    shape = (1, micro, 1, rows, D)
    return (
        acts.reshape(shape),
        in_grads.reshape(shape),
        small[0],
        small[1],
        qkv_grad[None],
        small[2],
        out_grad[None],
        small[3],
        small[4],
        small[5],
        fc_grad[None],
        small[6],
        proj_grad[None],
        small[7],
    )


def solution(mesh):
    torus = Mesh(
        mesh.devices.reshape(mesh.shape["section"], 2, 4, 4, 2),
        ("section", "ctx_0", "ctx_1", "fsdp_0", "fsdp_1"),
    )
    tokens = P(None, FSDP, CTX, None)
    vector = P("section", CTX_FSDP)
    matrix = P("section", CTX_FSDP, None)
    kinds = (vector, vector, matrix, vector, matrix, vector, vector, vector, matrix, vector, matrix, vector)
    results = P("section", None, FSDP, CTX, None)
    return jax.shard_map(
        on_device,
        mesh=torus,
        in_specs=(tokens, tokens, P()) + kinds,
        out_specs=(results, results) + kinds,
        check_vma=False,
    )
```

```python
import functools

import jax
import jax.numpy as jnp
from jax import lax
from jax.experimental import pallas as pl
from jax.experimental.pallas import tpu as pltpu
from jax.sharding import Mesh
from jax.sharding import PartitionSpec as P

D = 1024
HEADS = 16
HEAD_DIM = 64
FF = 4096
PAIRS = 8
PAIR = 128
QUAD = 256
TILE = 256
BLOCK = 64
CTX = ("ctx_0", "ctx_1")
FSDP = ("fsdp_0", "fsdp_1")
CTX_FSDP = CTX + FSDP
Y, Z, X, CORE = CTX_FSDP
EPSILON = 1e-05
MASKED = -1e30
SCALE = HEAD_DIM**-0.5
BF16 = jnp.bfloat16
F32 = jnp.float32
VMEM_LIMIT = 24 * 2**20
SMALL_LIMIT = 16 * 2**20
FREE = pl.CostEstimate(flops=0, bytes_accessed=0, transcendentals=0)
SOME = pl.CostEstimate(flops=2 * 10**9, bytes_accessed=8 * 10**6, transcendentals=0)


def dot(left, right):
    return jnp.dot(left, right, preferred_element_type=F32)


def dot_rows(left, right):
    return lax.dot_general(left, right, (((0,), (0,)), ((), ())), preferred_element_type=F32)


def dot_back(left, right):
    return lax.dot_general(left, right, (((1,), (1,)), ((), ())), preferred_element_type=F32)


def shift(value, axis, by):
    n = lax.axis_size(axis)
    return lax.ppermute(value, axis, [(i, (i + by) % n) for i in range(n)])


def swap_cores(value):
    return shift(value, CORE, 1)


def swap_y(value, section):
    at = 2 * section
    return lax.ppermute(value, ("section", Y), [(at, at + 1), (at + 1, at)])


def half(value, which, dim):
    size = value.shape[dim] // 2
    return lax.dynamic_slice_in_dim(value, which * size, size, dim)


def in_order(which, mine, other, dim):
    return jnp.where(
        which == 0,
        jnp.concatenate([mine, other], axis=dim),
        jnp.concatenate([other, mine], axis=dim),
    )


def both_y(rows):
    return jnp.stack([rows, shift(rows, Y, 1)])


def first_ring(both, axis):
    return jnp.stack([both] + [shift(both, axis, k) for k in range(1, 4)])


def second_ring(ring, axis):
    return [ring] + [shift(ring, axis, k) for k in (2, 1, 3)]


def to_neighbours(halves, axis):
    return [shift(v, axis, by) for v, by in zip(halves, (1, -1))]


def assemble_kernel(first, cuts, count, coords_ref, *refs):
    outs = refs[4 * count :]
    pieces = [[refs[m * count + k * count // 4].at[k % (4 // count)] for k in range(4)] for m in range(4)]
    y, me = coords_ref[0], coords_ref[1] if first == Z else coords_ref[2]
    for m in range(4):

        @pl.when(pl.program_id(0) == m)
        def _():
            for k in range(4):
                place = lax.rem(me + 4 - k, 4)
                for dy in range(2):
                    at_y = lax.rem(y + dy, 2)
                    for start, width, out, row in cuts:
                        block = pieces[m][k][dy, :, start : start + width]
                        rows = pl.ds(row, block.shape[0])
                        if first == Z:
                            outs[out][at_y, place, 0, rows] = block
                        else:
                            outs[out][at_y, 0, place, rows] = block


def assemble(coords, first, cuts, pieces):
    pieces = [p if isinstance(p, (tuple, list)) else (p,) for p in pieces]
    count = len(pieces[0])
    one = pieces[0][0].shape
    rows = one[2]
    at = 2 if first == Z else 1
    shapes = {}
    for _, width, out, row in cuts:
        shapes[out] = (row + rows, width)
    shapes = [shapes[out] for out in range(len(shapes))]

    def place(m, coords):
        by = jnp.where(m == 1, 2, jnp.where(m == 2, 1, m))
        ring = lax.rem(coords[at] + 4 - by, 4)
        return (0, 0, ring, 0, 0) if first == Z else (0, ring, 0, 0, 0)

    along = (2, 4, 1) if first == Z else (2, 1, 4)
    whole = pl.BlockSpec(one, lambda m, coords: (0, 0, 0, 0))
    outs = pl.pallas_call(
        functools.partial(assemble_kernel, first, cuts, count),
        grid_spec=pltpu.PrefetchScalarGridSpec(
            num_scalar_prefetch=1,
            grid=(4,),
            in_specs=[whole] * (4 * count),
            out_specs=[pl.BlockSpec((*along, *shape), place) for shape in shapes],
        ),
        out_shape=[jax.ShapeDtypeStruct((2, 4, 4, *shape), BF16) for shape in shapes],
        compiler_params=pltpu.CompilerParams(vmem_limit_bytes=VMEM_LIMIT),
        cost_estimate=FREE,
    )(coords, *[streamed(part) for piece in pieces for part in piece])
    return [out.reshape(-1, out.shape[-1]) for out in outs]


def weight_grad_kernel(n_jobs, ring, coords_ref, *refs):
    jobs = [refs[4 * j : 4 * j + 4] for j in range(n_jobs)]
    extra = () if ring else (refs[4 * n_jobs],)
    outs, whole = refs[4 * n_jobs + len(extra) : -1], refs[-1]
    rows = whole.shape[2]
    at = 0
    for own_left, other_left, own_right, other_right in jobs:
        for own, other in zip(column_parts(own_right), column_parts(other_right)):
            grad = dot_rows(own_left[...], own()) + dot_rows(other_left[...], other())
            width = grad.shape[1]
            whole[:, :, :, pl.ds(at, width)] = grad.astype(BF16).reshape(4, 4, rows, width)
            at += width
    if not ring:
        for x in range(4):
            whole[:, x, :, pl.ds(at, 128)] = extra[0][:, 0]
        outs[0][:, :, 0] = whole[...]
        return
    own, up, down, up_later, down_later = outs
    part = [whole.at[lax.rem(coords_ref[1] + k, 4)] for k in range(4)]
    own[:, 0] = part[0][...]
    up[0, :, 0], up[1, :, 0] = part[2][0:2], part[1][2:4]
    down[0, :, 0], down[1, :, 0] = part[2][2:4], part[3][0:2]
    up_later[:, 0] = part[1][0:2]
    down_later[:, 0] = part[3][2:4]


def column_parts(ref):
    if len(ref.shape) == 4:
        return [lambda t=t: ref[0, t] for t in range(2)]
    return [lambda at=at: ref[:, pl.ds(at, 256)] for at in range(0, ref.shape[1], 256)]


def weight_grad(coords, ring, jobs, extra=None):
    rows = jobs[0][0].shape[1] // 32
    tokens = jobs[0][0].shape[0]
    columns = 0
    in_specs, arrays = [], []
    for *job, at, width in jobs:
        left = pl.BlockSpec((tokens, 16 * rows), lambda y, coords: (0, y))
        if job[2].ndim == 4:
            shape = (1, *job[2].shape[1:])
            right = pl.BlockSpec(shape, lambda y, coords, at=at: (lax.rem(coords[0] + at, 2), 0, 0, 0))
        elif at is None:
            right = pl.BlockSpec((tokens, width), lambda y, coords: (0, coords[3]))
        else:
            right = pl.BlockSpec((tokens, width), lambda y, coords, at=at: (0, at))
        columns += width
        in_specs += [left, left, right, right]
        arrays += [streamed(v) for v in job]
    if extra is not None:
        in_specs.append(pl.BlockSpec((4, 1, rows, 128), lambda y, coords: (0, y, 0, 0)))
        arrays.append(extra)
        columns += 128
    leads = [(4,), (2, 2), (2, 2), (2,), (2,)] if ring else [(4, 4)]

    def along_y(lead):
        return pl.BlockSpec((*lead, 1, rows, columns), lambda y, coords: (*(0,) * len(lead), y, 0, 0))

    return pl.pallas_call(
        functools.partial(weight_grad_kernel, len(jobs), ring),
        grid_spec=pltpu.PrefetchScalarGridSpec(
            num_scalar_prefetch=1,
            grid=(2,),
            in_specs=in_specs,
            out_specs=[along_y(lead) for lead in leads],
            scratch_shapes=[pltpu.VMEM((4, 4, rows, columns), BF16)],
        ),
        out_shape=[pltpu.HBM((*lead, 2, rows, columns), BF16) for lead in leads],
        compiler_params=pltpu.CompilerParams(vmem_limit_bytes=VMEM_LIMIT),
        cost_estimate=SOME if ring else FREE,
    )(coords, *arrays)


def plain_grad_kernel(own_left, other_left, own_right, other_right, out):
    grad = dot_rows(own_left[...], own_right[...])
    grad = (grad + dot_rows(other_left[...], other_right[...])).astype(BF16)
    for z in range(4):
        for y in range(2):
            out[(y * 4 + z) * 64 : (y * 4 + z + 1) * 64, :] = grad[(z * 2 + y) * 64 : (z * 2 + y + 1) * 64, :]


def plain_grad(own_left, other_left, own_right, other_right):
    tokens, rows = own_left.shape
    columns = own_right.shape[1]
    block = 512
    left = pl.BlockSpec((tokens, block), lambda i: (0, i))
    right = pl.BlockSpec((tokens, columns), lambda i: (0, 0))
    return pl.pallas_call(
        plain_grad_kernel,
        grid=(rows // block,),
        in_specs=[left, left, right, right],
        out_specs=pl.BlockSpec((block, columns), lambda i: (i, 0)),
        out_shape=pltpu.HBM((rows, columns), BF16),
        compiler_params=pltpu.CompilerParams(vmem_limit_bytes=VMEM_LIMIT),
        cost_estimate=SOME,
    )(*[streamed(v) for v in (own_left, other_left, own_right, other_right)])


def sum_by_axes(parts, axes):
    for axis in axes:
        parts = lax.psum_scatter(parts, axis, scatter_dimension=0, tiled=False)
    return parts


def total(parts):
    return functools.reduce(lambda a, b: a + b, [p.astype(F32) for p in parts])


def start_sum(parts, first):
    return [parts[0]] + [shift(parts[k], first, k) for k in (2, 1, 3)]


def relay_kernel(coords_ref, up, low, down, high, up_out, down_out):
    up_out[...] = total([up[...], low[0]]).astype(BF16)
    down_out[...] = total([down[...], high[0]]).astype(BF16)


def relay(coords, parts, low, high):
    shape = pltpu.HBM(parts[3].shape, BF16)
    up, down = small_kernel(relay_kernel, coords, [parts[3], low, parts[4], high], [shape] * 2)
    return shift(up, Z, 1), shift(down, Z, -1)


def layer_norm(values, gain, bias):
    average = jnp.mean(values, axis=-1, keepdims=True)
    centred = values - average
    spread_of = jnp.mean(centred * centred, axis=-1, keepdims=True)
    inverse = lax.rsqrt(spread_of + EPSILON)
    normal = centred * inverse
    return normal * gain + bias, normal, inverse


def norm_back(upstream, normal, inverse, gain):
    scaled = upstream * gain
    first = jnp.mean(scaled, axis=-1, keepdims=True)
    second = jnp.mean(scaled * normal, axis=-1, keepdims=True)
    return (
        inverse * (scaled - first - normal * second),
        jnp.sum(upstream * normal, axis=0),
        jnp.sum(upstream, axis=0),
    )


def head_lanes(shape, head):
    return lax.broadcasted_iota(jnp.int32, shape, 1) // HEAD_DIM == head


def causal(keys):
    rows = lax.broadcasted_iota(jnp.int32, (keys, TILE), 0)
    columns = lax.broadcasted_iota(jnp.int32, (keys, TILE), 1)
    return rows <= columns + (keys - TILE)


def stored_blocks(order_ref, coords_ref):
    y, c = coords_ref[0], coords_ref[3]
    for dy in range(2):
        for dc in range(2):
            for z in range(4):
                stored = lax.rem(y + dy, 2) * 8 + z * 2 + lax.rem(c + dc, 2)
                at = pl.multiple_of(order_ref[stored] * BLOCK, BLOCK)
                yield dy, dc, slice(z * BLOCK, (z + 1) * BLOCK), pl.ds(at, BLOCK)


def chosen(coords_ref, active, refs, index):
    if len(refs) == 1:
        return refs[0][index]
    return jnp.where(coords_ref[4] == active, refs[0][index], refs[1][index])


def attention_kernel(active, order_ref, coords_ref, own, got, *refs):
    far, (out_near, out_far, lse_ref, q, k, v, out) = refs[:-7], refs[-7:]
    for dy, dc, rows, place in stored_blocks(order_ref, coords_ref):
        if dy == 0:
            block = (own, got)[dc][0, 0, rows, :]
        else:
            block = chosen(coords_ref, active, far, (dc, rows, slice(None)))
        q[place, :] = block[:, 0:PAIR]
        k[place, :] = block[:, PAIR : 2 * PAIR] * SCALE
        v[place, :] = block[:, 2 * PAIR :]
    length = q.shape[0]
    lse_ref[...] = jnp.zeros_like(lse_ref)
    for tile in range(length // TILE):
        keys = (tile + 1) * TILE
        here = pl.ds(tile * TILE, TILE)
        outs = []
        for head in range(2):
            queries = q[here, :]
            queries = jnp.where(head_lanes(queries.shape, head), queries, jnp.zeros_like(queries))
            scores = dot_back(k[0:keys, :], queries)
            scores = jnp.where(causal(keys), scores, MASKED)
            highest = jnp.max(scores, axis=0, keepdims=True)
            probs = jnp.exp(scores - highest)
            total_of = jnp.sum(probs, axis=0, keepdims=True)
            lse_ref[head : head + 1, here] = highest + jnp.log(total_of)
            attended = dot_rows(v[0:keys, :], probs.astype(BF16)) / total_of
            outs.append(attended[head * HEAD_DIM : (head + 1) * HEAD_DIM, :])
        out[here, :] = jnp.concatenate(outs, axis=0).T.astype(BF16)
    for dy, dc, rows, place in stored_blocks(order_ref, coords_ref):
        (out_near, out_far)[dy][dc, rows, :] = out[place, :]


def attention_back_kernel(actives, n_far, n_grad, order_ref, coords_ref, *refs):
    own, got = refs[:2]
    far = refs[2 : 2 + n_far]
    grad_own, grad_got = refs[2 + n_far : 4 + n_far]
    grad_far = refs[4 + n_far : 4 + n_far + n_grad]
    lse_ref, out_near, out_far, q, k, v, g, dq, dk, dv = refs[4 + n_far + n_grad :]
    for dy, dc, rows, place in stored_blocks(order_ref, coords_ref):
        if dy == 0:
            block = (own, got)[dc][0, 0, rows, :]
            grads = (grad_own, grad_got)[dc][0, 0, rows, :]
        else:
            block = chosen(coords_ref, actives[0], far, (dc, rows, slice(None)))
            grads = chosen(coords_ref, actives[1], grad_far, (dc, rows, slice(None)))
        q[place, :] = block[:, 0:PAIR]
        k[place, :] = block[:, PAIR : 2 * PAIR] * SCALE
        v[place, :] = block[:, 2 * PAIR :]
        g[place, :] = grads
    length = q.shape[0]
    dk[...] = jnp.zeros_like(dk)
    dv[...] = jnp.zeros_like(dv)
    for tile in range(length // TILE):
        keys = (tile + 1) * TILE
        here = pl.ds(tile * TILE, TILE)
        outs = []
        for head in range(2):
            lanes = head_lanes((TILE, PAIR), head)
            queries = q[here, :]
            queries = jnp.where(lanes, queries, jnp.zeros_like(queries))
            grads = g[here, :]
            grads = jnp.where(lanes, grads, jnp.zeros_like(grads))
            scores = dot_back(k[0:keys, :], queries)
            probs = jnp.exp(scores - lse_ref[head : head + 1, here])
            probs = jnp.where(causal(keys), probs, 0.0)
            grad_probs = dot_back(v[0:keys, :], grads)
            term = jnp.sum(probs * grad_probs, axis=0, keepdims=True)
            grad_scores = (probs * (grad_probs - term)).astype(BF16)
            dv[0:keys, :] += dot(probs.astype(BF16), grads)
            dk[0:keys, :] += dot(grad_scores, queries)
            grad_q = dot_rows(k[0:keys, :], grad_scores)
            outs.append(grad_q[head * HEAD_DIM : (head + 1) * HEAD_DIM, :])
        dq[here, :] = jnp.concatenate(outs, axis=0).T
    for dy, dc, rows, place in stored_blocks(order_ref, coords_ref):
        ref = (out_near, out_far)[dy]
        ref[dc, rows, 0:PAIR] = dq[place, :].astype(BF16)
        ref[dc, rows, PAIR : 2 * PAIR] = (dk[place, :] * SCALE).astype(BF16)
        ref[dc, rows, 2 * PAIR :] = dv[place, :].astype(BF16)


def own_pair(tokens, width, pair):
    return pl.BlockSpec((1, 1, tokens, width), lambda i, order, coords: (0, pair, 0, 0))


def all_of(shape):
    return pl.BlockSpec(shape, lambda i, *scalars: (0,) * len(shape))


def attention(order, coords, own, got, far, active, pair):
    tokens = far[0].shape[1]
    length = 4 * tokens
    out = (2, tokens, PAIR)
    return pl.pallas_call(
        functools.partial(attention_kernel, active),
        grid_spec=pltpu.PrefetchScalarGridSpec(
            num_scalar_prefetch=2,
            grid=(1,),
            in_specs=[own_pair(tokens, 3 * PAIR, pair)] * 2 + [all_of(f.shape) for f in far],
            out_specs=[all_of(out)] * 2 + [all_of((8, length))],
            scratch_shapes=[pltpu.VMEM((length, PAIR), BF16)] * 4,
        ),
        out_shape=[jax.ShapeDtypeStruct(out, BF16)] * 2 + [jax.ShapeDtypeStruct((8, length), F32)],
        compiler_params=pltpu.CompilerParams(vmem_limit_bytes=SMALL_LIMIT),
        cost_estimate=FREE,
    )(order, coords, own, got, *far)


def attention_back(order, coords, own, got, far, grad_own, grad_got, grad_far, lse, actives, pair):
    tokens = far[0].shape[1]
    length = 4 * tokens
    out = (2, tokens, 3 * PAIR)
    return pl.pallas_call(
        functools.partial(attention_back_kernel, actives, len(far), len(grad_far)),
        grid_spec=pltpu.PrefetchScalarGridSpec(
            num_scalar_prefetch=2,
            grid=(1,),
            in_specs=[own_pair(tokens, 3 * PAIR, pair)] * 2
            + [all_of(f.shape) for f in far]
            + [own_pair(tokens, PAIR, pair)] * 2
            + [all_of(f.shape) for f in grad_far]
            + [all_of(lse.shape)],
            out_specs=[all_of(out)] * 2,
            scratch_shapes=[pltpu.VMEM((length, PAIR), BF16)] * 4
            + [pltpu.VMEM((length, PAIR), F32)] * 3,
        ),
        out_shape=[jax.ShapeDtypeStruct(out, BF16)] * 2,
        compiler_params=pltpu.CompilerParams(vmem_limit_bytes=SMALL_LIMIT),
        cost_estimate=FREE,
    )(order, coords, own, got, *far, grad_own, grad_got, *grad_far, lse)


def small_kernel(kernel, coords, arrays, out_shape):
    return pl.pallas_call(
        kernel,
        grid_spec=pltpu.PrefetchScalarGridSpec(
            num_scalar_prefetch=1,
            grid=(1,),
            in_specs=[all_of(a.shape) for a in arrays],
            out_specs=[all_of(o.shape) for o in out_shape],
        ),
        out_shape=out_shape,
        compiler_params=pltpu.CompilerParams(vmem_limit_bytes=SMALL_LIMIT),
        cost_estimate=FREE,
    )(coords, *arrays)


def leaving_kernel(coords_ref, mine, got, *outs):
    for pair in range(2):
        outs[pair][0] = mine[1, pair]
        outs[pair][1] = got[1, pair]


def collect_kernel(active, coords_ref, *refs):
    near, new, old, (mine, send) = refs[:2], refs[2:4], refs[4:-2], refs[-2:]
    for pair in range(2):
        here = (new[pair], old[pair]) if old else (new[pair],)
        for dc, out in enumerate((mine, send)):
            out[0, pair] = near[pair][dc]
            out[1, pair] = chosen(coords_ref, active, here, dc)


def streamed(value):
    return pltpu.with_memory_space_constraint(value, pltpu.HBM)


K_STEPS = 2
K_BLOCK = D // K_STEPS


def qkv_kernel(coords_ref, entry, gain, bias, *refs):
    weights, biases, outs, normed_out, blocks, acc = refs[:4], refs[4:8], refs[8:10], refs[10], refs[11], refs[12]
    step = pl.program_id(0)

    @pl.when(step == 0)
    def _():
        normed = layer_norm(entry[...].astype(F32), gain[...], bias[...])[0].astype(BF16)
        normed_out[...] = normed
        for b in range(K_STEPS):
            blocks[b] = normed[:, b * K_BLOCK : (b + 1) * K_BLOCK]
        acc[...] = jnp.zeros_like(acc)

    for quad in range(4):
        acc[quad] += dot(blocks[step], weights[quad][...])

    @pl.when(step == K_STEPS - 1)
    def _():
        for quad in range(4):
            core, y = quad // 2, quad % 2
            value = (acc[quad] + biases[quad][...]).astype(BF16)
            for pair in range(2):
                outs[core][lax.rem(coords_ref[0] + y, 2), pair] = value[:, pair * 3 * PAIR : (pair + 1) * 3 * PAIR]


def qkv_forward(coords, entry, w):
    tokens = entry.shape[0]
    weights = [streamed(w["qkv"][i][j]) for i in range(2) for j in range(2)]
    biases = [w["qkv_bias"][i][:, j * 768 : (j + 1) * 768] for i in range(2) for j in range(2)]
    wide, row = all_of((tokens, D)), all_of((1, D))
    heads = (2, 2, tokens, 3 * PAIR)
    return pl.pallas_call(
        qkv_kernel,
        grid_spec=pltpu.PrefetchScalarGridSpec(
            num_scalar_prefetch=1,
            grid=(K_STEPS,),
            in_specs=[wide, row, row]
            + [pl.BlockSpec((K_BLOCK, 768), lambda j, coords: (j, 0))] * 4
            + [all_of((1, 768))] * 4,
            out_specs=[all_of(heads)] * 2 + [wide],
            scratch_shapes=[pltpu.VMEM((K_STEPS, tokens, K_BLOCK), BF16), pltpu.VMEM((4, tokens, 768), F32)],
        ),
        out_shape=[jax.ShapeDtypeStruct(heads, BF16), pltpu.HBM(heads, BF16), pltpu.HBM((tokens, D), BF16)],
        compiler_params=pltpu.CompilerParams(vmem_limit_bytes=VMEM_LIMIT),
        cost_estimate=FREE,
    )(coords, entry, w["ln1_gain"], w["ln1_bias"], *weights, *biases)


def qkv_back_kernel(coords_ref, mine, other, entry, gain, d_mid, *refs):
    weights, d_entry, ln_gain, ln_bias, sums, blocks = refs[:4], refs[4], refs[5], refs[6], refs[7:9], refs[9]
    step = pl.program_id(0)
    grad = jnp.zeros(blocks.shape[1:], F32)
    for quad in range(4):
        ref = (mine, other)[quad // 2]
        rel = lax.rem(coords_ref[0] + quad % 2, 2)
        for pair in range(2):
            columns = slice(pair * 3 * PAIR, (pair + 1) * 3 * PAIR)
            grad += dot_back(ref[rel, pair], weights[quad][:, columns])
    blocks[step] = grad

    @pl.when(step == K_STEPS - 1)
    def _():
        for quad in range(4):
            ref = (mine, other)[quad // 2]
            rel = lax.rem(coords_ref[0] + quad % 2, 2)
            for pair in range(2):
                columns = slice(pair * 3 * PAIR, (pair + 1) * 3 * PAIR)
                values = ref[rel, pair].astype(F32)
                sums[quad // 2][quad % 2 : quad % 2 + 1, columns] = jnp.sum(values, axis=0, keepdims=True)
        whole = jnp.concatenate([blocks[b] for b in range(K_STEPS)], axis=1)
        _, normal, inverse = layer_norm(entry[...].astype(F32), gain[...], 0.0)
        through, d_gain, d_bias = norm_back(whole, normal, inverse, gain[...])
        ln_gain[...] = d_gain.reshape(1, D)
        ln_bias[...] = d_bias.reshape(1, D)
        d_entry[...] = (d_mid[...] + through).astype(BF16)


def qkv_back(coords, mine, other, entry, d_mid, w):
    tokens = entry.shape[0]
    weights = [streamed(w["qkv"][i][j]) for i in range(2) for j in range(2)]
    wide, row = all_of((tokens, D)), all_of((1, D))
    line = jax.ShapeDtypeStruct((1, D), F32)
    return pl.pallas_call(
        qkv_back_kernel,
        grid_spec=pltpu.PrefetchScalarGridSpec(
            num_scalar_prefetch=1,
            grid=(K_STEPS,),
            in_specs=[all_of(mine.shape)] * 2
            + [wide, row, wide]
            + [pl.BlockSpec((K_BLOCK, 768), lambda j, coords: (j, 0))] * 4,
            out_specs=[wide, row, row] + [all_of((2, 768))] * 2,
            scratch_shapes=[pltpu.VMEM((K_STEPS, tokens, K_BLOCK), F32)],
        ),
        out_shape=[jax.ShapeDtypeStruct((tokens, D), BF16), line, line]
        + [jax.ShapeDtypeStruct((2, 768), F32)] * 2,
        compiler_params=pltpu.CompilerParams(vmem_limit_bytes=VMEM_LIMIT),
        cost_estimate=FREE,
    )(coords, mine, other, entry, w["ln1_gain"], d_mid, *weights)


def head_columns(coords_ref, core, y, pair):
    quad = lax.rem(coords_ref[3] + core, 2) * 2 + lax.rem(coords_ref[0] + y, 2)
    return pl.multiple_of((quad * 2 + pair) * PAIR, PAIR)


def half_columns(coords_ref, core):
    return pl.ds(pl.multiple_of(lax.rem(coords_ref[3] + core, 2) * (D // 2), D // 2), D // 2)


def out_kernel(coords_ref, entry, mine, other, own_weight, other_weight, bias, mid, att):
    for core, ref in enumerate((mine, other)):
        for y in range(2):
            for pair in range(2):
                att[:, pl.ds(head_columns(coords_ref, core, y, pair), PAIR)] = ref[y, pair]
    for core, weight in enumerate((own_weight, other_weight)):
        columns = half_columns(coords_ref, core)
        mid[:, columns] = entry[:, columns].astype(F32) + (dot(att[...], weight[...]) + bias[:, columns])


def out_forward(coords, entry, mine, other, w):
    shape = entry.shape
    arrays = [entry, mine, other, *w["out"], w["out_bias"]]
    return small_kernel(out_kernel, coords, arrays, [jax.ShapeDtypeStruct(shape, F32), pltpu.HBM(shape, BF16)])


FF_BLOCK = 1024
FF_STEPS = FF // FF_BLOCK
CURVE = 0.044715
ROOT = (2.0 / jnp.pi) ** 0.5


def feed_up_kernel(first, *refs):
    if first:
        mid, gain, bias, fc, fc_bias, normed, act, slope = refs

        @pl.when(pl.program_id(0) == 0)
        def _():
            normed[...] = layer_norm(mid[...], gain[...], bias[...])[0].astype(BF16)
    else:
        normed, fc, fc_bias, act, slope = refs
    before = dot(normed[...], fc[...]) + fc_bias[...]
    square = before * before
    bent = jnp.tanh(ROOT * before * (1.0 + CURVE * square))
    act[...] = (0.5 * before * (1.0 + bent)).astype(BF16)
    slope[...] = (
        0.5 * (1.0 + bent) + 0.5 * ROOT * before * (1.0 - bent * bent) * (1.0 + 3.0 * CURVE * square)
    ).astype(BF16)


def feed_up_half(first, given, fc, fc_bias):
    tokens = given[0].shape[0]
    row, wide = all_of((1, D)), all_of((tokens, D))
    along = lambda rows: pl.BlockSpec((rows, FF_BLOCK), lambda j: (0, j))
    outs = [(wide, jax.ShapeDtypeStruct((tokens, D), BF16))] if first else []
    outs += [(along(tokens), jax.ShapeDtypeStruct((tokens, FF // 2), BF16))] * 2
    return pl.pallas_call(
        functools.partial(feed_up_kernel, first),
        grid=(FF_STEPS // 2,),
        in_specs=([wide, row, row] if first else [wide]) + [along(D), along(1)],
        out_specs=[spec for spec, _ in outs],
        out_shape=[shape for _, shape in outs],
        compiler_params=pltpu.CompilerParams(vmem_limit_bytes=VMEM_LIMIT),
        cost_estimate=FREE,
    )(*given, fc, fc_bias)


def feed_up(middle, w):
    given = (middle, w["ln2_gain"], w["ln2_bias"])
    normed, act_own, slope_own = feed_up_half(True, given, w["fc"][0], w["fc_bias"][0])
    act_other, slope_other = feed_up_half(False, (normed,), w["fc"][1], w["fc_bias"][1])
    return normed, (act_own, act_other), (slope_own, slope_other)


def copy_kernel(value, out):
    out[...] = value[...]


def held(value):
    rows, columns = value.shape
    block = pl.BlockSpec((rows // 4, columns), lambda i: (i, 0))
    return pl.pallas_call(
        copy_kernel,
        grid=(4,),
        in_specs=[block],
        out_specs=block,
        out_shape=pltpu.VMEM(value.shape, BF16),
        compiler_params=pltpu.CompilerParams(vmem_limit_bytes=8 * 2**20),
        cost_estimate=FREE,
    )(value)


def ff_at(i):
    count = FF_STEPS // 2
    return (lambda j: jnp.minimum(j, count - 1)) if i == 0 else (lambda j: jnp.maximum(j - count, 0))


def ff_specs(rows, axis):
    def one(i):
        at = ff_at(i)
        if axis == 1:
            return pl.BlockSpec((rows, FF_BLOCK), lambda j, *scalars: (0, at(j)))
        return pl.BlockSpec((FF_BLOCK, rows), lambda j, *scalars: (at(j), 0))

    return [one(0), one(1)]


def feed_down_kernel(mid, bias, act_own, act_other, proj_own, proj_other, result, acc):
    step = pl.program_id(0)

    @pl.when(step == 0)
    def _():
        acc[...] = mid[...] + bias[...]

    for i, (act, proj) in enumerate(((act_own, proj_own), (act_other, proj_other))):

        @pl.when(step // (FF_STEPS // 2) == i)
        def _():
            acc[...] += dot(act[...], proj[...])

    @pl.when(step == FF_STEPS - 1)
    def _():
        result[...] = acc[...].astype(BF16)


def feed_down(middle, act, w):
    tokens = middle.shape[0]
    wide = all_of((tokens, D))
    return pl.pallas_call(
        feed_down_kernel,
        grid=(FF_STEPS,),
        in_specs=[wide, all_of((1, D))] + ff_specs(tokens, 1) + ff_specs(D, 0),
        out_specs=wide,
        out_shape=jax.ShapeDtypeStruct((tokens, D), BF16),
        scratch_shapes=[pltpu.VMEM((tokens, D), F32)],
        compiler_params=pltpu.CompilerParams(vmem_limit_bytes=VMEM_LIMIT),
        cost_estimate=FREE,
    )(middle, w["proj_bias"], *act, *w["proj"])


def feed_back_kernel(coords_ref, *refs):
    upstream, mid, gain, fc, proj, slope, out_weights = refs[0], refs[1], refs[2], refs[3:5], refs[5:7], refs[7:9], refs[9:11]
    refs = refs[11:]
    d_mid, dy1, d_pre, fc_sum, ln_gain, ln_bias, proj_sum, heads, acc = (
        refs[0],
        refs[1],
        refs[2:4],
        refs[4:6],
        refs[6],
        refs[7],
        refs[8],
        refs[9:11],
        refs[11],
    )
    step = pl.program_id(0)

    @pl.when(step == 0)
    def _():
        acc[...] = jnp.zeros_like(acc)
        proj_sum[...] = jnp.sum(upstream[...].astype(F32), axis=0, keepdims=True)

    for i in range(2):

        @pl.when(step // (FF_STEPS // 2) == i)
        def _():
            grad = (slope[i][...].astype(F32) * dot_back(upstream[...], proj[i][...])).astype(BF16)
            d_pre[i][...] = grad
            fc_sum[i][...] = jnp.sum(grad.astype(F32), axis=0, keepdims=True)
            acc[...] += dot_back(grad, fc[i][...])

    @pl.when(step == FF_STEPS - 1)
    def _():
        _, normal, inverse = layer_norm(mid[...], gain[...], 0.0)
        through, d_gain, d_bias = norm_back(acc[...], normal, inverse, gain[...])
        ln_gain[...] = d_gain.reshape(1, D)
        ln_bias[...] = d_bias.reshape(1, D)
        d_mid[...] = upstream[...].astype(F32) + through
        dy1[...] = d_mid[...].astype(BF16)
        grads = [dy1[:, half_columns(coords_ref, core)] for core in range(2)]
        for core in range(2):
            for y in range(2):
                for pair in range(2):
                    rows = pl.ds(head_columns(coords_ref, core, y, pair), PAIR)
                    value = dot_back(grads[0], out_weights[0][rows, :]) + dot_back(grads[1], out_weights[1][rows, :])
                    heads[core][y, pair] = value.astype(BF16)


def feed_back(coords, upstream, middle, slope, w):
    tokens = upstream.shape[0]
    row, wide = all_of((1, D)), all_of((tokens, D))
    line = jax.ShapeDtypeStruct((1, D), F32)
    heads = (2, 2, tokens, PAIR)
    return pl.pallas_call(
        feed_back_kernel,
        grid_spec=pltpu.PrefetchScalarGridSpec(
            num_scalar_prefetch=1,
            grid=(FF_STEPS,),
            in_specs=[wide, wide, row]
            + ff_specs(D, 1)
            + ff_specs(D, 0)
            + ff_specs(tokens, 1)
            + [all_of((D, D // 2))] * 2,
            out_specs=[wide, wide] + ff_specs(tokens, 1) + ff_specs(1, 1) + [row] * 3 + [all_of(heads)] * 2,
            scratch_shapes=[pltpu.VMEM((tokens, D), F32)],
        ),
        out_shape=[
            pltpu.HBM((tokens, D), F32),
            pltpu.HBM((tokens, D), BF16),
            *[pltpu.HBM((tokens, FF // 2), BF16)] * 2,
            *[jax.ShapeDtypeStruct((1, FF // 2), F32)] * 2,
            line,
            line,
            line,
            *[jax.ShapeDtypeStruct(heads, BF16)] * 2,
        ],
        compiler_params=pltpu.CompilerParams(vmem_limit_bytes=VMEM_LIMIT),
        cost_estimate=FREE,
    )(coords, upstream, middle, w["ln2_gain"], *w["fc"], *w["proj"], *slope, *w["out"])


def together(first, *others):
    return lax.optimization_barrier((first, *others))


def to_heads(coords, mine, other, active):
    got = swap_cores(other)
    shape = pltpu.HBM((2, *mine.shape[2:]), BF16)
    return got, [swap_y(v, active) for v in small_kernel(leaving_kernel, coords, [mine, got], [shape] * 2)]


def to_tokens(coords, near, back, old, active):
    shape = (2, *near[0].shape)
    outs = [jax.ShapeDtypeStruct(shape, BF16), pltpu.HBM(shape, BF16)]
    mine, send = small_kernel(functools.partial(collect_kernel, active), coords, [*near, *back, *old], outs)
    return mine, swap_cores(send)


def layer_forward(entry, w, order, coords, active, old, late=None):
    mine, other, normed = qkv_forward(coords, entry, w)
    if late is not None:
        next(late)
        other = late.send(other)
    got, far = to_heads(coords, mine, other, active)
    if late is not None:
        far[1] = late.send(far[1])
    far = [(v, old["far"][pair][0]) if old else (v,) for pair, v in enumerate(far)]
    near, back, lse = [], [], []
    for pair in range(2):
        heads, heads_far, pair_lse = attention(order, coords, mine, got, far[pair], active, pair)
        near.append(heads)
        back.append(swap_y(heads_far, active))
        lse.append(pair_lse)
    middle, attended = out_forward(
        coords, entry, *to_tokens(coords, near, back, old["back"] if old else [], active), w
    )
    if late is not None:
        middle = late.send(middle)
    normed2, act, slope = feed_up(middle, w)
    return dict(
        entry=entry,
        normed=normed,
        qkv=(mine, got),
        far=far,
        back=back,
        lse=lse,
        attended=attended,
        middle=middle,
        normed2=normed2,
        act=act,
        slope=slope,
    )


def layer_backward(upstream, s, w, order, coords, active, old):
    g = {}
    last = old is not None
    d_mid, dy1, d_pre_own, d_pre_other, *sums, mine, other = feed_back(
        coords, upstream, s["middle"], s["slope"], w
    )
    got, far = to_heads(coords, mine, other, active)
    if last:
        jobs = [
            (s["normed2"], s["swapped"][1], d_pre_own, swap_cores(d_pre_other), 0, FF // 2),
            (s["attended"], s["swapped"][3], dy1, swap_cores(dy1), None, D // 2),
        ]
        grad = plain_grad(s["act"][0], s["swapped"][0], upstream, swap_cores(upstream))
        far[0], far[1], parts, grad = together(far[0], far[1], weight_grad(coords, True, jobs), grad)
        arrived = [shift(parts[1], Z, 1), shift(parts[2], Z, -1)]
        proj_part = sum_by_axes(grad.reshape(4, 2, 4, -1, D), (X,))
    far = [(v, old["far"][pair][0]) if old else (v,) for pair, v in enumerate(far)]
    near, back = [], []
    for pair in range(2):
        args = (*s["qkv"], s["far"][pair], mine, got, far[pair], s["lse"][pair], (1, active), pair)
        own, heads_far = attention_back(order, coords, *args)
        near.append(own)
        back.append(swap_y(heads_far, active))
    if last:
        back[1], arrived = together(back[1], arrived)
        later = relay(coords, parts, *arrived)
    d_mine, d_other = to_tokens(coords, near, back, old["back"] if old else [], active)
    d_entry, ln1_gain, ln1_bias, *qkv_sums = qkv_back(coords, d_mine, d_other, s["entry"], d_mid, w)
    if last:
        small = pack(coords, [ln1_gain, ln1_bias, dy1, *sums[2:5], *qkv_sums, *sums[0:2]])
        lefts = (s["normed"], s["swapped"][2])
        other = swap_cores(d_other)
        (qkv_part,) = weight_grad(coords, False, [(*lefts, d_mine, other, i, 768) for i in range(2)], small)
        d_entry, qkv_part, proj_part, later = together(d_entry, qkv_part, proj_part, later)
        g["qkv"] = lax.all_to_all(qkv_part.reshape(16, *qkv_part.shape[2:]), (Z, X), 0, 0, tiled=True)
        g["proj"] = sum_by_axes(proj_part, (Y,))
        shape = pltpu.HBM((2, *parts[0].shape[2:]), BF16)
        chunks = small_kernel(chunks_kernel, coords, [parts[0], *arrived, *later], [shape] * 4)
        g["fc"] = [chunks[0]] + [shift(chunks[k], X, k) for k in (1, 2, 3)]
    g.update(far=far, back=back)
    return d_entry, g


SMALL_ROWS = 12


def pack_kernel(
    coords_ref, ln1_gain, ln1_bias, dy1, ln2_gain, ln2_bias, proj, qkv_own, qkv_other, fc_own, fc_other, out
):
    first = coords_ref[3] == 0
    out_bias = jnp.sum(dy1[...].astype(F32), axis=0, keepdims=True)
    whole = [ln1_gain[...], ln1_bias[...], out_bias, ln2_gain[...], ln2_bias[...], proj[...]]
    fc = [jnp.where(first, fc_own[...], fc_other[...]), jnp.where(first, fc_other[...], fc_own[...])]
    qkv = [jnp.where(first, qkv_own[...], qkv_other[...]), jnp.where(first, qkv_other[...], qkv_own[...])]
    out[...] = jnp.zeros_like(out)
    for z in range(4):
        for y in range(2):
            blocks = [v[:, y * 512 + z * 128 : y * 512 + (z + 1) * 128] for v in whole]
            quad = qkv[z // 2][z % 2 : z % 2 + 1]
            for pair in range(2):
                at = pair * 3 * PAIR + y * 2 * PAIR
                blocks.append(quad[:, at : at + PAIR])
            for x in range(4):
                at = ((x * 4 + z) * 2 + y) * 64
                blocks.append(jnp.concatenate([v[:, at : at + 64] for v in fc], axis=1))
            rows = jnp.concatenate(blocks, axis=0).astype(BF16)
            for core in range(2):
                out[z, y, core * 16 : core * 16 + SMALL_ROWS] = rows


def pack(coords, sums):
    return small_kernel(pack_kernel, coords, sums, [jax.ShapeDtypeStruct((4, 2, 32, 128), BF16)])[0]


def chunks_kernel(coords_ref, own, up, down, up_later, down_later, *outs):
    for k in range(4):
        x = lax.rem(coords_ref[2] + k, 4)
        low, place = x < 2, lax.rem(x, 2)
        below = jnp.where(low, up_later[place], up[1, place]).astype(F32)
        above = jnp.where(low, down[1, place], down_later[place]).astype(F32)
        outs[k][...] = (own[x].astype(F32) + below + above).astype(BF16)


def y_kernel(coords_ref, *refs):
    parts, qkv, mine, send = refs[:4], refs[4], refs[5], refs[6]
    columns = parts[0].shape[2]
    for dy, out in enumerate((mine, send)):
        y = lax.rem(coords_ref[0] + dy, 2)
        out[:, 0:columns] = total([part[y] for part in parts]).astype(out.dtype)
        out[:, columns:] = total([qkv[i, y] for i in range(16)]).astype(out.dtype)


def core_kernel(coords_ref, mine, got, keep, send):
    rows = keep.shape[0]
    for core, out in enumerate((keep, send)):
        here = pl.ds(pl.multiple_of(lax.rem(coords_ref[3] + core, 2) * rows, rows), rows)
        out[...] = mine[here, :] + got[here, :].astype(F32)


def final_kernel(coords_ref, keep, got, qkv, out, fc, ln1_gain, ln1_bias, qv, out_bias, ln2_gain, ln2_bias, fc_bias, proj):
    first = coords_ref[3] == 0
    halves = [jnp.where(first, keep[...], got[...]), jnp.where(first, got[...], keep[...])]
    half_fc, half_out, small = FF // 2, D // 2, 128
    for core in range(2):
        out[:, core * half_out : (core + 1) * half_out] = halves[core][:, half_fc : half_fc + half_out]
        for pair in range(4):
            for part in range(3):
                at = half_fc + half_out + (pair * 3 + part) * PAIR
                to = part * D + (core * 4 + pair) * PAIR
                qkv[:, to : to + PAIR] = halves[core][:, at : at + PAIR]
    for y in range(2):
        for z in range(4):
            for x in range(4):
                at = ((x * 4 + z) * 2 + y) * 64
                to = ((y * 4 + z) * 4 + x) * 128
                fc[:, to : to + 128] = jnp.concatenate([v[:, at : at + 64] for v in halves], axis=1)
    at = half_fc + half_out + 3 * half_out
    rows = keep[:, at : at + small] + got[:, at : at + small]
    x, c = coords_ref[2], coords_ref[3]
    part = x * 2 + c
    number = lax.broadcasted_iota(jnp.int32, rows.shape, 0)

    def one(at, count, width):
        per_row = small // width
        row = at + part // per_row
        line = jnp.sum(jnp.where(number == row, rows, 0.0), axis=0, keepdims=True)
        lane = (part % per_row) * width
        line = pltpu.roll(jnp.broadcast_to(line, (8, small)), lax.rem(small - lane, small), 1)
        return line[0:1, 0:width]

    for i, ref in enumerate((ln1_gain, ln1_bias, out_bias, ln2_gain, ln2_bias, proj)):
        ref[...] = one(i, 1, 16)
    qv[...] = one(6, 2, 32)
    fc_bias[...] = one(8, 4, 64)


def to_sequence(values, core):
    micro, rows, width = values.shape
    cut = values.reshape(micro, 2, rows // 2, width)
    keep = lax.dynamic_index_in_dim(cut, core, 1)
    got = swap_cores(lax.dynamic_index_in_dim(cut, 1 - core, 1))
    each = in_order(core, keep, got, 1).reshape(2 * micro, rows // 2, width)
    return lax.all_to_all(each, Z, 0, 0, tiled=True).reshape(2 * rows, width)


def to_z_kernel(coords_ref, first, second, *outs):
    rows = outs[0].shape[1]
    for k in range(4):
        z = lax.rem(coords_ref[1] + k, 4)
        for i, values in enumerate((first, second)):
            outs[k][i] = values[pl.ds(pl.multiple_of(z * rows, rows), rows), :]


def to_rows_of_z(coords, first, second):
    shape = pltpu.HBM((2, first.shape[0] // 4, D), BF16)
    chunks = small_kernel(to_z_kernel, coords, [first, second], [shape] * 4)
    return [chunks[0]] + [shift(chunks[k], Z, k) for k in (1, 2, 3)]


def by_sequence_kernel(coords_ref, *refs):
    arrived, (keep, send, blocks) = refs[:4], refs[4:]
    for i in range(2):
        for k in range(4):
            blocks[i, lax.rem(coords_ref[1] + 4 - k, 4)] = arrived[k][i]
    for i in range(2):
        for micro in range(2):
            keep[i, micro] = blocks[i, micro * 2 + coords_ref[3]]
            send[i, micro] = blocks[i, micro * 2 + 1 - coords_ref[3]]


def rows_kernel(coords_ref, keep, got, acts, in_grads):
    rows = keep.shape[2]
    for core, ref in enumerate((keep, got)):
        here = pl.ds(pl.multiple_of(lax.rem(coords_ref[3] + core, 2) * rows, rows), rows)
        for micro in range(2):
            acts[micro, here, :] = ref[0, micro]
            in_grads[micro, here, :] = ref[1, micro].astype(F32)


def own_rows(coords, arrays):
    rows = arrays[0].shape[1]
    shape = (2, 2, rows, D)
    keep, send = pl.pallas_call(
        by_sequence_kernel,
        grid_spec=pltpu.PrefetchScalarGridSpec(
            num_scalar_prefetch=1,
            grid=(1,),
            in_specs=[all_of(a.shape) for a in arrays],
            out_specs=[all_of(shape)] * 2,
            scratch_shapes=[pltpu.VMEM((2, 4, rows, D), BF16)],
        ),
        out_shape=[jax.ShapeDtypeStruct(shape, BF16), pltpu.HBM(shape, BF16)],
        compiler_params=pltpu.CompilerParams(vmem_limit_bytes=VMEM_LIMIT),
        cost_estimate=FREE,
    )(coords, *arrays)
    outs = [pltpu.HBM((2, 2 * rows, D), t) for t in (BF16, F32)]
    return small_kernel(rows_kernel, coords, [keep, swap_cores(send)], outs)


def by_pair(values):
    lead = values.shape[:-1]
    return values.reshape(*lead, 3, PAIRS, PAIR).swapaxes(-2, -3).reshape(*lead, 3 * D)


def by_core(values):
    lead = values.shape[:-1]
    return jnp.moveaxis(values.reshape(*lead, 2, 4, 4, 2, 64), (-2, -3, -4, -5), (-5, -4, -3, -2)).reshape(*lead, FF)


def on_device(
    inputs,
    cotangent,
    block_order,
    ln1_gain,
    ln1_bias,
    qkv_weight,
    qv_bias,
    out_weight,
    out_bias,
    ln2_gain,
    ln2_bias,
    fc_weight,
    fc_bias,
    proj_weight,
    proj_bias,
):
    section = lax.axis_index("section")
    core = lax.axis_index(CORE)
    coords = jnp.stack([lax.axis_index(a) for a in (*CTX_FSDP, "section")]).astype(jnp.int32)
    first = section == 0
    micro, _, rows, _ = inputs.shape

    vectors = (ln1_gain, ln1_bias, qv_bias, out_bias, ln2_gain, ln2_bias, fc_bias, proj_bias)
    widths = [v.shape[-1] for v in vectors]
    starts = [sum(widths[:i]) for i in range(len(widths))]
    packed = jnp.concatenate([v.reshape(-1) for v in vectors])
    packed = jnp.pad(packed, (0, 16 * 128 - packed.shape[0])).reshape(16, 128)

    qkv_cut = by_pair(qkv_weight[0]).reshape(16, 2, 2, 768)
    out_cut = out_weight[0].reshape(16, 2, 2, 256)
    fc_cut = by_core(fc_weight[0]).reshape(16, 2, 2048)
    halves = [
        jnp.concatenate(
            [qkv_cut[:, i, 0], out_cut[:, i, 0], packed, fc_cut[:, i], qkv_cut[:, i, 1], out_cut[:, i, 1]],
            axis=1,
        )
        for i in range(2)
    ]
    mine = jnp.where(core == 0, halves[0], halves[1])
    other = jnp.where(core == 0, halves[1], halves[0])
    blob = in_order(core, mine, swap_cores(other), 0)
    proj_own = in_order(coords[0], proj_weight[0], shift(proj_weight[0], Y, 1), 0)
    proj_own = lax.all_gather(proj_own, Z, axis=0, tiled=True)
    ring_x = first_ring(both_y(blob[:, :3200]), X)
    ring_z = first_ring(both_y(blob[:, 3200:]), Z)
    tokens = to_sequence(jnp.concatenate([inputs[:, 0], cotangent[:, 0]], axis=-1), core)
    ring_x, ring_z, tokens = together(ring_x, ring_z, tokens)
    entry, given = tokens[:, :D], tokens[:, D:]
    pieces_x = second_ring(ring_x[..., :1152], Z)
    pieces_z = second_ring(ring_z, X)
    fc_halves = (ring_x[:2, ..., 1152:], ring_x[2:, ..., 1152:])
    (pieces_x, pieces_z), fc_halves, proj_own, entry = together((pieces_x, pieces_z), fc_halves, proj_own, entry)
    proj_own = lax.all_gather(proj_own, X, axis=0, tiled=True)
    cuts = ((0, 768, 0, 0), (768, 256, 1, 0))
    qkv_0, out_0, packed = assemble(coords, X, cuts + ((1024, 128, 2, 0),), pieces_x)
    qkv_1, out_1 = assemble(coords, Z, cuts, pieces_z)
    out_own = jnp.concatenate([out_0, out_1], axis=1)
    w = {
        "qkv": ((qkv_0, qkv_1), (swap_cores(qkv_0), swap_cores(qkv_1))),
        "out": (out_own, swap_cores(out_own)),
    }

    def late_weights():
        value = yield
        low, high = to_neighbours(fc_halves, Z)
        value, low, high = together(value, low, high)
        far = to_neighbours((low, high), Z)
        value = yield value
        value, low_late, high_late = together(value, *to_neighbours(fc_halves[::-1], Z))
        value = yield value
        pieces = [fc_halves, far, (low, low_late), (high_late, high)]
        value, pieces = together(value, pieces)
        (fc_own,) = assemble(coords, X, ((0, 2048, 0, 0),), pieces)
        w["fc"] = (fc_own, swap_cores(fc_own))
        w["proj"] = (proj_own, swap_cores(proj_own))
        yield value

    packed = packed.reshape(32, 2, 16, 128)[:, :, :2].reshape(64, 256)
    names = ("ln1_gain", "ln1_bias", "qv", "out_bias", "ln2_gain", "ln2_bias", "fc", "proj_bias")
    vector = {
        name: packed[:, start : start + width].reshape(1, -1).astype(F32)
        for name, start, width in zip(names, starts, widths)
    }
    qv, fc_vector = vector.pop("qv"), by_core(vector.pop("fc"))
    qkv_vector = by_pair(jnp.concatenate([qv[:, :D], jnp.zeros((1, D), F32), qv[:, D:]], axis=1))
    w.update(vector)
    w["qkv_bias"] = (half(qkv_vector, core, 1), half(qkv_vector, 1 - core, 1))
    w["fc_bias"] = (half(fc_vector, core, 1), half(fc_vector, 1 - core, 1))

    early = layer_forward(entry, w, block_order, coords, 0, None, late_weights())
    result = feed_down(early["middle"], early["act"], w)
    arriving = lax.ppermute(result, "section", [(0, 1)])
    heavy, result = together((w["fc"], w["proj"]), result)
    heavy = jax.tree.map(held, heavy)
    arriving, (w["fc"], w["proj"]) = together(arriving, heavy)
    entry = jnp.where(first, entry, arriving)
    saved = layer_forward(entry, w, block_order, coords, 1, early)

    d_entry, early = layer_backward(given, saved, w, block_order, coords, 1, None)
    arriving = lax.ppermute(d_entry, "section", [(1, 0)])
    middle, act_other, normed2, normed, attended, _ = together(
        saved["middle"], saved["act"][1], saved["normed2"], saved["normed"], saved["attended"], d_entry
    )
    swapped = [swap_cores(v) for v in (act_other, normed2, normed, attended)]
    result = feed_down(middle, saved["act"], w)
    arriving, result, saved["swapped"] = together(arriving, result, swapped)
    upstream = jnp.where(first, arriving, given)
    d_entry, g = layer_backward(upstream, saved, w, block_order, coords, 0, early)
    d_entry, proj_part = together(d_entry, g["proj"])
    proj_grad = sum_by_axes(proj_part, (Z,)).astype(F32)
    tokens = to_rows_of_z(coords, result, d_entry)
    parts = [streamed(v) for v in (*g["fc"], g["qkv"])]
    columns = parts[0].shape[2] + g["qkv"].shape[3]
    outs = [jax.ShapeDtypeStruct((32, columns), F32), pltpu.HBM((32, columns), BF16)]
    mine, send = small_kernel(y_kernel, coords, parts, outs)
    mine, tokens = together(mine, tokens)
    acts, in_grads = own_rows(coords, tokens)
    outs = [jax.ShapeDtypeStruct((16, columns), F32), pltpu.HBM((16, columns), F32)]
    got, proj_grad = together(shift(send, Y, 1), proj_grad)
    keep, send = small_kernel(core_kernel, coords, [mine, got], outs)
    widths = (3 * D, D, FF, 16, 16, 32, 16, 16, 16, 64, 16)
    outs = [pltpu.HBM((16 if n >= D else 1, n), F32) for n in widths]
    qkv_grad, out_grad, fc_grad, *small = small_kernel(final_kernel, coords, [keep, swap_cores(send)], outs)
    shape = (1, micro, 1, rows, D)
    return (
        acts.reshape(shape),
        in_grads.reshape(shape),
        small[0],
        small[1],
        qkv_grad[None],
        small[2],
        out_grad[None],
        small[3],
        small[4],
        small[5],
        fc_grad[None],
        small[6],
        proj_grad[None],
        small[7],
    )


def solution(mesh):
    torus = Mesh(
        mesh.devices.reshape(mesh.shape["section"], 2, 4, 4, 2),
        ("section", "ctx_0", "ctx_1", "fsdp_0", "fsdp_1"),
    )
    tokens = P(None, FSDP, CTX, None)
    vector = P("section", CTX_FSDP)
    matrix = P("section", CTX_FSDP, None)
    kinds = (vector, vector, matrix, vector, matrix, vector, vector, vector, matrix, vector, matrix, vector)
    results = P("section", None, FSDP, CTX, None)
    return jax.shard_map(
        on_device,
        mesh=torus,
        in_specs=(tokens, tokens, P()) + kinds,
        out_specs=(results, results) + kinds,
        check_vma=False,
    )
```
